256 devices in a mesh: gx: 4 (over z_hi), gy: 4 (over x), gz: 16 (over z_lo, y, core).
Axes of the slice: x: 4, y: 4, z: 8 (z_hi: 4, z_lo: 2; z = z_hi * 2 + z_lo), core: 2. Of those that a mesh axis runs over, the one named last changes fastest.
Arguments:
- volume_features: bfloat16 [64, 128, 256, 64], P('gx', 'gy', 'gz'), may hold values from -6 to 6
- fine_weight: bfloat16 [3, 3, 3, 64, 64], replicated, may hold values from -0.21875 to 0.21875
- fine_bias: float32 [64], replicated, may hold values from -1.5 to 1.5
- middle_weight: bfloat16 [3, 3, 3, 64, 128], replicated, may hold values from -0.21875 to 0.21875
- middle_bias: float32 [128], replicated, may hold values from -1.5 to 1.5
- bottom_weight: bfloat16 [3, 3, 3, 128, 256], replicated, may hold values from -0.15625 to 0.15625
- bottom_bias: float32 [256], replicated, may hold values from -1.5 to 1.5
- rise_middle_weight: bfloat16 [3, 3, 3, 384, 128], replicated, may hold values from -0.078125 to 0.078125
- rise_middle_bias: float32 [128], replicated, may hold values from -1.5 to 1.5
- rise_fine_weight: bfloat16 [3, 3, 3, 192, 64], replicated, may hold values from -0.125 to 0.125
- rise_fine_bias: float32 [64], replicated, may hold values from -1.5 to 1.5
Outputs:
- decoded: bfloat16 [64, 128, 256, 64], P('gx', 'gy', 'gz')
The draws below stay inside these ranges and needn't reach their ends.
All inputs are finite; a program needn't handle non-finite values.
Results may differ from the reference program's by a relative error of at most 0.012.
Values may be sent and summed in bfloat16 or wider, within the bound.
A program may use at most 128 MiB of HBM per device.

```python
import jax
import jax.numpy as jnp
from jax import lax

C0 = 64
C1 = 128
C2 = 256
NX = 64
NY = 128
NZ = 256


def level_of(own_key, extent, pieces, low, high):
    factor_of = 1.0
    for position, parts in pieces:
        steps = jax.random.uniform(jax.random.fold_in(jax.random.fold_in(own_key, 6), position), (parts,), jnp.float32, low / len(pieces), high / len(pieces))
        factor_of = factor_of * jnp.repeat(jnp.exp(steps), extent[position] // parts).reshape((-1,) + (1,) * (len(extent) - 1 - position))
    return factor_of


def scatter_about(stream_key, extent, scale, bound, split=(), dtype=jnp.bfloat16):
    entries = scale * jax.random.normal(stream_key, extent, jnp.float32)
    if split:
        entries = entries * level_of(stream_key, extent, split, -0.22, 0.18)
    return jnp.clip(entries, -bound, bound).astype(dtype)


def setup_inputs(seed: int = 0) -> dict:
    key_of = jax.random.split(jax.random.key(seed), 12)
    return {
        "volume_features": scatter_about(key_of[0], (NX, NY, NZ, C0), 1.0, 6.0, ((0, 4), (1, 4), (2, 16))),
        "fine_weight": scatter_about(key_of[1], (3, 3, 3, C0, C0), (27 * C0 // 2) ** -0.5, 0.21875),
        "fine_bias": scatter_about(key_of[2], (C0,), 0.3, 1.5, (), jnp.float32),
        "middle_weight": scatter_about(key_of[3], (3, 3, 3, C0, C1), (27 * C0 // 2) ** -0.5, 0.21875),
        "middle_bias": scatter_about(key_of[4], (C1,), 0.3, 1.5, (), jnp.float32),
        "bottom_weight": scatter_about(key_of[5], (3, 3, 3, C1, C2), (27 * C1 // 2) ** -0.5, 0.15625),
        "bottom_bias": scatter_about(key_of[6], (C2,), 0.3, 1.5, (), jnp.float32),
        "rise_middle_weight": scatter_about(key_of[7], (3, 3, 3, C1 + C2, C1), (27 * (C1 + C2) // 2) ** -0.5, 0.078125),
        "rise_middle_bias": scatter_about(key_of[8], (C1,), 0.3, 1.5, (), jnp.float32),
        "rise_fine_weight": scatter_about(key_of[9], (3, 3, 3, C0 + C1, C0), (27 * (C0 + C1) // 2) ** -0.5, 0.125),
        "rise_fine_bias": scatter_about(key_of[10], (C0,), 0.3, 1.5, (), jnp.float32),
    }


def convolve(field, weight, bias):
    result = lax.conv_general_dilated(field[None], weight, (1, 1, 1), "SAME", dimension_numbers=("NDHWC", "DHWIO", "NDHWC"), preferred_element_type=jnp.float32)
    return result[0] + bias


def pooled(field):
    depth, height, width, chans = field.shape
    blocks = field.reshape(depth // 2, 2, height // 2, 2, width // 2, 2, chans)
    return jnp.max(blocks, axis=(1, 3, 5))


def enlarge(field):
    return jnp.repeat(jnp.repeat(jnp.repeat(field, 2, axis=0), 2, axis=1), 2, axis=2)


def activate(values):
    return jnp.maximum(values, 0.0).astype(jnp.bfloat16)


def reference(volume_features, fine_weight, fine_bias, middle_weight, middle_bias, bottom_weight, bottom_bias, rise_middle_weight, rise_middle_bias, rise_fine_weight, rise_fine_bias):
    enc_fine = activate(convolve(volume_features, fine_weight, fine_bias))
    pool_fine = pooled(enc_fine)
    enc_middle = activate(convolve(pool_fine, middle_weight, middle_bias))
    pool_middle = pooled(enc_middle)
    enc_bottom = activate(convolve(pool_middle, bottom_weight, bottom_bias))
    joined = jnp.concatenate([enc_middle, enlarge(enc_bottom)], axis=3)
    dec_middle = activate(convolve(joined, rise_middle_weight, rise_middle_bias))
    joined = jnp.concatenate([enc_fine, enlarge(dec_middle)], axis=3)
    return convolve(joined, rise_fine_weight, rise_fine_bias).astype(jnp.bfloat16)
```

```python
import functools

import jax
import jax.numpy as jnp
from jax import lax
from jax.experimental import pallas as pl
from jax.experimental.pallas import tpu as pltpu
from jax.sharding import PartitionSpec as P

BF = jnp.bfloat16
F32 = jnp.float32
MESH = pl.DeviceIdType.MESH

NXF, NZF, ROWS = 16, 16, 16
NXM, NZM = 8, 8
TF, TM = 336, 112
LEVELS = 6


def dot(a, b):
    return jnp.dot(a, b, preferred_element_type=F32)


def cells(ref, *index):
    value = ref[index]
    return value.reshape(-1, value.shape[-1])


def kernel(
    sizes,
    vol, wf_hbm, wm_hbm, wb_hbm, wrm_hbm, wrf_hbm, bias_ref,
    out_hbm,
    r_in, h_in, s_fine, y_in, yr_in,
    r_enc, h_enc, y_enc, yr_enc,
    r_pool, h_pool, s_pool, y_pool, yr_pool,
    r_mid, hu_mid, hd_mid, s_mid, y_mid, yr_mid,
    r_low, s_low, y_low, yr_low, pair_tmp,
    low_lanes, bottom_tmp, s_up, up_lanes,
    r_dec, hu_dec, hd_dec, s_dec, y_dec, yr_dec,
    wf_raw, wrf_raw, wrm_raw,
    w_fine, w_skip, w_mid, w_bottom, w_rm_skip, w_rm_up, w_rf_up,
    skip, out_v,
    send_sem, recv_sem, local_sem,
):
    spots = {axis: lax.axis_index(axis) for axis in ("gx", "gy", "gz")}

    def near(axis, step):
        count = sizes[axis]
        return lax.rem(spots[axis] + (step + count), count)

    def at_low(axis):
        return spots[axis] == 0

    def at_high(axis):
        return spots[axis] == sizes[axis] - 1

    def message(number, src, dst, axis, step):
        return pltpu.make_async_remote_copy(
            src_ref=src, dst_ref=dst, send_sem=send_sem.at[number], recv_sem=recv_sem.at[number],
            device_id={axis: near(axis, step)}, device_id_type=MESH,
        )

    sent = []

    def start(copies):
        for copy in copies:
            copy.start()
        sent.extend(copies)
        return copies

    def arrived(copies):
        for copy in copies:
            copy.wait_recv()

    loads = {}

    def load(name, src, dst):
        copy = pltpu.make_async_copy(src, dst, local_sem.at[len(loads)])
        copy.start()
        loads[name] = copy

    load("vol0", vol.at[:, :, 0], r_in.at[1:NXF + 1, 0:8, 1])
    load("vol1", vol.at[:, :, 1], r_in.at[1:NXF + 1, 1:9, 0])
    load("wf", wf_hbm, wf_raw)
    load("wrf", wrf_hbm, wrf_raw)
    for dz in range(2):
        lanes = pl.ds(dz * 128, 128)
        for q, slot in ((1, 0), (2, 2), (0, 3)):
            load(("wm", dz, q), wm_hbm.at[:, q], w_mid.at[:, dz:dz + 3, slot, :, lanes])
    for q, slot in ((1, 0), (2, 1), (0, 2)):
        load(("wb", q), wb_hbm.at[:, q], w_bottom.at[:, :, slot])
    for dz in range(2):
        lanes = pl.ds(dz * 128, 128)
        for q, slot in ((1, 0), (2, 1), (0, 2)):
            load(("wrm", dz, q), wrm_hbm.at[:, q, :, 0:128, :], w_rm_skip.at[:, dz:dz + 3, slot, :, lanes])
    load("wrm_raw", wrm_hbm.at[:, :, :, 128:384, :], wrm_raw)

    barrier = pltpu.get_barrier_semaphore()
    for axis in ("gx", "gy", "gz"):
        for step in (-1, 1):
            pl.semaphore_signal(barrier, inc=1, device_id={axis: near(axis, step)}, device_id_type=MESH)
    pl.semaphore_wait(barrier, 6)

    def start_z(base, ref, nx, nz):
        own = pl.ds(1, nx)
        return start([
            message(base, ref.at[own, 0, 1], ref.at[own, nz // 2, 1], "gz", -1),
            message(base + 1, ref.at[own, nz // 2, 0], ref.at[own, 0, 0], "gz", 1),
        ])

    def wait_z(copies, ref, s, nx, nz):
        arrived(copies)
        own = pl.ds(1, nx)

        @pl.when(at_low("gz"))
        def _():
            ref[own, 0, 0] = jnp.zeros((nx, ROWS, 128), BF)

        @pl.when(at_high("gz"))
        def _():
            ref[own, nz // 2, 1] = jnp.zeros((nx, ROWS, 128), BF)

        s[own, 0, 0, 8:24] = ref[own, 0, 0].astype(F32)
        s[own, nz // 2, 1, 8:24] = ref[own, nz // 2, 1].astype(F32)

    def start_x(base, ref, nx):
        return start([
            message(base + 2, ref.at[1], ref.at[nx + 1], "gx", -1),
            message(base + 3, ref.at[nx], ref.at[0], "gx", 1),
        ])

    def wait_x(copies, ref, s, nx):
        arrived(copies)
        for plane, edge in ((0, at_low("gx")), (nx + 1, at_high("gx"))):
            @pl.when(edge)
            def _():
                ref[plane] = jnp.zeros(ref.shape[1:], BF)

            s[plane, :, :, 8:24] = ref[plane].astype(F32)

    def start_y(base, s, ys, yr):
        count = ys.shape[1]
        rows = s.reshape(s.shape[0] * s.shape[1] * s.shape[2] * 32, 128)
        ys[0] = rows[pl.ds(8, count, stride=32), :].astype(BF)
        ys[1] = rows[pl.ds(23, count, stride=32), :].astype(BF)
        return start([
            message(base + 4, ys.at[0], yr.at[1], "gy", -1),
            message(base + 5, ys.at[1], yr.at[0], "gy", 1),
        ])

    def wait_y(copies, s, yr):
        arrived(copies)
        count = yr.shape[1]
        rows = s.reshape(s.shape[0] * s.shape[1] * s.shape[2] * 32, 128)
        low = jnp.where(at_low("gy"), 0.0, yr[0].astype(F32))
        high = jnp.where(at_high("gy"), 0.0, yr[1].astype(F32))
        rows[pl.ds(7, count, stride=32), :] = low
        rows[pl.ds(24, count, stride=32), :] = high

    def beside(s, dst, planes):
        lane = lax.broadcasted_iota(jnp.int32, dst.shape[1:], 3)

        def plane(x, carry):
            dst[x] = jnp.where(lane < 64, s[x, :, :, 9:25], s[x, :, :, 7:23]).astype(BF)
            return carry

        lax.fori_loop(0, planes, plane, 0)

    def beside_both(s, up, down, planes):
        def plane(x, carry):
            up[x] = s[x, :, :, 9:25].astype(BF)
            down[x] = s[x, :, :, 7:23].astype(BF)
            return carry

        lax.fori_loop(0, planes, plane, 0)

    def spread(raw, first, dst):
        dst[...] = jnp.zeros(dst.shape, BF)

        def one(p, carry):
            for r in range(3):
                taps = [raw[p, q, r, first:first + 64, :] for q in range(3)]
                none = jnp.zeros_like(taps[0])
                pairs = ((taps[1], taps[0]), (taps[2], taps[1]), (none, taps[2]), (taps[0], none))
                for slot, pair in enumerate(pairs):
                    block = jnp.concatenate(pair, axis=1)
                    for dz in range(2):
                        dst[p, r + dz, slot, :, dz * 128:(dz + 1) * 128] = block
            return carry

        lax.fori_loop(0, 3, one, 0)

    def fine_window(ref, side, x, count):
        parts = []
        for p in range(3):
            for zo in range(4):
                index = (pl.ds(x + p, count), pl.ds(zo // 2, 8), zo % 2)
                parts += [cells(ref, *index), cells(side, *index)]
        return jnp.concatenate(parts, axis=1)

    loads["vol0"].wait()
    loads["vol1"].wait()
    going = start_z(0, r_in, NXF, NZF)

    def widen(x, carry):
        s_fine[x, 0:8, 1, 8:24] = r_in[x, 0:8, 1].astype(F32)
        s_fine[x, 1:9, 0, 8:24] = r_in[x, 1:9, 0].astype(F32)
        return carry

    lax.fori_loop(1, NXF + 1, widen, 0)
    loads["wf"].wait()
    spread(wf_raw, 0, w_fine)
    wait_z(going, r_in, s_fine, NXF, NZF)
    going = start_x(0, r_in, NXF)
    w_mid[:, :, 1] = jnp.zeros((3, 4, 64, 256), BF)
    w_mid[:, 3, :, :, 0:128] = jnp.zeros((3, 4, 64, 128), BF)
    w_mid[:, 0, :, :, 128:256] = jnp.zeros((3, 4, 64, 128), BF)
    w_rm_skip[:, 3, :, :, 0:128] = jnp.zeros((3, 3, 128, 128), BF)
    w_rm_skip[:, 0, :, :, 128:256] = jnp.zeros((3, 3, 128, 128), BF)
    loads["wrf"].wait()
    spread(wrf_raw, 0, w_skip)
    wait_x(going, r_in, s_fine, NXF)
    going = start_y(0, s_fine, y_in, yr_in)
    wait_y(going, s_fine, yr_in)
    beside(s_fine, h_in, NXF + 2)

    w_fine_all = w_fine.reshape(3072, 256)

    def fine(pair, carry):
        x = 2 * pair
        result = dot(fine_window(r_in, h_in, x, 2), w_fine_all[...])
        result = jnp.maximum(result + bias_ref[0:1, :], 0.0).reshape(2, 8, ROWS, 256)
        for dz, (index, half) in enumerate((((pl.ds(0, 8), 1), 0), ((pl.ds(1, 8), 0), 1))):
            value = result[..., half * 128:(half + 1) * 128]
            r_enc[(pl.ds(x + 1, 2),) + index] = value.astype(BF)
            s_fine[(pl.ds(x + 1, 2),) + index + (pl.ds(8, 16),)] = value
        most = jnp.max(result, axis=0)
        most = jnp.maximum(most[..., 0:128], most[..., 128:256]).reshape(128, 128)
        most = jnp.maximum(most, pltpu.roll(most, 64, 1)).reshape(4, 2, ROWS, 128)
        r_pool[pair + 1, 0:4, 1] = most[:, 0].astype(BF)
        s_pool[pair + 1, 0:4, 1, 8:24] = most[:, 0]
        r_pool[pair + 1, 1:5, 0] = most[:, 1].astype(BF)
        s_pool[pair + 1, 1:5, 0, 8:24] = most[:, 1]
        return carry

    lax.fori_loop(0, 8, fine, 0)

    going = start_z(6, r_pool, NXM, NZM)
    skipping = start_z(12, r_enc, NXF, NZF)
    loads["wrm_raw"].wait()

    def sums(parts):
        return (parts[0], parts[1] + parts[2], parts[0] + parts[1], parts[2])

    def rise_mid(chunk, carry):
        rows = pl.ds(pl.multiple_of(chunk * 16, 16), 16)
        for q, slot in ((1, 0), (2, 1), (0, 2)):
            by_r = [sums([wrm_raw[p, q, r, rows, :].astype(F32) for p in range(3)]) for r in range(3)]
            for x_sum in range(4):
                z_sums = sums([by_r[r][x_sum] for r in range(3)])
                for z_sum, (zt, dz) in enumerate(((0, 0), (1, 0), (1, 1), (2, 1))):
                    w_rm_up[x_sum, zt, slot, rows, dz * 128:(dz + 1) * 128] = z_sums[z_sum].astype(BF)
        return carry

    w_rm_up[:, 0, :, :, 128:256] = jnp.zeros((4, 3, 256, 128), BF)
    w_rm_up[:, 2, :, :, 0:128] = jnp.zeros((4, 3, 256, 128), BF)
    lax.fori_loop(0, 16, rise_mid, 0)

    wait_z(going, r_pool, s_pool, NXM, NZM)
    going = start_x(6, r_pool, NXM)
    wait_z(skipping, r_enc, s_fine, NXF, NZF)
    skipping = start_x(12, r_enc, NXF)

    def rise_fine(chunk, carry):
        src = pl.ds(pl.multiple_of(64 + chunk * 16, 16), 16)
        rows = pl.ds(pl.multiple_of(chunk * 16, 16), 16)
        by_q = []
        for q in range(3):
            by_r = [sums([wrf_raw[p, q, r, src, :].astype(F32) for p in range(3)]) for r in range(3)]
            by_q.append([sums([by_r[r][x_sum] for r in range(3)]) for x_sum in range(4)])
        none = jnp.zeros((16, 64), F32)
        for x_sum in range(4):
            for z_sum, (zt, dz) in enumerate(((0, 0), (1, 0), (1, 1), (2, 1))):
                taps = [by_q[q][x_sum][z_sum] for q in range(3)]
                pairs = ((taps[1] + taps[2], taps[0] + taps[1]), (none, taps[2]), (taps[0], none))
                for slot, pair in enumerate(pairs):
                    block = jnp.concatenate(pair, axis=1).astype(BF)
                    w_rf_up[x_sum, zt, slot, rows, dz * 128:(dz + 1) * 128] = block
        return carry

    w_rf_up[:, 0, :, :, 128:256] = jnp.zeros((4, 3, 128, 128), BF)
    w_rf_up[:, 2, :, :, 0:128] = jnp.zeros((4, 3, 128, 128), BF)
    lax.fori_loop(0, 8, rise_fine, 0)

    wait_x(going, r_pool, s_pool, NXM)
    going = start_y(6, s_pool, y_pool, yr_pool)
    wait_x(skipping, r_enc, s_fine, NXF)
    skipping = start_y(12, s_fine, y_enc, yr_enc)
    for dz in range(2):
        for q in range(3):
            loads[("wm", dz, q)].wait()
    wait_y(going, s_pool, yr_pool)
    beside(s_pool, h_pool, NXM + 2)

    parts = []
    for p in range(3):
        for zo in range(4):
            index = (pl.ds(p, 8), pl.ds(zo // 2, 4), zo % 2)
            parts += [cells(r_pool, *index), cells(h_pool, *index)]
    result = dot(jnp.concatenate(parts, axis=1), w_mid.reshape(3072, 256)[...])
    result = jnp.maximum(result + bias_ref[1:2, :], 0.0).reshape(4, 2, 4, ROWS, 256)
    for dz, index in enumerate(((pl.ds(0, 4), 1), (pl.ds(1, 4), 0))):
        value = result[..., dz * 128:(dz + 1) * 128]
        for dx in range(2):
            place = (pl.ds(0, 4), 1) if dx == 0 else (pl.ds(1, 4), 0)
            r_mid[place + index] = value[:, dx].astype(BF)
            s_mid[place + index + (pl.ds(8, 16),)] = value[:, dx]
    most = jnp.maximum(result[:, 0], result[:, 1])
    pair_tmp[...] = jnp.maximum(most[..., 0:128], most[..., 128:256]).reshape(256, 128)
    low = jnp.maximum(pair_tmp[pl.ds(0, 128, stride=2), :], pair_tmp[pl.ds(1, 128, stride=2), :])
    r_low[2:6, 1:3] = low.astype(BF).reshape(4, 2, ROWS, 128)

    base = 18
    going = start([
        message(base, r_low.at[2:6, 1], r_low.at[2:6, 3], "gz", -1),
        message(base + 1, r_low.at[2:6, 2], r_low.at[2:6, 0], "gz", 1),
    ])
    r_mid_planes = r_mid.reshape(10, 5, 2, ROWS, 128)
    s_mid_planes = s_mid.reshape(12, 5, 2, 32, 128)
    middle = start_z(24, r_mid_planes, NXM, NZM)

    wait_y(skipping, s_fine, yr_enc)
    beside(s_fine, h_enc, NXF + 2)
    w_skip_all = w_skip.reshape(3072, 256)

    def skip_part(pair, carry):
        x = 2 * pair
        result = dot(fine_window(r_enc, h_enc, x, 2), w_skip_all[...]) + bias_ref[4:5, :]
        skip[pl.ds(x, 2)] = result.reshape(2, 128, 256)
        return carry

    arrived(going)

    @pl.when(at_low("gz"))
    def _():
        r_low[2:6, 0] = jnp.zeros((4, ROWS, 128), BF)

    @pl.when(at_high("gz"))
    def _():
        r_low[2:6, 3] = jnp.zeros((4, ROWS, 128), BF)

    going = start([
        message(base + 2, r_low.at[2:4], r_low.at[6:8], "gx", -1),
        message(base + 3, r_low.at[4:6], r_low.at[0:2], "gx", 1),
    ])
    wait_z(middle, r_mid_planes, s_mid_planes, NXM, NZM)
    middle = start_x(24, r_mid_planes, NXM)
    lax.fori_loop(0, 3, skip_part, 0)
    arrived(going)

    @pl.when(at_low("gx"))
    def _():
        r_low[0:2] = jnp.zeros((2, 4, ROWS, 128), BF)

    @pl.when(at_high("gx"))
    def _():
        r_low[6:8] = jnp.zeros((2, 4, ROWS, 128), BF)

    low = r_low[...].astype(F32).reshape(8, 4, 2, 8, 128).reshape(8, 8, 8, 128)
    s_low[:, :, 8:16] = low
    s_low[:, :, 0:8] = jnp.zeros_like(low)
    s_low[:, :, 16:24] = jnp.zeros_like(low)
    rows = s_low.reshape(2048, 128)
    for number, row in enumerate((8, 9, 14, 15)):
        y_low[number // 2, pl.ds((number % 2) * 64, 64), :] = rows[pl.ds(row, 64, stride=32), :].astype(BF)
    going = start([
        message(base + 4, y_low.at[0], yr_low.at[1], "gy", -1),
        message(base + 5, y_low.at[1], yr_low.at[0], "gy", 1),
    ])
    wait_x(middle, r_mid_planes, s_mid_planes, NXM)
    middle = start_y(24, s_mid_planes, y_mid, yr_mid)
    for q in range(3):
        loads[("wb", q)].wait()
    lax.fori_loop(3, 5, skip_part, 0)
    arrived(going)
    for number, row in enumerate((6, 7, 16, 17)):
        edge = at_low("gy") if number < 2 else at_high("gy")
        value = yr_low[number // 2, pl.ds((number % 2) * 64, 64), :].astype(F32)
        rows[pl.ds(row, 64, stride=32), :] = jnp.where(edge, 0.0, value)

    def low_plane(x, carry):
        for slot, first in enumerate((4, 5, 3)):
            low_lanes[x, :, :, slot * 128:(slot + 1) * 128] = s_low[x, :, first:first + 16].astype(BF)
        return carry

    lax.fori_loop(0, 8, low_plane, 0)
    parts = [cells(low_lanes, pl.ds(p, 6), pl.ds(r, 6)) for p in range(3) for r in range(3)]
    result = dot(jnp.concatenate(parts, axis=1), w_bottom.reshape(3456, 256)[...])
    result = jnp.maximum(result + bias_ref[2:3, :], 0.0).reshape(6, 6, ROWS, 256)
    index = lax.broadcasted_iota(jnp.int32, (6, 6, ROWS, 256), 0)
    zindex = lax.broadcasted_iota(jnp.int32, (6, 6, ROWS, 256), 1)
    yindex = lax.broadcasted_iota(jnp.int32, (6, 6, ROWS, 256), 2)
    outside = False
    for where, first, last, axis in ((index, 0, 5, "gx"), (zindex, 0, 5, "gz"), (yindex, 3, 12, "gy")):
        outside = outside | ((where == first) & at_low(axis)) | ((where == last) & at_high(axis))
    result = jnp.where(outside, 0.0, result).reshape(576, 256)
    for half in range(2):
        bottom_tmp[half] = result[:, half * 128:(half + 1) * 128]

    for half in range(2):
        doubled = s_up.at[half].reshape(36 * 32, 128)
        for step in range(10):
            value = bottom_tmp.at[half][pl.ds(3 + step, 36, stride=16), :]
            doubled[pl.ds(6 + 2 * step, 36, stride=32), :] = value
            doubled[pl.ds(7 + 2 * step, 36, stride=32), :] = value
    for slot, first in enumerate((8, 9, 7)):
        for half in range(2):
            lanes = slice(slot * 256 + half * 128, slot * 256 + half * 128 + 128)
            up_lanes[:, :, :, lanes] = s_up[half, :, first:first + 16].astype(BF).reshape(6, 6, ROWS, 128)

    wait_y(middle, s_mid_planes, yr_mid)
    beside_both(s_mid_planes, hu_mid.reshape(10, 5, 2, ROWS, 128), hd_mid.reshape(10, 5, 2, ROWS, 128), NXM + 2)
    for dz in range(2):
        for q in range(3):
            loads[("wrm", dz, q)].wait()

    for dx in range(2):
        parts = []
        for p in range(3):
            for zo in range(4):
                index = (pl.ds((dx + p) // 2, 4), (dx + p) % 2, pl.ds(zo // 2, 4), zo % 2)
                parts += [cells(ref, *index) for ref in (r_mid, hu_mid, hd_mid)]
        result = dot(jnp.concatenate(parts, axis=1), w_rm_skip.reshape(4608, 256)[...])
        parts = []
        for xt in range(2):
            for zt in range(3):
                parts.append(cells(up_lanes, pl.ds(xt + dx, 4), pl.ds(zt, 4)))
        weight = w_rm_up.reshape(2, 4608, 256)[dx]
        result = result + dot(jnp.concatenate(parts, axis=1), weight)
        result = jnp.maximum(result + bias_ref[3:4, :], 0.0).reshape(4, 4, ROWS, 256)
        for dz, index in enumerate(((pl.ds(0, 4), 1), (pl.ds(1, 4), 0))):
            place = (pl.ds(0, 4), 1) if dx == 0 else (pl.ds(1, 4), 0)
            value = result[..., dz * 128:(dz + 1) * 128]
            r_dec[place + index] = value.astype(BF)
            s_dec[place + index + (pl.ds(8, 16),)] = value

    r_dec_planes = r_dec.reshape(10, 5, 2, ROWS, 128)
    s_dec_planes = s_dec.reshape(12, 5, 2, 32, 128)
    going = start_z(30, r_dec_planes, NXM, NZM)
    lax.fori_loop(5, 6, skip_part, 0)
    wait_z(going, r_dec_planes, s_dec_planes, NXM, NZM)
    going = start_x(30, r_dec_planes, NXM)
    lax.fori_loop(6, 7, skip_part, 0)
    wait_x(going, r_dec_planes, s_dec_planes, NXM)
    going = start_y(30, s_dec_planes, y_dec, yr_dec)
    lax.fori_loop(7, 8, skip_part, 0)
    wait_y(going, s_dec_planes, yr_dec)
    beside_both(s_dec_planes, hu_dec.reshape(10, 5, 2, ROWS, 128), hd_dec.reshape(10, 5, 2, ROWS, 128), NXM + 2)

    flat = [ref.reshape(10, 10, ROWS, 128) for ref in (r_dec, hu_dec, hd_dec)]
    for dx in range(2):
        weight = w_rf_up.reshape(2, 2304, 256)

        def last(step, carry):
            x = 2 * step
            parts = []
            for xt in range(2):
                for zt in range(3):
                    parts += [cells(ref, pl.ds(x + xt + dx, 2), pl.ds(zt, 8)) for ref in flat]
            result = dot(jnp.concatenate(parts, axis=1), weight[dx]).reshape(2, 128, 256)
            for i in range(2):
                spot = 4 * step + 2 * i + dx
                out_v[spot] = (result[i] + skip[spot]).astype(BF).reshape(8, ROWS, 256)
            return carry

        lax.fori_loop(0, 4, last, 0)

    copy = pltpu.make_async_copy(out_v, out_hbm, local_sem.at[len(loads)])
    copy.start()
    for message_sent in sent:
        message_sent.wait_send()
    copy.wait()


def scratch():
    vmem = pltpu.VMEM
    fine = (NXF + 2, 9, 2, ROWS, 128)
    pool = (NXM + 2, 5, 2, ROWS, 128)
    mid = (5, 2, 5, 2, ROWS, 128)
    mid_s = (6, 2, 5, 2, 32, 128)
    return [
        vmem(fine, BF), vmem(fine, BF), vmem((NXF + 3, 9, 2, 32, 128), F32), vmem((2, TF, 128), BF), vmem((2, TF, 128), BF),
        vmem(fine, BF), vmem(fine, BF), vmem((2, TF, 128), BF), vmem((2, TF, 128), BF),
        vmem(pool, BF), vmem(pool, BF), vmem((NXM + 4, 5, 2, 32, 128), F32), vmem((2, TM, 128), BF), vmem((2, TM, 128), BF),
        vmem(mid, BF), vmem(mid, BF), vmem(mid, BF), vmem(mid_s, F32), vmem((2, TM, 128), BF), vmem((2, TM, 128), BF),
        vmem((8, 4, ROWS, 128), BF), vmem((8, 8, 32, 128), F32), vmem((2, 128, 128), BF), vmem((2, 128, 128), BF),
        vmem((256, 128), F32),
        vmem((8, 8, ROWS, 384), BF), vmem((2, 576, 128), F32), vmem((2, 36, 32, 128), F32), vmem((6, 6, ROWS, 768), BF),
        vmem(mid, BF), vmem(mid, BF), vmem(mid, BF), vmem(mid_s, F32), vmem((2, TM, 128), BF), vmem((2, TM, 128), BF),
        vmem((3, 3, 3, 64, 64), BF), vmem((3, 3, 3, 192, 64), BF), vmem((3, 3, 3, 256, 128), BF),
        vmem((3, 4, 4, 64, 256), BF), vmem((3, 4, 4, 64, 256), BF), vmem((3, 4, 4, 64, 256), BF),
        vmem((3, 3, 3, 128, 256), BF), vmem((3, 4, 3, 128, 256), BF), vmem((4, 3, 3, 256, 256), BF),
        vmem((4, 3, 3, 128, 256), BF),
        vmem((NXF, 128, 256), F32), vmem((NXF, 8, ROWS, 256), BF),
        pltpu.SemaphoreType.DMA((6 * LEVELS,)), pltpu.SemaphoreType.DMA((6 * LEVELS,)), pltpu.SemaphoreType.DMA((32,)),
    ]


def on_device(sizes, volume, wf, bf, wm, bm, wb, bb, wrm, brm, wrf, brf):
    block = volume.reshape(NXF, ROWS, 2, 8, 2, 64).transpose(0, 3, 4, 1, 2, 5).reshape(NXF, 8, 2, ROWS, 128)
    bias = jnp.stack([jnp.tile(bf, 4), jnp.tile(bm, 2), bb, jnp.tile(brm, 2), jnp.tile(brf, 4)])
    hbm = pl.BlockSpec(memory_space=pl.ANY)
    result = pl.pallas_call(
        functools.partial(kernel, sizes),
        out_shape=jax.ShapeDtypeStruct((NXF, 8, ROWS, 256), BF),
        in_specs=[hbm] * 6 + [pl.BlockSpec(memory_space=pltpu.VMEM)],
        out_specs=hbm,
        scratch_shapes=scratch(),
        compiler_params=pltpu.CompilerParams(
            collective_id=0, has_side_effects=True, vmem_limit_bytes=60 * 2**20
        ),
    )(block, wf, wm, wb, wrm, wrf, bias)
    return result.reshape(NXF, 8, ROWS, 2, 2, 64).transpose(0, 2, 4, 1, 3, 5).reshape(NXF, 32, NZF, 64)


def solution(mesh):
    return jax.shard_map(
        functools.partial(on_device, dict(mesh.shape)),
        mesh=mesh,
        in_specs=(P("gx", "gy", "gz", None),) + (P(),) * 10,
        out_specs=P("gx", "gy", "gz", None),
        check_vma=False,
    )
```

```python
import functools

import jax
import jax.numpy as jnp
from jax import lax
from jax.experimental import pallas as pl
from jax.experimental.pallas import tpu as pltpu
from jax.sharding import PartitionSpec as P

BF = jnp.bfloat16
F32 = jnp.float32
MESH = pl.DeviceIdType.MESH

NXF, NZF, ROWS = 16, 16, 16
NXM, NZM = 8, 8
TF, TM = 336, 112
LEVELS = 6
PEERS = [(x, 0, z) for x in (-1, 0, 1) for z in (-1, 0, 1) if x or z] + [(0, -1, 0), (0, 1, 0)]


def dot(a, b):
    return jnp.dot(a, b, preferred_element_type=F32)


def cells(ref, *index):
    value = ref[index]
    return value.reshape(-1, value.shape[-1])


def kernel(
    sizes,
    vol, wf_hbm, wm_hbm, wb_hbm, wrm_hbm, wrf_hbm, bf_ref, bm_ref, bb_ref, brm_ref, brf_ref,
    out_hbm,
    r_in, h_in, s_fine, y_in, yr_in,
    r_enc, h_enc, y_enc, yr_enc,
    r_pool, h_pool, s_pool, y_pool, yr_pool,
    r_mid, hu_mid, hd_mid, s_mid, y_mid, yr_mid,
    r_low, s_low, y_low, yr_low, pair_tmp,
    low_lanes, bottom_tmp, s_up, up_lanes,
    r_dec, hu_dec, hd_dec, s_dec, y_dec, yr_dec,
    wf_raw, wrf_raw, wrm_raw,
    w_fine, w_skip, w_mid, w_bottom, w_rm_skip, w_rm_up, w_rf_up,
    skip, vol_v, out_v, turn,
    send_sem, recv_sem, local_sem,
):
    spots = {axis: lax.axis_index(axis) for axis in ("gx", "gy", "gz")}

    def near(steps):
        return {
            axis: lax.rem(spots[axis] + (step + sizes[axis]), sizes[axis]) for axis, step in zip(sizes, steps) if step
        }

    def at_low(axis):
        return spots[axis] == 0

    def at_high(axis):
        return spots[axis] == sizes[axis] - 1

    def message(number, src, dst, *steps):
        return pltpu.make_async_remote_copy(
            src_ref=src, dst_ref=dst, send_sem=send_sem.at[number], recv_sem=recv_sem.at[number],
            device_id=near(steps), device_id_type=MESH,
        )

    sent = []

    def start(copies):
        for copy in copies:
            copy.start()
        sent.extend(copies)
        return copies

    def arrived(copies):
        for copy in copies:
            copy.wait_recv()

    loads = {}

    def load(name, src, dst):
        copy = pltpu.make_async_copy(src, dst, local_sem.at[len(loads)])
        copy.start()
        loads[name] = copy

    load("vol", vol, vol_v)
    load("wf", wf_hbm, wf_raw)
    load("wrf", wrf_hbm, wrf_raw)
    for dz in range(2):
        lanes = pl.ds(dz * 128, 128)
        for q, slot in ((1, 0), (2, 2), (0, 3)):
            load(("wm", dz, q), wm_hbm.at[:, q], w_mid.at[:, dz:dz + 3, slot, :, lanes])
    for q, slot in ((1, 0), (2, 1), (0, 2)):
        load(("wb", q), wb_hbm.at[:, q], w_bottom.at[:, :, slot])
    for dz in range(2):
        lanes = pl.ds(dz * 128, 128)
        for q, slot in ((1, 0), (2, 1), (0, 2)):
            load(("wrm", dz, q), wrm_hbm.at[:, q, :, 0:128, :], w_rm_skip.at[:, dz:dz + 3, slot, :, lanes])
    load("wrm_raw", wrm_hbm.at[:, :, :, 128:384, :], wrm_raw)

    barrier = pltpu.get_barrier_semaphore()
    for peer in PEERS:
        pl.semaphore_signal(barrier, inc=1, device_id=near(peer), device_id_type=MESH)
    pl.semaphore_wait(barrier, len(PEERS))

    def start_xz(base, ref, depth):
        depths = depth if isinstance(depth, tuple) else (depth, depth)
        nx, nz = ref.shape[0] - 2 * depths[0], ref.shape[1] - 2 * depths[1]

        def part(n, side, depth):
            own, rim = pl.ds(depth, n), pl.ds(depth, depth)
            if side == 0:
                return own, own
            if side < 0:
                return rim, pl.ds(n + depth, depth)
            return pl.ds(n, depth), pl.ds(0, depth)

        copies = []
        for number, (dx, dz) in enumerate(((-1, -1), (-1, 1), (1, -1), (1, 1), (-1, 0), (1, 0), (0, -1), (0, 1))):
            (src_x, dst_x), (src_z, dst_z) = part(nx, dx, depths[0]), part(nz, dz, depths[1])
            copies.append(message(base + number, ref.at[src_x, src_z], ref.at[dst_x, dst_z], dx, 0, dz))
        return start(copies)

    def clear_rim(ref, depth):
        dx, dz = depth if isinstance(depth, tuple) else (depth, depth)
        nx, nz = ref.shape[0], ref.shape[1]
        for edge, index in (
            (at_low("gx"), (pl.ds(0, dx),)), (at_high("gx"), (pl.ds(nx - dx, dx),)),
            (at_low("gz"), (pl.ds(0, nx), pl.ds(0, dz))), (at_high("gz"), (pl.ds(0, nx), pl.ds(nz - dz, dz))),
        ):
            @pl.when(edge)
            def _():
                ref[index] = jnp.zeros(ref.at[index].shape, BF)

    def wait_xz(copies, ref, s):
        arrived(copies)
        clear_rim(ref, 1)
        nx, nz = ref.shape[0], ref.shape[1]
        for plane in (0, nx - 1):
            s[plane, :, 8:24] = ref[plane].astype(F32)
        for plane in (0, nz - 1):
            s[1:nx - 1, plane, 8:24] = ref[1:nx - 1, plane].astype(F32)

    def start_y(base, s, ys, yr):
        count = ys.shape[1]
        rows = s.reshape(s.shape[0] * s.shape[1] * 32, 128)
        ys[0] = rows[pl.ds(8, count, stride=32), :].astype(BF)
        ys[1] = rows[pl.ds(23, count, stride=32), :].astype(BF)
        return start([
            message(base + 8, ys.at[0], yr.at[1], 0, -1, 0),
            message(base + 9, ys.at[1], yr.at[0], 0, 1, 0),
        ])

    def wait_y(copies, s, yr):
        arrived(copies)
        count = yr.shape[1]
        rows = s.reshape(s.shape[0] * s.shape[1] * 32, 128)
        low = jnp.where(at_low("gy"), 0.0, yr[0].astype(F32))
        high = jnp.where(at_high("gy"), 0.0, yr[1].astype(F32))
        rows[pl.ds(7, count, stride=32), :] = low
        rows[pl.ds(24, count, stride=32), :] = high

    def beside(s, dst, planes):
        lane = lax.broadcasted_iota(jnp.int32, dst.shape[1:], 2)

        def plane(x, carry):
            dst[x] = jnp.where(lane < 64, s[x, :, 9:25], s[x, :, 7:23]).astype(BF)
            return carry

        lax.fori_loop(0, planes, plane, 0)

    def beside_both(s, up, down, planes):
        def plane(x, carry):
            up[x] = s[x, :, 9:25].astype(BF)
            down[x] = s[x, :, 7:23].astype(BF)
            return carry

        lax.fori_loop(0, planes, plane, 0)

    def spread(raw, first, dst):
        dst[...] = jnp.zeros(dst.shape, BF)

        def one(p, carry):
            for r in range(3):
                taps = [raw[p, q, r, first:first + 64, :] for q in range(3)]
                none = jnp.zeros_like(taps[0])
                pairs = ((taps[1], taps[0]), (taps[2], taps[1]), (none, taps[2]), (taps[0], none))
                for slot, pair in enumerate(pairs):
                    block = jnp.concatenate(pair, axis=1)
                    for dz in range(2):
                        dst[p, r + dz, slot, :, dz * 128:(dz + 1) * 128] = block
            return carry

        lax.fori_loop(0, 3, one, 0)

    def fine_window(ref, side, x, count):
        ref, side = (value.reshape(NXF + 2, 9, 2, ROWS, 128) for value in (ref, side))
        parts = []
        for p in range(3):
            for zo in range(4):
                index = (pl.ds(x + p, count), pl.ds(zo // 2, 8), zo % 2)
                parts += [cells(ref, *index), cells(side, *index)]
        return jnp.concatenate(parts, axis=1)

    loads["vol"].wait()
    fine_rows = s_fine.reshape((NXF + 3) * (NZF + 2) * 32, 128)

    def turn_in(x, carry):
        for y in range(ROWS):
            pair = jnp.concatenate([vol_v[x, 2 * y], vol_v[x, 2 * y + 1]], axis=1)
            fine_rows[pl.ds(((x + 1) * (NZF + 2) + 1) * 32 + 8 + y, NZF, stride=32), :] = pair.astype(F32)
        r_in[x + 1, 1:NZF + 1] = s_fine[x + 1, 1:NZF + 1, 8:24].astype(BF)
        return carry

    lax.fori_loop(0, NXF, turn_in, 0)
    going = start_xz(0, r_in, 1)
    loads["wf"].wait()
    spread(wf_raw, 0, w_fine)
    w_mid[:, :, 1] = jnp.zeros((3, 4, 64, 256), BF)
    w_mid[:, 3, :, :, 0:128] = jnp.zeros((3, 4, 64, 128), BF)
    w_mid[:, 0, :, :, 128:256] = jnp.zeros((3, 4, 64, 128), BF)
    w_rm_skip[:, 3, :, :, 0:128] = jnp.zeros((3, 3, 128, 128), BF)
    w_rm_skip[:, 0, :, :, 128:256] = jnp.zeros((3, 3, 128, 128), BF)
    loads["wrf"].wait()
    spread(wrf_raw, 0, w_skip)
    wait_xz(going, r_in, s_fine)
    going = start_y(0, s_fine, y_in, yr_in)
    loads["wrm_raw"].wait()

    def sums(parts):
        return (parts[0], parts[1] + parts[2], parts[0] + parts[1], parts[2])

    def rise_mid(chunk, carry):
        rows = pl.ds(pl.multiple_of(chunk * 16, 16), 16)
        for q, slot in ((1, 0), (2, 1), (0, 2)):
            by_r = [sums([wrm_raw[p, q, r, rows, :].astype(F32) for p in range(3)]) for r in range(3)]
            for x_sum in range(4):
                z_sums = sums([by_r[r][x_sum] for r in range(3)])
                for z_sum, (zt, dz) in enumerate(((0, 0), (1, 0), (1, 1), (2, 1))):
                    w_rm_up[x_sum, zt, slot, rows, dz * 128:(dz + 1) * 128] = z_sums[z_sum].astype(BF)
        return carry

    w_rm_up[:, 0, :, :, 128:256] = jnp.zeros((4, 3, 256, 128), BF)
    w_rm_up[:, 2, :, :, 0:128] = jnp.zeros((4, 3, 256, 128), BF)
    lax.fori_loop(0, 16, rise_mid, 0)

    wait_y(going, s_fine, yr_in)
    beside(s_fine, h_in, NXF + 2)

    w_fine_all = w_fine.reshape(3072, 256)

    bias_fine = jnp.concatenate([bf_ref[...]] * 4, axis=1)
    bias_last = jnp.concatenate([brf_ref[...]] * 4, axis=1)
    r_enc_pairs = r_enc.reshape(NXF + 2, 9, 2, ROWS, 128)
    s_fine_pairs = s_fine.reshape(NXF + 3, 9, 2, 32, 128)
    r_pool_pairs = r_pool.reshape(NXM + 2, 5, 2, ROWS, 128)
    s_pool_pairs = s_pool.reshape(NXM + 4, 5, 2, 32, 128)

    def fine(pair, carry):
        x = 2 * pair
        result = dot(fine_window(r_in, h_in, x, 2), w_fine_all[...])
        result = jnp.maximum(result + bias_fine, 0.0).reshape(2, 8, ROWS, 256)
        for index, half in (((pl.ds(0, 8), 1), 0), ((pl.ds(1, 8), 0), 1)):
            value = result[..., half * 128:(half + 1) * 128]
            r_enc_pairs[(pl.ds(x + 1, 2),) + index] = value.astype(BF)
            s_fine_pairs[(pl.ds(x + 1, 2),) + index + (pl.ds(8, 16),)] = value
        most = jnp.max(result, axis=0)
        most = jnp.maximum(most[..., 0:128], most[..., 128:256]).reshape(128, 128)
        most = jnp.maximum(most, pltpu.roll(most, 64, 1)).reshape(4, 2, ROWS, 128)
        for index, half in (((pl.ds(0, 4), 1), 0), ((pl.ds(1, 4), 0), 1)):
            r_pool_pairs[(pair + 1,) + index] = most[:, half].astype(BF)
            s_pool_pairs[(pair + 1,) + index + (pl.ds(8, 16),)] = most[:, half]
        return carry

    lax.fori_loop(0, 8, fine, 0)

    going = start_xz(10, r_pool, 1)
    skipping = start_xz(20, r_enc, 1)

    def rise_fine(chunk, carry):
        src = pl.ds(pl.multiple_of(64 + chunk * 16, 16), 16)
        rows = pl.ds(pl.multiple_of(chunk * 16, 16), 16)
        by_q = []
        for q in range(3):
            by_r = [sums([wrf_raw[p, q, r, src, :].astype(F32) for p in range(3)]) for r in range(3)]
            by_q.append([sums([by_r[r][x_sum] for r in range(3)]) for x_sum in range(4)])
        none = jnp.zeros((16, 64), F32)
        for x_sum in range(4):
            for z_sum, (zt, dz) in enumerate(((0, 0), (1, 0), (1, 1), (2, 1))):
                taps = [by_q[q][x_sum][z_sum] for q in range(3)]
                pairs = ((taps[1] + taps[2], taps[0] + taps[1]), (none, taps[2]), (taps[0], none))
                for slot, pair in enumerate(pairs):
                    block = jnp.concatenate(pair, axis=1).astype(BF)
                    w_rf_up[x_sum, zt, slot, rows, dz * 128:(dz + 1) * 128] = block
        return carry

    w_rf_up[:, 0, :, :, 128:256] = jnp.zeros((4, 3, 128, 128), BF)
    w_rf_up[:, 2, :, :, 0:128] = jnp.zeros((4, 3, 128, 128), BF)
    lax.fori_loop(0, 8, rise_fine, 0)

    wait_xz(going, r_pool, s_pool)
    going = start_y(10, s_pool, y_pool, yr_pool)
    wait_xz(skipping, r_enc, s_fine)
    skipping = start_y(20, s_fine, y_enc, yr_enc)
    for dz in range(2):
        for q in range(3):
            loads[("wm", dz, q)].wait()
    wait_y(going, s_pool, yr_pool)
    beside(s_pool, h_pool, NXM + 2)

    parts = []
    for p in range(3):
        for zo in range(4):
            index = (pl.ds(p, 8), pl.ds(zo // 2, 4), zo % 2)
            parts += [cells(ref, *index) for ref in (r_pool_pairs, h_pool.reshape(NXM + 2, 5, 2, ROWS, 128))]
    result = dot(jnp.concatenate(parts, axis=1), w_mid.reshape(3072, 256)[...])
    r_mid_pairs, hu_mid_pairs, hd_mid_pairs, r_dec_pairs = (
        ref.reshape(5, 2, 5, 2, ROWS, 128) for ref in (r_mid, hu_mid, hd_mid, r_dec)
    )
    s_mid_pairs, s_dec_pairs = (ref.reshape(6, 2, 5, 2, 32, 128) for ref in (s_mid, s_dec))
    bias_mid = jnp.concatenate([bm_ref[...]] * 2, axis=1)
    bias_rise = jnp.concatenate([brm_ref[...]] * 2, axis=1)
    result = jnp.maximum(result + bias_mid, 0.0).reshape(4, 2, 4, ROWS, 256)
    for dz, index in enumerate(((pl.ds(0, 4), 1), (pl.ds(1, 4), 0))):
        value = result[..., dz * 128:(dz + 1) * 128]
        for dx in range(2):
            place = (pl.ds(0, 4), 1) if dx == 0 else (pl.ds(1, 4), 0)
            r_mid_pairs[place + index] = value[:, dx].astype(BF)
            s_mid_pairs[place + index + (pl.ds(8, 16),)] = value[:, dx]
    most = jnp.maximum(result[:, 0], result[:, 1])
    pair_tmp[...] = jnp.maximum(most[..., 0:128], most[..., 128:256]).reshape(256, 128)
    low = jnp.maximum(pair_tmp[pl.ds(0, 128, stride=2), :], pair_tmp[pl.ds(1, 128, stride=2), :])
    r_low[2:6, 1:3] = low.astype(BF).reshape(4, 2, ROWS, 128)

    going = start_xz(30, r_low, (2, 1))
    middle = start_xz(40, r_mid, 1)

    wait_y(skipping, s_fine, yr_enc)
    beside(s_fine, h_enc, NXF + 2)
    w_skip_all = w_skip.reshape(3072, 256)

    def skip_part(pair, carry):
        x = 2 * pair
        result = dot(fine_window(r_enc, h_enc, x, 2), w_skip_all[...]) + bias_last
        skip[pl.ds(x, 2)] = result.reshape(2, 128, 256)
        return carry

    lax.fori_loop(0, 3, skip_part, 0)
    arrived(going)
    clear_rim(r_low, (2, 1))
    low = r_low[...].astype(F32).reshape(8, 4, 2, 8, 128).reshape(8, 8, 8, 128)
    s_low[:, :, 8:16] = low
    s_low[:, :, 0:8] = jnp.zeros_like(low)
    s_low[:, :, 16:24] = jnp.zeros_like(low)
    rows = s_low.reshape(2048, 128)
    for number, row in enumerate((8, 9, 14, 15)):
        y_low[number // 2, pl.ds((number % 2) * 64, 64), :] = rows[pl.ds(row, 64, stride=32), :].astype(BF)
    going = start([
        message(38, y_low.at[0], yr_low.at[1], 0, -1, 0),
        message(39, y_low.at[1], yr_low.at[0], 0, 1, 0),
    ])
    wait_xz(middle, r_mid, s_mid)
    middle = start_y(40, s_mid, y_mid, yr_mid)
    for q in range(3):
        loads[("wb", q)].wait()
    lax.fori_loop(3, 5, skip_part, 0)
    arrived(going)
    for number, row in enumerate((6, 7, 16, 17)):
        edge = at_low("gy") if number < 2 else at_high("gy")
        value = yr_low[number // 2, pl.ds((number % 2) * 64, 64), :].astype(F32)
        rows[pl.ds(row, 64, stride=32), :] = jnp.where(edge, 0.0, value)

    def low_plane(x, carry):
        for slot, first in enumerate((4, 5, 3)):
            low_lanes[x, :, :, slot * 128:(slot + 1) * 128] = s_low[x, :, first:first + 16].astype(BF)
        return carry

    lax.fori_loop(0, 8, low_plane, 0)
    parts = [cells(low_lanes, pl.ds(p, 6), pl.ds(r, 6)) for p in range(3) for r in range(3)]
    result = dot(jnp.concatenate(parts, axis=1), w_bottom.reshape(3456, 256)[...])
    result = jnp.maximum(result + bb_ref[...], 0.0).reshape(6, 6, ROWS, 256)
    index = lax.broadcasted_iota(jnp.int32, (6, 6, ROWS, 256), 0)
    zindex = lax.broadcasted_iota(jnp.int32, (6, 6, ROWS, 256), 1)
    yindex = lax.broadcasted_iota(jnp.int32, (6, 6, ROWS, 256), 2)
    outside = False
    for where, first, last, axis in ((index, 0, 5, "gx"), (zindex, 0, 5, "gz"), (yindex, 3, 12, "gy")):
        outside = outside | ((where == first) & at_low(axis)) | ((where == last) & at_high(axis))
    result = jnp.where(outside, 0.0, result).reshape(576, 256)
    for half in range(2):
        bottom_tmp[half] = result[:, half * 128:(half + 1) * 128]

    for half in range(2):
        doubled = s_up.at[half].reshape(36 * 32, 128)
        for step in range(10):
            value = bottom_tmp.at[half][pl.ds(3 + step, 36, stride=16), :]
            doubled[pl.ds(6 + 2 * step, 36, stride=32), :] = value
            doubled[pl.ds(7 + 2 * step, 36, stride=32), :] = value
    for slot, first in enumerate((8, 9, 7)):
        for half in range(2):
            lanes = slice(slot * 256 + half * 128, slot * 256 + half * 128 + 128)
            up_lanes[:, :, :, lanes] = s_up[half, :, first:first + 16].astype(BF).reshape(6, 6, ROWS, 128)

    wait_y(middle, s_mid, yr_mid)
    beside_both(s_mid, hu_mid, hd_mid, NXM + 2)
    for dz in range(2):
        for q in range(3):
            loads[("wrm", dz, q)].wait()

    for dx in range(2):
        parts = []
        for p in range(3):
            for zo in range(4):
                index = (pl.ds((dx + p) // 2, 4), (dx + p) % 2, pl.ds(zo // 2, 4), zo % 2)
                parts += [cells(ref, *index) for ref in (r_mid_pairs, hu_mid_pairs, hd_mid_pairs)]
        result = dot(jnp.concatenate(parts, axis=1), w_rm_skip.reshape(4608, 256)[...])
        parts = []
        for xt in range(2):
            for zt in range(3):
                parts.append(cells(up_lanes, pl.ds(xt + dx, 4), pl.ds(zt, 4)))
        weight = w_rm_up.reshape(2, 4608, 256)[dx]
        result = result + dot(jnp.concatenate(parts, axis=1), weight)
        result = jnp.maximum(result + bias_rise, 0.0).reshape(4, 4, ROWS, 256)
        for dz, index in enumerate(((pl.ds(0, 4), 1), (pl.ds(1, 4), 0))):
            place = (pl.ds(0, 4), 1) if dx == 0 else (pl.ds(1, 4), 0)
            value = result[..., dz * 128:(dz + 1) * 128]
            r_dec_pairs[place + index] = value.astype(BF)
            s_dec_pairs[place + index + (pl.ds(8, 16),)] = value

    going = start_xz(50, r_dec, 1)
    lax.fori_loop(5, 7, skip_part, 0)
    wait_xz(going, r_dec, s_dec)
    going = start_y(50, s_dec, y_dec, yr_dec)
    lax.fori_loop(7, 8, skip_part, 0)
    wait_y(going, s_dec, yr_dec)
    beside_both(s_dec, hu_dec, hd_dec, NXM + 2)

    weight = w_rf_up.reshape(2, 2304, 256)
    turn_rows = turn.reshape(4 * NZF * ROWS, 128)

    def leave(step):
        planes = pl.ds(4 * step, 4)
        return pltpu.make_async_copy(out_v.at[planes], out_hbm.at[planes], local_sem.at[len(loads) + step])

    def last(step, carry):
        x = 2 * step
        for dx in range(2):
            parts = []
            for xt in range(2):
                for zt in range(3):
                    parts += [cells(ref, pl.ds(x + xt + dx, 2), pl.ds(zt, 8)) for ref in (r_dec, hu_dec, hd_dec)]
            result = dot(jnp.concatenate(parts, axis=1), weight[dx]).reshape(2, 128, 256)
            for i in range(2):
                value = (result[i] + skip[4 * step + 2 * i + dx]).reshape(8, ROWS, 256)
                for dz in range(2):
                    turn[2 * i + dx, :, dz] = value[..., dz * 128:(dz + 1) * 128]
        for i in range(4):
            for y in range(ROWS):
                value = turn_rows[pl.ds(i * NZF * ROWS + y, NZF, stride=ROWS), :].astype(BF)
                out_v[4 * step + i, 2 * y] = value[:, 0:64]
                out_v[4 * step + i, 2 * y + 1] = value[:, 64:128]
        leave(step).start()
        return carry

    lax.fori_loop(0, 4, last, 0)
    for message_sent in sent:
        message_sent.wait_send()
    for step in range(4):
        leave(step).wait()


def scratch():
    vmem = pltpu.VMEM
    fine = (NXF + 2, NZF + 2, ROWS, 128)
    mid = pool = (NXM + 2, NZM + 2, ROWS, 128)
    mid_s = (NXM + 4, NZM + 2, 32, 128)
    return [
        vmem(fine, BF), vmem(fine, BF), vmem((NXF + 3, NZF + 2, 32, 128), F32), vmem((2, TF, 128), BF), vmem((2, TF, 128), BF),
        vmem(fine, BF), vmem(fine, BF), vmem((2, TF, 128), BF), vmem((2, TF, 128), BF),
        vmem(pool, BF), vmem(pool, BF), vmem(mid_s, F32), vmem((2, TM, 128), BF), vmem((2, TM, 128), BF),
        vmem(mid, BF), vmem(mid, BF), vmem(mid, BF), vmem(mid_s, F32), vmem((2, TM, 128), BF), vmem((2, TM, 128), BF),
        vmem((8, 4, ROWS, 128), BF), vmem((8, 8, 32, 128), F32), vmem((2, 128, 128), BF), vmem((2, 128, 128), BF),
        vmem((256, 128), F32),
        vmem((8, 8, ROWS, 384), BF), vmem((2, 576, 128), F32), vmem((2, 36, 32, 128), F32), vmem((6, 6, ROWS, 768), BF),
        vmem(mid, BF), vmem(mid, BF), vmem(mid, BF), vmem(mid_s, F32), vmem((2, TM, 128), BF), vmem((2, TM, 128), BF),
        vmem((3, 3, 3, 64, 64), BF), vmem((3, 3, 3, 192, 64), BF), vmem((3, 3, 3, 256, 128), BF),
        vmem((3, 4, 4, 64, 256), BF), vmem((3, 4, 4, 64, 256), BF), vmem((3, 4, 4, 64, 256), BF),
        vmem((3, 3, 3, 128, 256), BF), vmem((3, 4, 3, 128, 256), BF), vmem((4, 3, 3, 256, 256), BF),
        vmem((4, 3, 3, 128, 256), BF),
        vmem((NXF, 128, 256), F32), vmem((NXF, 32, NZF, 64), BF), vmem((NXF, 32, NZF, 64), BF),
        vmem((4, 8, 2, ROWS, 128), F32),
        pltpu.SemaphoreType.DMA((10 * LEVELS,)), pltpu.SemaphoreType.DMA((10 * LEVELS,)), pltpu.SemaphoreType.DMA((32,)),
    ]


def on_device(sizes, volume, wf, bf, wm, bm, wb, bb, wrm, brm, wrf, brf):
    hbm = pl.BlockSpec(memory_space=pl.ANY)
    return pl.pallas_call(
        functools.partial(kernel, sizes),
        out_shape=jax.ShapeDtypeStruct((NXF, 32, NZF, 64), BF),
        in_specs=[hbm] * 6 + [pl.BlockSpec(memory_space=pltpu.VMEM)] * 5,
        out_specs=hbm,
        scratch_shapes=scratch(),
        compiler_params=pltpu.CompilerParams(
            collective_id=0, has_side_effects=True, vmem_limit_bytes=62 * 2**20
        ),
    )(volume, wf, wm, wb, wrm, wrf, *(bias.reshape(1, -1) for bias in (bf, bm, bb, brm, brf)))


def solution(mesh):
    return jax.shard_map(
        functools.partial(on_device, dict(mesh.shape)),
        mesh=mesh,
        in_specs=(P("gx", "gy", "gz", None),) + (P(),) * 10,
        out_specs=P("gx", "gy", "gz", None),
        check_vma=False,
    )
```

```python
import functools

import jax
import jax.numpy as jnp
from jax import lax
from jax.experimental import pallas as pl
from jax.experimental.pallas import tpu as pltpu
from jax.sharding import PartitionSpec as P

BF = jnp.bfloat16
F32 = jnp.float32
MESH = pl.DeviceIdType.MESH

NXF, NZF, ROWS = 16, 16, 16
NXM, NZM = 8, 8
TF, TM = 352, 112
LEVELS = 6
PEERS = [(x, 0, z) for x in (-1, 0, 1) for z in (-1, 0, 1) if x or z] + [(0, -1, 0), (0, 1, 0)]


def dot(a, b):
    return jnp.dot(a, b, preferred_element_type=F32)


def cells(ref, *index):
    value = ref[index]
    return value.reshape(-1, value.shape[-1])


def kernel(
    sizes,
    vol, wf_hbm, wm_hbm, wb_hbm, wrm_hbm, wrf_hbm, bf_ref, bm_ref, bb_ref, brm_ref, brf_ref,
    out_v,
    r_in, h_in, rim_in, side_in, y_in, yr_in,
    r_enc, h_enc, rim_enc, side_enc, y_enc, yr_enc,
    s_fine, s_rim, y_wide, y_grid, y_window,
    r_pool, h_pool, s_pool, y_pool, yr_pool,
    r_mid, hu_mid, hd_mid, s_mid, y_mid, yr_mid,
    r_low, s_low, y_low, yr_low, pair_tmp,
    low_lanes, bottom_tmp, s_up, up_lanes,
    r_dec, hu_dec, hd_dec, rim_dec, up_dec, down_dec, y_dec, yr_dec, s_dec, s_dec_rim, y_dec_wide, y_dec_grid, y_dec_window,
    wf_raw, wrf_raw, wrm_raw,
    w_fine, w_skip, w_mid, w_bottom, w_rm_skip, w_rm_up, w_rf_up,
    acc, vol_v,
    send_sem, recv_sem, local_sem,
):
    spots = {axis: lax.axis_index(axis) for axis in ("gx", "gy", "gz")}

    def near(steps):
        return {
            axis: lax.rem(spots[axis] + (step + sizes[axis]), sizes[axis]) for axis, step in zip(sizes, steps) if step
        }

    def at_low(axis):
        return spots[axis] == 0

    def at_high(axis):
        return spots[axis] == sizes[axis] - 1

    def message(number, src, dst, *steps):
        return pltpu.make_async_remote_copy(
            src_ref=src, dst_ref=dst, send_sem=send_sem.at[number], recv_sem=recv_sem.at[number],
            device_id=near(steps), device_id_type=MESH,
        )

    sent = []

    def start(copies):
        for copy in copies:
            copy.start()
        sent.extend(copies)
        return copies

    def arrived(copies):
        for copy in copies:
            copy.wait_recv()

    loads = {}

    def load(name, src, dst):
        copy = pltpu.make_async_copy(src, dst, local_sem.at[len(loads)])
        copy.start()
        loads[name] = copy

    load("vol", vol, vol_v)
    load("wf", wf_hbm, wf_raw)
    load("wrf", wrf_hbm, wrf_raw)
    for dz in range(2):
        lanes = pl.ds(dz * 128, 128)
        for q, slot in ((1, 0), (2, 2), (0, 3)):
            load(("wm", dz, q), wm_hbm.at[:, q], w_mid.at[:, dz:dz + 3, slot, :, lanes])
    for q, slot in ((1, 0), (2, 1), (0, 2)):
        load(("wb", q), wb_hbm.at[:, q], w_bottom.at[:, :, slot])
    for dz in range(2):
        lanes = pl.ds(dz * 128, 128)
        for q, slot in ((1, 0), (2, 1), (0, 2)):
            load(("wrm", dz, q), wrm_hbm.at[:, q, :, 0:128, :], w_rm_skip.at[:, dz:dz + 3, slot, :, lanes])
    load("wrm_raw", wrm_hbm.at[:, :, :, 128:384, :], wrm_raw)

    for ref in (r_in, h_in, r_enc, h_enc, r_dec, hu_dec, hd_dec):
        nx, nz = ref.shape[0], ref.shape[1]
        for plane in (0, nx - 1):
            ref[plane] = jnp.zeros(ref.shape[1:], BF)
        for plane in (0, nz - 1):
            ref[:, plane] = jnp.zeros((nx, ROWS, 128), BF)
    for ref in (rim_in, rim_enc, rim_dec, side_in, side_enc, up_dec, down_dec):
        for end in (0, ref.shape[1] - 1):
            ref[0:2, end] = jnp.zeros((2, ROWS, 128), BF)
    for ref, count in ((s_fine, 256), (s_dec, 64), (s_rim, 96), (s_dec_rim, 48)):
        rows = ref.reshape(count * 32, 128)
        for row in (7, 24):
            rows[pl.ds(row, count, stride=32), :] = jnp.zeros((count, 128), F32)

    barrier = pltpu.get_barrier_semaphore()
    for peer in PEERS:
        pl.semaphore_signal(barrier, inc=1, device_id=near(peer), device_id_type=MESH)
    pl.semaphore_wait(barrier, len(PEERS))

    def start_xz(base, ref, depth):
        depths = depth if isinstance(depth, tuple) else (depth, depth)
        nx, nz = ref.shape[0] - 2 * depths[0], ref.shape[1] - 2 * depths[1]

        def part(n, side, depth):
            own, rim = pl.ds(depth, n), pl.ds(depth, depth)
            if side == 0:
                return own, own
            if side < 0:
                return rim, pl.ds(n + depth, depth)
            return pl.ds(n, depth), pl.ds(0, depth)

        copies = []
        for number, (dx, dz) in enumerate(((-1, -1), (-1, 1), (1, -1), (1, 1), (-1, 0), (1, 0), (0, -1), (0, 1))):
            (src_x, dst_x), (src_z, dst_z) = part(nx, dx, depths[0]), part(nz, dz, depths[1])
            copies.append(message(base + number, ref.at[src_x, src_z], ref.at[dst_x, dst_z], dx, 0, dz))
        return start(copies)

    def clear_rim(ref, depth):
        dx, dz = depth if isinstance(depth, tuple) else (depth, depth)
        nx, nz = ref.shape[0], ref.shape[1]
        for edge, index in (
            (at_low("gx"), (pl.ds(0, dx),)), (at_high("gx"), (pl.ds(nx - dx, dx),)),
            (at_low("gz"), (pl.ds(0, nx), pl.ds(0, dz))), (at_high("gz"), (pl.ds(0, nx), pl.ds(nz - dz, dz))),
        ):
            @pl.when(edge)
            def _():
                ref[index] = jnp.zeros(ref.at[index].shape, BF)

    def wait_xz(copies, ref, s):
        arrived(copies)
        clear_rim(ref, 1)
        nx, nz = ref.shape[0], ref.shape[1]
        for plane in (0, nx - 1):
            s[plane, :, 8:24] = ref[plane].astype(F32)
        for plane in (0, nz - 1):
            s[1:nx - 1, plane, 8:24] = ref[1:nx - 1, plane].astype(F32)

    def start_y(base, s, ys, yr):
        count = ys.shape[1]
        rows = s.reshape(s.shape[0] * s.shape[1] * 32, 128)
        ys[0] = rows[pl.ds(8, count, stride=32), :].astype(BF)
        ys[1] = rows[pl.ds(23, count, stride=32), :].astype(BF)
        return start([
            message(base + 8, ys.at[0], yr.at[1], 0, -1, 0),
            message(base + 9, ys.at[1], yr.at[0], 0, 1, 0),
        ])

    def wait_y(copies, s, yr):
        arrived(copies)
        count = yr.shape[1]
        rows = s.reshape(s.shape[0] * s.shape[1] * 32, 128)
        low = jnp.where(at_low("gy"), 0.0, yr[0].astype(F32))
        high = jnp.where(at_high("gy"), 0.0, yr[1].astype(F32))
        rows[pl.ds(7, count, stride=32), :] = low
        rows[pl.ds(24, count, stride=32), :] = high

    def start_rims(base, ref, rim):
        nx, nz = ref.shape[0] - 2, ref.shape[1] - 2
        own_x, own_z = pl.ds(1, nx), pl.ds(1, nz)
        return start([
            message(base, ref.at[1, 1], rim.at[3, nx + 1], -1, 0, -1),
            message(base + 1, ref.at[1, nz], rim.at[2, nx + 1], -1, 0, 1),
            message(base + 2, ref.at[nx, 1], rim.at[3, 0], 1, 0, -1),
            message(base + 3, ref.at[nx, nz], rim.at[2, 0], 1, 0, 1),
            message(base + 4, ref.at[1, own_z], rim.at[1, own_z], -1, 0, 0),
            message(base + 5, ref.at[nx, own_z], rim.at[0, own_z], 1, 0, 0),
            message(base + 6, ref.at[own_x, 1], rim.at[3, own_x], 0, 0, -1),
            message(base + 7, ref.at[own_x, nz], rim.at[2, own_x], 0, 0, 1),
        ])

    def wait_rims(copies, rim, s):
        arrived(copies)
        n = rim.shape[1] - 2
        empty = jnp.zeros((n + 2, ROWS, 128), BF)
        for edge, side, end in (
            (at_low("gx"), 0, 0), (at_high("gx"), 1, n + 1), (at_low("gz"), 2, None), (at_high("gz"), 3, None),
        ):
            @pl.when(edge)
            def _():
                rim[side] = empty
                if end is not None:
                    rim[2:4, end] = empty[0:2]

        s[0:n, 8:24] = rim[0, 1:n + 1].astype(F32)
        s[n:2 * n, 8:24] = rim[1, 1:n + 1].astype(F32)
        s[2 * n:3 * n + 2, 8:24] = rim[2].astype(F32)
        s[4 * n:5 * n + 2, 8:24] = rim[3].astype(F32)

    def start_rows(base, s, s_side, ys, yr):
        count, more = s.shape[0] * s.shape[1], s_side.shape[0]
        rows, side_rows = s.reshape(count * 32, 128), s_side.reshape(more * 32, 128)
        for number, row in enumerate((8, 23)):
            ys[number, 0:count] = rows[pl.ds(row, count, stride=32), :].astype(BF)
            ys[number, count:count + more] = side_rows[pl.ds(row, more, stride=32), :].astype(BF)
        return start([
            message(base + 8, ys.at[0], yr.at[1], 0, -1, 0),
            message(base + 9, ys.at[1], yr.at[0], 0, 1, 0),
        ])

    def wait_rows(copies, s_side, yr, wide, grid, window, step):
        arrived(copies)
        more = s_side.shape[0]
        count = yr.shape[1] - more
        n = grid.shape[1] - 2
        for number, edge in enumerate((at_low("gy"), at_high("gy"))):
            value = jnp.where(edge, 0.0, yr[number].astype(F32))
            wide[number] = value
            grid[number, 1:n + 1, 8:8 + n] = value[0:count].reshape(n, n, 128)
            grid[number, 0, 8:8 + n] = value[count:count + n]
            grid[number, n + 1, 8:8 + n] = value[count + n:count + 2 * n]
            flat = grid.at[number].reshape((n + 2) * 32, 128)
            flat[pl.ds(7, n + 2, stride=32), :] = wide[number, count + 2 * n:count + 3 * n + 2]
            flat[pl.ds(8 + n, n + 2, stride=32), :] = wide[number, count + 4 * n:count + 5 * n + 2]

            def gather(x, carry):
                for tap in range(window.shape[1]):
                    window[number, tap, x] = flat[pl.ds(x * 32 + 7 + tap, 8, stride=step), :]
                return carry

            lax.fori_loop(0, n + 2, gather, 0)

    def select_rows(s, index):
        lane = lax.broadcasted_iota(jnp.int32, (ROWS, 128), 1)
        return jnp.where(lane < 64, s[index + (slice(9, 25),)], s[index + (slice(7, 23),)]).astype(BF)

    def beside(s, dst, planes):
        lane = lax.broadcasted_iota(jnp.int32, dst.shape[1:], 2)

        def plane(x, carry):
            dst[x] = jnp.where(lane < 64, s[x, :, 9:25], s[x, :, 7:23]).astype(BF)
            return carry

        lax.fori_loop(0, planes, plane, 0)

    def beside_both(s, up, down, planes):
        def plane(x, carry):
            up[x] = s[x, :, 9:25].astype(BF)
            down[x] = s[x, :, 7:23].astype(BF)
            return carry

        lax.fori_loop(0, planes, plane, 0)

    def spread(raw, first, dst):
        dst[...] = jnp.zeros(dst.shape, BF)

        def one(p, carry):
            for r in range(3):
                taps = [raw[p, q, r, first:first + 64, :] for q in range(3)]
                none = jnp.zeros_like(taps[0])
                pairs = ((taps[1], taps[0]), (taps[2], taps[1]), (none, taps[2]), (taps[0], none))
                for slot, pair in enumerate(pairs):
                    block = jnp.concatenate(pair, axis=1)
                    for dz in range(2):
                        dst[p, r + dz, slot, :, dz * 128:(dz + 1) * 128] = block
            return carry

        lax.fori_loop(0, 3, one, 0)

    def fine_window(ref, side, x, count):
        ref, side = (value.reshape(NXF + 2, 9, 2, ROWS, 128) for value in (ref, side))
        parts = []
        for p in range(3):
            for zo in range(4):
                index = (pl.ds(x + p, count), pl.ds(zo // 2, 8), zo % 2)
                parts += [cells(ref, *index), cells(side, *index)]
        return jnp.concatenate(parts, axis=1)

    acc_rows = acc.reshape(NXF * 8 * 2 * ROWS, 128)
    halves = ((0, slice(0, 128)), (1, slice(128, 256)))

    def fine_own(ref, side, weight, first, last):
        def step(pair, carry):
            x = 2 * pair
            result = dot(fine_window(ref, side, x, 2), weight.reshape(3072, 256)[...])
            for dz, lanes in halves:
                acc[pl.ds(x, 2), :, dz] = result[:, lanes].reshape(2, 8, ROWS, 128)
            return carry

        lax.fori_loop(first, last, step, 0)

    def fine_sides(ref, side):
        def plane(x, carry):
            side[x + 1, 1:NZF + 1] = select_rows(ref, (x, slice(None)))
            return carry

        lax.fori_loop(0, NXF, plane, 0)

    def fine_rims(rim, side, weight):
        n = NXF
        side[0, 1:n + 1] = select_rows(s_rim, (slice(0, n),))
        side[1, 1:n + 1] = select_rows(s_rim, (slice(n, 2 * n),))
        side[2] = select_rows(s_rim, (slice(2 * n, 3 * n + 2),))
        side[3] = select_rows(s_rim, (slice(4 * n, 5 * n + 2),))
        rim_pairs, side_pairs = (value.reshape(4, 9, 2, ROWS, 128) for value in (rim, side))
        for low_high, x, p in ((0, 0, 0), (1, NXF - 1, 2)):
            parts = []
            for zo in range(4):
                index = (low_high, pl.ds(zo // 2, 8), zo % 2)
                parts += [cells(rim_pairs, *index), cells(side_pairs, *index)]
            result = dot(jnp.concatenate(parts, axis=1), weight[p].reshape(1024, 256))
            for dz, lanes in halves:
                acc[x, :, dz] += result[:, lanes].reshape(8, ROWS, 128)
        for low_high, z, zo in ((2, 0, 0), (3, 7, 3)):
            parts = []
            for p in range(3):
                parts += [cells(rim, low_high, pl.ds(p, NXF)), cells(side, low_high, pl.ds(p, NXF))]
            result = dot(jnp.concatenate(parts, axis=1), weight[:, zo].reshape(768, 256))
            for dz, lanes in halves:
                acc[:, z, dz] += result[:, lanes].reshape(NXF, ROWS, 128)

    def fine_ends(weight):
        lane = lax.broadcasted_iota(jnp.int32, (128, 128), 1)
        for number, row in ((0, 0), (1, ROWS - 1)):
            used = (lane >= 64) if number == 0 else (lane < 64)
            parts = []
            for p in range(3):
                for zo in range(4):
                    value = y_window[number, zo, p:p + NXF].reshape(128, 128)
                    parts.append(jnp.where(used, value, 0.0).astype(BF))
            result = dot(jnp.concatenate(parts, axis=1), weight[:, :, 2:4].reshape(1536, 256))
            for dz, lanes in halves:
                acc_rows[pl.ds(dz * ROWS + row, 128, stride=32), :] += result[:, lanes]

    loads["vol"].wait()
    fine_rows = s_fine.reshape(NXF * NZF * 32, 128)

    def turn_in(x, carry):
        for y in range(ROWS):
            pair = jnp.concatenate([vol_v[x, 2 * y], vol_v[x, 2 * y + 1]], axis=1)
            fine_rows[pl.ds(x * NZF * 32 + 8 + y, NZF, stride=32), :] = pair.astype(F32)
        r_in[x + 1, 1:NZF + 1] = s_fine[x, :, 8:24].astype(BF)
        return carry

    lax.fori_loop(0, NXF, turn_in, 0)
    going = start_rims(0, r_in, rim_in)
    fine_sides(s_fine, h_in)
    loads["wf"].wait()
    spread(wf_raw, 0, w_fine)
    fine_own(r_in, h_in, w_fine, 0, 6)
    wait_rims(going, rim_in, s_rim)
    going = start_rows(0, s_fine, s_rim, y_in, yr_in)
    fine_own(r_in, h_in, w_fine, 6, 8)
    fine_rims(rim_in, side_in, w_fine)
    w_mid[:, :, 1] = jnp.zeros((3, 4, 64, 256), BF)
    w_mid[:, 3, :, :, 0:128] = jnp.zeros((3, 4, 64, 128), BF)
    w_mid[:, 0, :, :, 128:256] = jnp.zeros((3, 4, 64, 128), BF)
    w_rm_skip[:, 3, :, :, 0:128] = jnp.zeros((3, 3, 128, 128), BF)
    w_rm_skip[:, 0, :, :, 128:256] = jnp.zeros((3, 3, 128, 128), BF)
    loads["wrf"].wait()
    spread(wrf_raw, 0, w_skip)
    loads["wrm_raw"].wait()

    def sums(parts):
        return (parts[0], parts[1] + parts[2], parts[0] + parts[1], parts[2])

    def rise_mid(chunk, carry):
        rows = pl.ds(pl.multiple_of(chunk * 16, 16), 16)
        for q, slot in ((1, 0), (2, 1), (0, 2)):
            by_r = [sums([wrm_raw[p, q, r, rows, :].astype(F32) for p in range(3)]) for r in range(3)]
            for x_sum in range(4):
                z_sums = sums([by_r[r][x_sum] for r in range(3)])
                for z_sum, (zt, dz) in enumerate(((0, 0), (1, 0), (1, 1), (2, 1))):
                    w_rm_up[x_sum, zt, slot, rows, dz * 128:(dz + 1) * 128] = z_sums[z_sum].astype(BF)
        return carry

    w_rm_up[:, 0, :, :, 128:256] = jnp.zeros((4, 3, 256, 128), BF)
    w_rm_up[:, 2, :, :, 0:128] = jnp.zeros((4, 3, 256, 128), BF)
    lax.fori_loop(0, 16, rise_mid, 0)

    wait_rows(going, s_rim, yr_in, y_wide, y_grid, y_window, 2)
    fine_ends(w_fine)

    bias_fine = jnp.concatenate([bf_ref[...]] * 2, axis=1)
    bias_last = jnp.concatenate([brf_ref[...]] * 2, axis=1)
    r_enc_pairs = r_enc.reshape(NXF + 2, 9, 2, ROWS, 128)
    s_fine_pairs = s_fine.reshape(NXF, 8, 2, 32, 128)
    r_pool_pairs = r_pool.reshape(NXM + 2, 5, 2, ROWS, 128)
    s_pool_pairs = s_pool.reshape(NXM + 4, 5, 2, 32, 128)

    def fine(pair, carry):
        x = 2 * pair
        values = []
        for dz, index in enumerate(((pl.ds(0, 8), 1), (pl.ds(1, 8), 0))):
            value = jnp.maximum(acc[pl.ds(x, 2), :, dz] + bias_fine, 0.0)
            r_enc_pairs[(pl.ds(x + 1, 2),) + index] = value.astype(BF)
            s_fine_pairs[pl.ds(x, 2), :, dz, 8:24] = value
            values.append(value)
        most = jnp.maximum(jnp.max(values[0], axis=0), jnp.max(values[1], axis=0)).reshape(128, 128)
        most = jnp.maximum(most, pltpu.roll(most, 64, 1)).reshape(4, 2, ROWS, 128)
        for index, half in (((pl.ds(0, 4), 1), 0), ((pl.ds(1, 4), 0), 1)):
            r_pool_pairs[(pair + 1,) + index] = most[:, half].astype(BF)
            s_pool_pairs[(pair + 1,) + index + (pl.ds(8, 16),)] = most[:, half]
        return carry

    lax.fori_loop(0, 8, fine, 0)

    going = start_xz(10, r_pool, 1)
    skipping = start_rims(20, r_enc, rim_enc)
    fine_sides(s_fine, h_enc)
    fine_own(r_enc, h_enc, w_skip, 0, 4)

    def rise_fine(chunk, carry):
        src = pl.ds(pl.multiple_of(64 + chunk * 16, 16), 16)
        rows = pl.ds(pl.multiple_of(chunk * 16, 16), 16)
        by_q = []
        for q in range(3):
            by_r = [sums([wrf_raw[p, q, r, src, :].astype(F32) for p in range(3)]) for r in range(3)]
            by_q.append([sums([by_r[r][x_sum] for r in range(3)]) for x_sum in range(4)])
        none = jnp.zeros((16, 64), F32)
        for x_sum in range(4):
            for z_sum, (zt, dz) in enumerate(((0, 0), (1, 0), (1, 1), (2, 1))):
                taps = [by_q[q][x_sum][z_sum] for q in range(3)]
                pairs = ((taps[1] + taps[2], taps[0] + taps[1]), (none, taps[2]), (taps[0], none))
                for slot, pair in enumerate(pairs):
                    block = jnp.concatenate(pair, axis=1).astype(BF)
                    w_rf_up[x_sum, zt, slot, rows, dz * 128:(dz + 1) * 128] = block
        return carry

    w_rf_up[:, 0, :, :, 128:256] = jnp.zeros((4, 3, 128, 128), BF)
    w_rf_up[:, 2, :, :, 0:128] = jnp.zeros((4, 3, 128, 128), BF)
    lax.fori_loop(0, 8, rise_fine, 0)

    wait_xz(going, r_pool, s_pool)
    going = start_y(10, s_pool, y_pool, yr_pool)
    wait_rims(skipping, rim_enc, s_rim)
    skipping = start_rows(20, s_fine, s_rim, y_enc, yr_enc)
    fine_own(r_enc, h_enc, w_skip, 4, 5)
    for dz in range(2):
        for q in range(3):
            loads[("wm", dz, q)].wait()
    wait_y(going, s_pool, yr_pool)
    beside(s_pool, h_pool, NXM + 2)

    parts = []
    for p in range(3):
        for zo in range(4):
            index = (pl.ds(p, 8), pl.ds(zo // 2, 4), zo % 2)
            parts += [cells(ref, *index) for ref in (r_pool_pairs, h_pool.reshape(NXM + 2, 5, 2, ROWS, 128))]
    result = dot(jnp.concatenate(parts, axis=1), w_mid.reshape(3072, 256)[...])
    r_mid_pairs, hu_mid_pairs, hd_mid_pairs, r_dec_pairs = (
        ref.reshape(5, 2, 5, 2, ROWS, 128) for ref in (r_mid, hu_mid, hd_mid, r_dec)
    )
    s_mid_pairs = s_mid.reshape(6, 2, 5, 2, 32, 128)
    s_dec_pairs = s_dec.reshape(4, 2, 4, 2, 32, 128)
    bias_mid = jnp.concatenate([bm_ref[...]] * 2, axis=1)
    bias_rise = jnp.concatenate([brm_ref[...]] * 2, axis=1)
    result = jnp.maximum(result + bias_mid, 0.0).reshape(4, 2, 4, ROWS, 256)
    for dz, index in enumerate(((pl.ds(0, 4), 1), (pl.ds(1, 4), 0))):
        value = result[..., dz * 128:(dz + 1) * 128]
        for dx in range(2):
            place = (pl.ds(0, 4), 1) if dx == 0 else (pl.ds(1, 4), 0)
            r_mid_pairs[place + index] = value[:, dx].astype(BF)
            s_mid_pairs[place + index + (pl.ds(8, 16),)] = value[:, dx]
    most = jnp.maximum(result[:, 0], result[:, 1])
    pair_tmp[...] = jnp.maximum(most[..., 0:128], most[..., 128:256]).reshape(256, 128)
    low = jnp.maximum(pair_tmp[pl.ds(0, 128, stride=2), :], pair_tmp[pl.ds(1, 128, stride=2), :])
    r_low[2:6, 1:3] = low.astype(BF).reshape(4, 2, ROWS, 128)

    going = start_xz(30, r_low, (2, 1))
    middle = start_xz(40, r_mid, 1)

    fine_own(r_enc, h_enc, w_skip, 5, 8)
    fine_rims(rim_enc, side_enc, w_skip)
    arrived(going)
    clear_rim(r_low, (2, 1))
    low = r_low[...].astype(F32).reshape(8, 4, 2, 8, 128).reshape(8, 8, 8, 128)
    s_low[:, :, 8:16] = low
    s_low[:, :, 0:8] = jnp.zeros_like(low)
    s_low[:, :, 16:24] = jnp.zeros_like(low)
    rows = s_low.reshape(2048, 128)
    for number, row in enumerate((8, 9, 14, 15)):
        y_low[number // 2, pl.ds((number % 2) * 64, 64), :] = rows[pl.ds(row, 64, stride=32), :].astype(BF)
    going = start([
        message(38, y_low.at[0], yr_low.at[1], 0, -1, 0),
        message(39, y_low.at[1], yr_low.at[0], 0, 1, 0),
    ])
    wait_xz(middle, r_mid, s_mid)
    middle = start_y(40, s_mid, y_mid, yr_mid)
    for q in range(3):
        loads[("wb", q)].wait()
    wait_rows(skipping, s_rim, yr_enc, y_wide, y_grid, y_window, 2)
    fine_ends(w_skip)
    arrived(going)
    for number, row in enumerate((6, 7, 16, 17)):
        edge = at_low("gy") if number < 2 else at_high("gy")
        value = yr_low[number // 2, pl.ds((number % 2) * 64, 64), :].astype(F32)
        rows[pl.ds(row, 64, stride=32), :] = jnp.where(edge, 0.0, value)

    def low_plane(x, carry):
        for slot, first in enumerate((4, 5, 3)):
            low_lanes[x, :, :, slot * 128:(slot + 1) * 128] = s_low[x, :, first:first + 16].astype(BF)
        return carry

    lax.fori_loop(0, 8, low_plane, 0)
    parts = [cells(low_lanes, pl.ds(p, 6), pl.ds(r, 6)) for p in range(3) for r in range(3)]
    result = dot(jnp.concatenate(parts, axis=1), w_bottom.reshape(3456, 256)[...])
    result = jnp.maximum(result + bb_ref[...], 0.0).reshape(6, 6, ROWS, 256)
    index = lax.broadcasted_iota(jnp.int32, (6, 6, ROWS, 256), 0)
    zindex = lax.broadcasted_iota(jnp.int32, (6, 6, ROWS, 256), 1)
    yindex = lax.broadcasted_iota(jnp.int32, (6, 6, ROWS, 256), 2)
    outside = False
    for where, first, last, axis in ((index, 0, 5, "gx"), (zindex, 0, 5, "gz"), (yindex, 3, 12, "gy")):
        outside = outside | ((where == first) & at_low(axis)) | ((where == last) & at_high(axis))
    result = jnp.where(outside, 0.0, result).reshape(576, 256)
    for half in range(2):
        bottom_tmp[half] = result[:, half * 128:(half + 1) * 128]

    for half in range(2):
        doubled = s_up.at[half].reshape(36 * 32, 128)
        for step in range(10):
            value = bottom_tmp.at[half][pl.ds(3 + step, 36, stride=16), :]
            doubled[pl.ds(6 + 2 * step, 36, stride=32), :] = value
            doubled[pl.ds(7 + 2 * step, 36, stride=32), :] = value
    for slot, first in enumerate((8, 9, 7)):
        for half in range(2):
            lanes = slice(slot * 256 + half * 128, slot * 256 + half * 128 + 128)
            up_lanes[:, :, :, lanes] = s_up[half, :, first:first + 16].astype(BF).reshape(6, 6, ROWS, 128)

    wait_y(middle, s_mid, yr_mid)
    beside_both(s_mid, hu_mid, hd_mid, NXM + 2)
    for dz in range(2):
        for q in range(3):
            loads[("wrm", dz, q)].wait()

    for dx in range(2):
        parts = []
        for p in range(3):
            for zo in range(4):
                index = (pl.ds((dx + p) // 2, 4), (dx + p) % 2, pl.ds(zo // 2, 4), zo % 2)
                parts += [cells(ref, *index) for ref in (r_mid_pairs, hu_mid_pairs, hd_mid_pairs)]
        result = dot(jnp.concatenate(parts, axis=1), w_rm_skip.reshape(4608, 256)[...])
        parts = []
        for xt in range(2):
            for zt in range(3):
                parts.append(cells(up_lanes, pl.ds(xt + dx, 4), pl.ds(zt, 4)))
        weight = w_rm_up.reshape(2, 4608, 256)[dx]
        result = result + dot(jnp.concatenate(parts, axis=1), weight)
        result = jnp.maximum(result + bias_rise, 0.0).reshape(4, 4, ROWS, 256)
        for dz, index in enumerate(((pl.ds(0, 4), 1), (pl.ds(1, 4), 0))):
            place = (pl.ds(0, 4), 1) if dx == 0 else (pl.ds(1, 4), 0)
            value = result[..., dz * 128:(dz + 1) * 128]
            r_dec_pairs[place + index] = value.astype(BF)
            s_dec_pairs[:, dx, :, dz, 8:24] = value

    going = start_rims(50, r_dec, rim_dec)

    def dec_sides(x, carry):
        hu_dec[x + 1, 1:NZM + 1] = s_dec[x, :, 9:25].astype(BF)
        hd_dec[x + 1, 1:NZM + 1] = s_dec[x, :, 7:23].astype(BF)
        return carry

    lax.fori_loop(0, NXM, dec_sides, 0)

    weight = w_rf_up.reshape(2, 2304, 256)

    def up_own(step, carry):
        x = 2 * step
        for dx in range(2):
            parts = []
            for xt in range(2):
                for zt in range(3):
                    parts += [cells(ref, pl.ds(x + xt + dx, 2), pl.ds(zt, 8)) for ref in (r_dec, hu_dec, hd_dec)]
            result = dot(jnp.concatenate(parts, axis=1), weight[dx])
            for i in range(2):
                for dz, lanes in halves:
                    acc[4 * step + 2 * i + dx, :, dz] += result[i * 128:(i + 1) * 128, lanes].reshape(8, ROWS, 128)
        return carry

    lax.fori_loop(0, 3, up_own, 0)
    wait_rims(going, rim_dec, s_dec_rim)
    going = start_rows(50, s_dec, s_dec_rim, y_dec, yr_dec)
    lax.fori_loop(3, 4, up_own, 0)
    n = NXM
    for dst, first in ((up_dec, 9), (down_dec, 7)):
        rows = slice(first, first + ROWS)
        dst[0, 1:n + 1] = s_dec_rim[0:n, rows].astype(BF)
        dst[1, 1:n + 1] = s_dec_rim[n:2 * n, rows].astype(BF)
        dst[2] = s_dec_rim[2 * n:3 * n + 2, rows].astype(BF)
        dst[3] = s_dec_rim[4 * n:5 * n + 2, rows].astype(BF)
    sides = (rim_dec, up_dec, down_dec)
    for low_high, x, first in ((0, 0, 0), (1, NXF - 1, 3)):
        parts = [cells(ref, low_high, pl.ds(zt, 8)) for zt in range(3) for ref in sides]
        result = dot(jnp.concatenate(parts, axis=1), w_rf_up[first].reshape(1152, 256))
        for dz, lanes in halves:
            acc[x, :, dz] += result[:, lanes].reshape(8, ROWS, 128)
    acc_pairs = acc.reshape(8, 2, 8, 2, ROWS, 128)
    for low_high, z, zt in ((2, 0, 0), (3, 7, 2)):
        for dx in range(2):
            parts = [cells(ref, low_high, pl.ds(xt + dx, 8)) for xt in range(2) for ref in sides]
            result = dot(jnp.concatenate(parts, axis=1), w_rf_up[2 * dx:2 * dx + 2, zt].reshape(768, 256))
            for dz, lanes in halves:
                acc_pairs[:, dx, z, dz] += result[:, lanes].reshape(8, ROWS, 128)
    wait_rows(going, s_dec_rim, yr_dec, y_dec_wide, y_dec_grid, y_dec_window, 1)
    for number, row, slot in ((0, 0, 2), (1, ROWS - 1, 1)):
        results = []
        for dx in range(2):
            parts = []
            for xt in range(2):
                for zt in range(3):
                    parts.append(y_dec_window[number, zt, xt + dx:xt + dx + 8].reshape(64, 128).astype(BF))
            part = dot(jnp.concatenate(parts, axis=1), w_rf_up[2 * dx:2 * dx + 2, :, slot].reshape(768, 256))
            results.append(part.reshape(8, 8, 256))
        result = jnp.stack(results, axis=1).reshape(128, 256)
        for dz, lanes in halves:
            acc_rows[pl.ds(dz * ROWS + row, 128, stride=32), :] += result[:, lanes]

    def turn_out(x, carry):
        for y in range(ROWS):
            value = acc_rows[pl.ds(x * NZF * ROWS + y, NZF, stride=ROWS), :]
            value = (value + bias_last).astype(BF)
            out_v[x, 2 * y] = value[:, 0:64]
            out_v[x, 2 * y + 1] = value[:, 64:128]
        return carry

    lax.fori_loop(0, NXF, turn_out, 0)
    for message_sent in sent:
        message_sent.wait_send()


def scratch():
    vmem = pltpu.VMEM
    fine = (NXF + 2, NZF + 2, ROWS, 128)
    mid = pool = (NXM + 2, NZM + 2, ROWS, 128)
    rim = (4, NXF + 2, ROWS, 128)
    rim_m = (4, NXM + 2, ROWS, 128)
    mid_s = (NXM + 4, NZM + 2, 32, 128)
    return [
        *[vmem(fine, BF), vmem(fine, BF), vmem(rim, BF), vmem(rim, BF), vmem((2, TF, 128), BF), vmem((2, TF, 128), BF)] * 2,
        vmem((NXF, NZF, 32, 128), F32), vmem((96, 32, 128), F32), vmem((2, TF, 128), F32), vmem((2, NXF + 2, 32, 128), F32),
        vmem((2, 4, NXF + 2, 8, 128), F32),
        vmem(pool, BF), vmem(pool, BF), vmem(mid_s, F32), vmem((2, TM, 128), BF), vmem((2, TM, 128), BF),
        vmem(mid, BF), vmem(mid, BF), vmem(mid, BF), vmem(mid_s, F32), vmem((2, TM, 128), BF), vmem((2, TM, 128), BF),
        vmem((8, 4, ROWS, 128), BF), vmem((8, 8, 32, 128), F32), vmem((2, 128, 128), BF), vmem((2, 128, 128), BF),
        vmem((256, 128), F32),
        vmem((8, 8, ROWS, 384), BF), vmem((2, 576, 128), F32), vmem((2, 36, 32, 128), F32), vmem((6, 6, ROWS, 768), BF),
        vmem(mid, BF), vmem(mid, BF), vmem(mid, BF), vmem(rim_m, BF), vmem(rim_m, BF), vmem(rim_m, BF),
        vmem((2, TM, 128), BF), vmem((2, TM, 128), BF), vmem((NXM, NZM, 32, 128), F32), vmem((48, 32, 128), F32),
        vmem((2, TM, 128), F32), vmem((2, NXM + 2, 32, 128), F32), vmem((2, 3, NXM + 2, 8, 128), F32),
        vmem((3, 3, 3, 64, 64), BF), vmem((3, 3, 3, 192, 64), BF), vmem((3, 3, 3, 256, 128), BF),
        vmem((3, 4, 4, 64, 256), BF), vmem((3, 4, 4, 64, 256), BF), vmem((3, 4, 4, 64, 256), BF),
        vmem((3, 3, 3, 128, 256), BF), vmem((3, 4, 3, 128, 256), BF), vmem((4, 3, 3, 256, 256), BF),
        vmem((4, 3, 3, 128, 256), BF),
        vmem((NXF, 8, 2, ROWS, 128), F32), vmem((NXF, 32, NZF, 64), BF),
        pltpu.SemaphoreType.DMA((10 * LEVELS,)), pltpu.SemaphoreType.DMA((10 * LEVELS,)), pltpu.SemaphoreType.DMA((32,)),
    ]


def on_device(sizes, volume, wf, bf, wm, bm, wb, bb, wrm, brm, wrf, brf):
    hbm = pl.BlockSpec(memory_space=pl.ANY)
    return pl.pallas_call(
        functools.partial(kernel, sizes),
        out_shape=pltpu.VMEM((NXF, 32, NZF, 64), BF),
        in_specs=[hbm] * 6 + [pl.BlockSpec(memory_space=pltpu.VMEM)] * 5,
        out_specs=pl.BlockSpec(memory_space=pltpu.VMEM),
        scratch_shapes=scratch(),
        compiler_params=pltpu.CompilerParams(
            collective_id=0, has_side_effects=True, vmem_limit_bytes=54 * 2**20
        ),
    )(volume, wf, wm, wb, wrm, wrf, *(bias.reshape(1, -1) for bias in (bf, bm, bb, brm, brf)))


def solution(mesh):
    return jax.shard_map(
        functools.partial(on_device, dict(mesh.shape)),
        mesh=mesh,
        in_specs=(P("gx", "gy", "gz", None),) + (P(),) * 10,
        out_specs=P("gx", "gy", "gz", None),
        check_vma=False,
    )
```

```python
import functools

import jax
import jax.numpy as jnp
from jax import lax
from jax.experimental import pallas as pl
from jax.experimental.pallas import tpu as pltpu
from jax.sharding import PartitionSpec as P

BF = jnp.bfloat16
F32 = jnp.float32
MESH = pl.DeviceIdType.MESH

NXF, NZF, ROWS = 16, 16, 16
NXM, NZM = 8, 8
TF, TM = 352, 112
LEVELS = 6
PEERS = [(x, 0, z) for x in (-1, 0, 1) for z in (-1, 0, 1) if x or z] + [(0, -1, 0), (0, 1, 0)]


def dot(a, b):
    return jnp.dot(a, b, preferred_element_type=F32)


def cells(ref, *index):
    value = ref[index]
    return value.reshape(-1, value.shape[-1])


def kernel(
    sizes,
    vol, wf_hbm, wm_hbm, wb_hbm, wrm_hbm, wrf_hbm, bf_ref, bm_ref, bb_ref, brm_ref, brf_ref,
    out_v,
    r_in, h_in, rim_in, side_in, y_in, yr_in,
    r_enc, h_enc, rim_enc, side_enc, y_enc, yr_enc,
    s_fine, s_rim, y_wide, y_grid, y_window,
    r_pool, h_pool, s_pool, y_pool, yr_pool,
    r_mid, hu_mid, hd_mid, s_mid, y_mid, yr_mid,
    r_low, s_low, y_low, yr_low, pair_tmp,
    low_lanes, bottom_tmp, s_up, up_lanes,
    r_dec, hu_dec, hd_dec, rim_dec, up_dec, down_dec, y_dec, yr_dec, s_dec, s_dec_rim, y_dec_wide, y_dec_grid, y_dec_window,
    wf_raw, wrf_turned, wrf_raw, wrm_raw,
    w_fine, w_skip, w_mid, w_bottom, w_rm_skip, w_rm_up, w_rf_up,
    acc, vol_v,
    send_sem, recv_sem, local_sem,
):
    spots = {axis: lax.axis_index(axis) for axis in ("gx", "gy", "gz")}

    def near(steps):
        return {
            axis: lax.rem(spots[axis] + (step + sizes[axis]), sizes[axis]) for axis, step in zip(sizes, steps) if step
        }

    def at_low(axis):
        return spots[axis] == 0

    def at_high(axis):
        return spots[axis] == sizes[axis] - 1

    def message(number, src, dst, *steps):
        return pltpu.make_async_remote_copy(
            src_ref=src, dst_ref=dst, send_sem=send_sem.at[number], recv_sem=recv_sem.at[number],
            device_id=near(steps), device_id_type=MESH,
        )

    sent = []

    def start(copies):
        for copy in copies:
            copy.start()
        sent.extend(copies)
        return copies

    def arrived(copies):
        for copy in copies:
            copy.wait_recv()

    loads = {}

    def load(name, src, dst):
        copy = pltpu.make_async_copy(src, dst, local_sem.at[len(loads)])
        copy.start()
        loads[name] = copy

    load("vol", vol, vol_v)

    for ref in (r_in, h_in, r_enc, h_enc, r_dec, hu_dec, hd_dec):
        nx, nz = ref.shape[0], ref.shape[1]
        for plane in (0, nx - 1):
            ref[plane] = jnp.zeros(ref.shape[1:], BF)
        for plane in (0, nz - 1):
            ref[:, plane] = jnp.zeros((nx, ROWS, 128), BF)
    for ref in (rim_in, rim_enc, rim_dec, side_in, side_enc, up_dec, down_dec):
        for end in (0, ref.shape[1] - 1):
            ref[0:2, end] = jnp.zeros((2, ROWS, 128), BF)
    for ref, count in ((s_fine, 256), (s_dec, 64), (s_rim, 96), (s_dec_rim, 48)):
        rows = ref.reshape(count * 32, 128)
        for row in (7, 24):
            rows[pl.ds(row, count, stride=32), :] = jnp.zeros((count, 128), F32)

    barrier = pltpu.get_barrier_semaphore()
    for peer in PEERS:
        pl.semaphore_signal(barrier, inc=1, device_id=near(peer), device_id_type=MESH)

    load("wf", wf_hbm, wf_raw)
    load("wrf", wrf_hbm, wrf_turned)
    for dz in range(2):
        lanes = pl.ds(dz * 128, 128)
        for q, slot in ((1, 0), (2, 2), (0, 3)):
            load(("wm", dz, q), wm_hbm.at[:, q], w_mid.at[:, dz:dz + 3, slot, :, lanes])
    for q, slot in ((1, 0), (2, 1), (0, 2)):
        load(("wb", q), wb_hbm.at[:, q], w_bottom.at[:, :, slot])
    for dz in range(2):
        lanes = pl.ds(dz * 128, 128)
        for q, slot in ((1, 0), (2, 1), (0, 2)):
            load(("wrm", dz, q), wrm_hbm.at[:, q, :, 0:128, :], w_rm_skip.at[:, dz:dz + 3, slot, :, lanes])
    load("wrm_raw", wrm_hbm.at[:, :, :, 128:384, :], wrm_raw)

    def start_xz(base, ref, depth):
        depths = depth if isinstance(depth, tuple) else (depth, depth)
        nx, nz = ref.shape[0] - 2 * depths[0], ref.shape[1] - 2 * depths[1]

        def part(n, side, depth):
            own, rim = pl.ds(depth, n), pl.ds(depth, depth)
            if side == 0:
                return own, own
            if side < 0:
                return rim, pl.ds(n + depth, depth)
            return pl.ds(n, depth), pl.ds(0, depth)

        copies = []
        for number, (dx, dz) in enumerate(((-1, -1), (-1, 1), (1, -1), (1, 1), (-1, 0), (1, 0), (0, -1), (0, 1))):
            (src_x, dst_x), (src_z, dst_z) = part(nx, dx, depths[0]), part(nz, dz, depths[1])
            copies.append(message(base + number, ref.at[src_x, src_z], ref.at[dst_x, dst_z], dx, 0, dz))
        return start(copies)

    def clear_rim(ref, depth):
        dx, dz = depth if isinstance(depth, tuple) else (depth, depth)
        nx, nz = ref.shape[0], ref.shape[1]
        for edge, index in (
            (at_low("gx"), (pl.ds(0, dx),)), (at_high("gx"), (pl.ds(nx - dx, dx),)),
            (at_low("gz"), (pl.ds(0, nx), pl.ds(0, dz))), (at_high("gz"), (pl.ds(0, nx), pl.ds(nz - dz, dz))),
        ):
            @pl.when(edge)
            def _():
                ref[index] = jnp.zeros(ref.at[index].shape, BF)

    def wait_xz(copies, ref, s):
        arrived(copies)
        clear_rim(ref, 1)
        nx, nz = ref.shape[0], ref.shape[1]
        for plane in (0, nx - 1):
            s[plane, :, 8:24] = ref[plane].astype(F32)
        for plane in (0, nz - 1):
            s[1:nx - 1, plane, 8:24] = ref[1:nx - 1, plane].astype(F32)

    def start_y(base, s, ys, yr):
        count = ys.shape[1]
        rows = s.reshape(s.shape[0] * s.shape[1] * 32, 128)
        ys[0] = rows[pl.ds(8, count, stride=32), :].astype(BF)
        ys[1] = rows[pl.ds(23, count, stride=32), :].astype(BF)
        return start([
            message(base + 8, ys.at[0], yr.at[1], 0, -1, 0),
            message(base + 9, ys.at[1], yr.at[0], 0, 1, 0),
        ])

    def wait_y(copies, s, yr):
        arrived(copies)
        count = yr.shape[1]
        rows = s.reshape(s.shape[0] * s.shape[1] * 32, 128)
        low = jnp.where(at_low("gy"), 0.0, yr[0].astype(F32))
        high = jnp.where(at_high("gy"), 0.0, yr[1].astype(F32))
        rows[pl.ds(7, count, stride=32), :] = low
        rows[pl.ds(24, count, stride=32), :] = high

    def start_rims(base, ref, rim):
        nx, nz = ref.shape[0] - 2, ref.shape[1] - 2
        own_x, own_z = pl.ds(1, nx), pl.ds(1, nz)
        return start([
            message(base, ref.at[1, 1], rim.at[3, nx + 1], -1, 0, -1),
            message(base + 1, ref.at[1, nz], rim.at[2, nx + 1], -1, 0, 1),
            message(base + 2, ref.at[nx, 1], rim.at[3, 0], 1, 0, -1),
            message(base + 3, ref.at[nx, nz], rim.at[2, 0], 1, 0, 1),
            message(base + 4, ref.at[1, own_z], rim.at[1, own_z], -1, 0, 0),
            message(base + 5, ref.at[nx, own_z], rim.at[0, own_z], 1, 0, 0),
            message(base + 6, ref.at[own_x, 1], rim.at[3, own_x], 0, 0, -1),
            message(base + 7, ref.at[own_x, nz], rim.at[2, own_x], 0, 0, 1),
        ])

    def wait_rims(copies, rim, s):
        arrived(copies)
        n = rim.shape[1] - 2
        empty = jnp.zeros((n + 2, ROWS, 128), BF)
        for edge, side, end in (
            (at_low("gx"), 0, 0), (at_high("gx"), 1, n + 1), (at_low("gz"), 2, None), (at_high("gz"), 3, None),
        ):
            @pl.when(edge)
            def _():
                rim[side] = empty
                if end is not None:
                    rim[2:4, end] = empty[0:2]

        s[0:n, 8:24] = rim[0, 1:n + 1].astype(F32)
        s[n:2 * n, 8:24] = rim[1, 1:n + 1].astype(F32)
        s[2 * n:3 * n + 2, 8:24] = rim[2].astype(F32)
        s[4 * n:5 * n + 2, 8:24] = rim[3].astype(F32)

    def start_rows(base, s, rows, ys, yr, first):
        count = s.shape[0] if len(s.shape) == 3 else s.shape[0] * s.shape[1]
        flat = s.reshape(count * 32, 128)
        part = pl.ds(first, count)
        for number, row in enumerate(rows):
            ys[number, part] = flat[pl.ds(row, count, stride=32), :].astype(BF)
        return start([
            message(base, ys.at[0, part], yr.at[1, part], 0, -1, 0),
            message(base + 1, ys.at[1, part], yr.at[0, part], 0, 1, 0),
        ])

    def wait_rows(copies, s_side, yr, wide, grid, window, step):
        arrived(copies)
        more = s_side.shape[0]
        count = yr.shape[1] - more
        n = grid.shape[1] - 2
        for number, edge in enumerate((at_low("gy"), at_high("gy"))):
            value = jnp.where(edge, 0.0, yr[number].astype(F32))
            wide[number] = value
            grid[number, 1:n + 1, 8:8 + n] = value[0:count].reshape(n, n, 128)
            grid[number, 0, 8:8 + n] = value[count:count + n]
            grid[number, n + 1, 8:8 + n] = value[count + n:count + 2 * n]
            flat = grid.at[number].reshape((n + 2) * 32, 128)
            flat[pl.ds(7, n + 2, stride=32), :] = wide[number, count + 2 * n:count + 3 * n + 2]
            flat[pl.ds(8 + n, n + 2, stride=32), :] = wide[number, count + 4 * n:count + 5 * n + 2]

            def gather(x, carry):
                for tap in range(window.shape[1]):
                    window[number, tap, x] = flat[pl.ds(x * 32 + 7 + tap, 8, stride=step), :]
                return carry

            lax.fori_loop(0, n + 2, gather, 0)

    def select_rows(s, index):
        lane = lax.broadcasted_iota(jnp.int32, (ROWS, 128), 1)
        return jnp.where(lane < 64, s[index + (slice(9, 25),)], s[index + (slice(7, 23),)]).astype(BF)

    def beside(s, dst, planes):
        lane = lax.broadcasted_iota(jnp.int32, dst.shape[1:], 2)

        def plane(x, carry):
            dst[x] = jnp.where(lane < 64, s[x, :, 9:25], s[x, :, 7:23]).astype(BF)
            return carry

        lax.fori_loop(0, planes, plane, 0)

    def beside_both(s, up, down, planes):
        def plane(x, carry):
            up[x] = s[x, :, 9:25].astype(BF)
            down[x] = s[x, :, 7:23].astype(BF)
            return carry

        lax.fori_loop(0, planes, plane, 0)

    def spread(raw, first, dst):
        dst[...] = jnp.zeros(dst.shape, BF)

        def one(p, carry):
            for r in range(3):
                taps = [raw[p, q, r, first:first + 64, :] for q in range(3)]
                none = jnp.zeros_like(taps[0])
                pairs = ((taps[1], taps[0]), (taps[2], taps[1]), (none, taps[2]), (taps[0], none))
                for slot, pair in enumerate(pairs):
                    block = jnp.concatenate(pair, axis=1)
                    for dz in range(2):
                        dst[p, r + dz, slot, :, dz * 128:(dz + 1) * 128] = block
            return carry

        lax.fori_loop(0, 3, one, 0)

    def fine_window(ref, side, x, count):
        ref, side = (value.reshape(NXF + 2, 9, 2, ROWS, 128) for value in (ref, side))
        parts = []
        for p in range(3):
            for zo in range(4):
                index = (pl.ds(x + p, count), pl.ds(zo // 2, 8), zo % 2)
                parts += [cells(ref, *index), cells(side, *index)]
        return jnp.concatenate(parts, axis=1)

    acc_rows = acc.reshape(NXF * 8 * 2 * ROWS, 128)
    halves = ((0, slice(0, 128)), (1, slice(128, 256)))

    def fine_own(ref, side, weight, first, last):
        def step(pair, carry):
            x = 2 * pair
            result = dot(fine_window(ref, side, x, 2), weight.reshape(3072, 256)[...])
            for dz, lanes in halves:
                acc[pl.ds(x, 2), :, dz] = result[:, lanes].reshape(2, 8, ROWS, 128)
            return carry

        lax.fori_loop(first, last, step, 0)

    def fine_sides(ref, side):
        def plane(x, carry):
            side[x + 1, 1:NZF + 1] = select_rows(ref, (x, slice(None)))
            return carry

        lax.fori_loop(0, NXF, plane, 0)

    def fine_rims(rim, side, weight):
        n = NXF
        side[0, 1:n + 1] = select_rows(s_rim, (slice(0, n),))
        side[1, 1:n + 1] = select_rows(s_rim, (slice(n, 2 * n),))
        side[2] = select_rows(s_rim, (slice(2 * n, 3 * n + 2),))
        side[3] = select_rows(s_rim, (slice(4 * n, 5 * n + 2),))
        rim_pairs, side_pairs = (value.reshape(4, 9, 2, ROWS, 128) for value in (rim, side))
        for low_high, x, p in ((0, 0, 0), (1, NXF - 1, 2)):
            parts = []
            for zo in range(4):
                index = (low_high, pl.ds(zo // 2, 8), zo % 2)
                parts += [cells(rim_pairs, *index), cells(side_pairs, *index)]
            result = dot(jnp.concatenate(parts, axis=1), weight[p].reshape(1024, 256))
            for dz, lanes in halves:
                acc[x, :, dz] += result[:, lanes].reshape(8, ROWS, 128)
        for low_high, z, zo in ((2, 0, 0), (3, 7, 3)):
            parts = []
            for p in range(3):
                parts += [cells(rim, low_high, pl.ds(p, NXF)), cells(side, low_high, pl.ds(p, NXF))]
            result = dot(jnp.concatenate(parts, axis=1), weight[:, zo].reshape(768, 256))
            for dz, lanes in halves:
                acc[:, z, dz] += result[:, lanes].reshape(NXF, ROWS, 128)

    def fine_ends(weight):
        lane = lax.broadcasted_iota(jnp.int32, (128, 128), 1)
        for number, row in ((0, 0), (1, ROWS - 1)):
            used = (lane >= 64) if number == 0 else (lane < 64)
            parts = []
            for p in range(3):
                for zo in range(4):
                    value = y_window[number, zo, p:p + NXF].reshape(128, 128)
                    parts.append(jnp.where(used, value, 0.0).astype(BF))
            result = dot(jnp.concatenate(parts, axis=1), weight[:, :, 2:4].reshape(1536, 256))
            for dz, lanes in halves:
                acc_rows[pl.ds(dz * ROWS + row, 128, stride=32), :] += result[:, lanes]

    loads["vol"].wait()
    fine_rows = s_fine.reshape(NXF * NZF * 32, 128)

    def turn_in(x, carry):
        for y in range(ROWS):
            pair = jnp.concatenate([vol_v[x, 2 * y], vol_v[x, 2 * y + 1]], axis=1)
            fine_rows[pl.ds(x * NZF * 32 + 8 + y, NZF, stride=32), :] = pair.astype(F32)
        r_in[x + 1, 1:NZF + 1] = s_fine[x, :, 8:24].astype(BF)
        return carry

    lax.fori_loop(0, NXF, turn_in, 0)
    pl.semaphore_wait(barrier, len(PEERS))
    going = start_rims(0, r_in, rim_in)
    ends = start_rows(8, s_fine, (8, 23), y_in, yr_in, 0)
    fine_sides(s_fine, h_in)
    loads["wf"].wait()
    spread(wf_raw, 0, w_fine)
    fine_own(r_in, h_in, w_fine, 0, 6)
    wait_rims(going, rim_in, s_rim)
    ends += start_rows(10, s_rim, (8, 23), y_in, yr_in, 256)
    fine_own(r_in, h_in, w_fine, 6, 8)
    fine_rims(rim_in, side_in, w_fine)
    w_mid[:, :, 1] = jnp.zeros((3, 4, 64, 256), BF)
    w_mid[:, 3, :, :, 0:128] = jnp.zeros((3, 4, 64, 128), BF)
    w_mid[:, 0, :, :, 128:256] = jnp.zeros((3, 4, 64, 128), BF)
    w_rm_skip[:, 3, :, :, 0:128] = jnp.zeros((3, 3, 128, 128), BF)
    w_rm_skip[:, 0, :, :, 128:256] = jnp.zeros((3, 3, 128, 128), BF)
    loads["wrf"].wait()
    same = lax.broadcasted_iota(jnp.int32, (192, 192), 0) == lax.broadcasted_iota(jnp.int32, (192, 192), 1)
    identity = jnp.where(same, 1.0, 0.0).astype(BF)

    def turn_weight(p, carry):
        turned = lax.dot_general(
            identity, wrf_turned[p].reshape(576, 192), (((1,), (1,)), ((), ())), preferred_element_type=F32
        ).astype(BF)
        for q in range(3):
            for r in range(3):
                first = (3 * q + r) * 64
                wrf_raw[p, q, r] = turned[:, first:first + 64]
        return carry

    lax.fori_loop(0, 3, turn_weight, 0)
    spread(wrf_raw, 0, w_skip)
    loads["wrm_raw"].wait()

    def sums(parts):
        return (parts[0], parts[1] + parts[2], parts[0] + parts[1], parts[2])

    def rise_mid(chunk, carry):
        rows = pl.ds(pl.multiple_of(chunk * 16, 16), 16)
        for q, slot in ((1, 0), (2, 1), (0, 2)):
            by_r = [sums([wrm_raw[p, q, r, rows, :].astype(F32) for p in range(3)]) for r in range(3)]
            for x_sum in range(4):
                z_sums = sums([by_r[r][x_sum] for r in range(3)])
                for z_sum, (zt, dz) in enumerate(((0, 0), (1, 0), (1, 1), (2, 1))):
                    w_rm_up[x_sum, zt, slot, rows, dz * 128:(dz + 1) * 128] = z_sums[z_sum].astype(BF)
        return carry

    w_rm_up[:, 0, :, :, 128:256] = jnp.zeros((4, 3, 256, 128), BF)
    w_rm_up[:, 2, :, :, 0:128] = jnp.zeros((4, 3, 256, 128), BF)
    lax.fori_loop(0, 16, rise_mid, 0)

    wait_rows(ends, s_rim, yr_in, y_wide, y_grid, y_window, 2)
    fine_ends(w_fine)

    bias_fine = jnp.concatenate([bf_ref[...]] * 2, axis=1)
    bias_last = jnp.concatenate([brf_ref[...]] * 2, axis=1)
    r_enc_pairs = r_enc.reshape(NXF + 2, 9, 2, ROWS, 128)
    s_fine_pairs = s_fine.reshape(NXF, 8, 2, 32, 128)
    r_pool_pairs = r_pool.reshape(NXM + 2, 5, 2, ROWS, 128)
    s_pool_pairs = s_pool.reshape(NXM + 4, 5, 2, 32, 128)

    def fine(pair, carry):
        x = 2 * pair
        values = []
        for dz, index in enumerate(((pl.ds(0, 8), 1), (pl.ds(1, 8), 0))):
            value = jnp.maximum(acc[pl.ds(x, 2), :, dz] + bias_fine, 0.0)
            r_enc_pairs[(pl.ds(x + 1, 2),) + index] = value.astype(BF)
            s_fine_pairs[pl.ds(x, 2), :, dz, 8:24] = value
            values.append(value)
        most = jnp.maximum(jnp.max(values[0], axis=0), jnp.max(values[1], axis=0)).reshape(128, 128)
        most = jnp.maximum(most, pltpu.roll(most, 64, 1)).reshape(4, 2, ROWS, 128)
        for index, half in (((pl.ds(0, 4), 1), 0), ((pl.ds(1, 4), 0), 1)):
            r_pool_pairs[(pair + 1,) + index] = most[:, half].astype(BF)
            s_pool_pairs[(pair + 1,) + index + (pl.ds(8, 16),)] = most[:, half]
        return carry

    lax.fori_loop(0, 8, fine, 0)

    going = start_xz(12, r_pool, 1)
    fine_sides(s_fine, h_enc)
    fine_own(r_enc, h_enc, w_skip, 0, 3)

    def rise_fine(chunk, carry):
        src = pl.ds(pl.multiple_of(64 + chunk * 16, 16), 16)
        rows = pl.ds(pl.multiple_of(chunk * 16, 16), 16)
        by_q = []
        for q in range(3):
            by_r = [sums([wrf_raw[p, q, r, src, :].astype(F32) for p in range(3)]) for r in range(3)]
            by_q.append([sums([by_r[r][x_sum] for r in range(3)]) for x_sum in range(4)])
        none = jnp.zeros((16, 64), F32)
        for x_sum in range(4):
            for z_sum, (zt, dz) in enumerate(((0, 0), (1, 0), (1, 1), (2, 1))):
                taps = [by_q[q][x_sum][z_sum] for q in range(3)]
                pairs = ((taps[1] + taps[2], taps[0] + taps[1]), (none, taps[2]), (taps[0], none))
                for slot, pair in enumerate(pairs):
                    block = jnp.concatenate(pair, axis=1).astype(BF)
                    w_rf_up[x_sum, zt, slot, rows, dz * 128:(dz + 1) * 128] = block
        return carry

    w_rf_up[:, 0, :, :, 128:256] = jnp.zeros((4, 3, 128, 128), BF)
    w_rf_up[:, 2, :, :, 0:128] = jnp.zeros((4, 3, 128, 128), BF)
    lax.fori_loop(0, 8, rise_fine, 0)

    wait_xz(going, r_pool, s_pool)
    going = start_y(12, s_pool, y_pool, yr_pool)
    skipping = start_rims(24, r_enc, rim_enc)
    ends = start_rows(32, s_fine, (8, 23), y_enc, yr_enc, 0)
    fine_own(r_enc, h_enc, w_skip, 3, 5)
    for dz in range(2):
        for q in range(3):
            loads[("wm", dz, q)].wait()
    wait_y(going, s_pool, yr_pool)
    beside(s_pool, h_pool, NXM + 2)

    parts = []
    for p in range(3):
        for zo in range(4):
            index = (pl.ds(p, 8), pl.ds(zo // 2, 4), zo % 2)
            parts += [cells(ref, *index) for ref in (r_pool_pairs, h_pool.reshape(NXM + 2, 5, 2, ROWS, 128))]
    result = dot(jnp.concatenate(parts, axis=1), w_mid.reshape(3072, 256)[...])
    r_mid_pairs, hu_mid_pairs, hd_mid_pairs, r_dec_pairs = (
        ref.reshape(5, 2, 5, 2, ROWS, 128) for ref in (r_mid, hu_mid, hd_mid, r_dec)
    )
    s_mid_pairs = s_mid.reshape(6, 2, 5, 2, 32, 128)
    s_dec_pairs = s_dec.reshape(4, 2, 4, 2, 32, 128)
    bias_mid = jnp.concatenate([bm_ref[...]] * 2, axis=1)
    bias_rise = jnp.concatenate([brm_ref[...]] * 2, axis=1)
    result = jnp.maximum(result + bias_mid, 0.0).reshape(4, 2, 4, ROWS, 256)
    for dz, index in enumerate(((pl.ds(0, 4), 1), (pl.ds(1, 4), 0))):
        value = result[..., dz * 128:(dz + 1) * 128]
        for dx in range(2):
            place = (pl.ds(0, 4), 1) if dx == 0 else (pl.ds(1, 4), 0)
            r_mid_pairs[place + index] = value[:, dx].astype(BF)
            s_mid_pairs[place + index + (pl.ds(8, 16),)] = value[:, dx]
    most = jnp.maximum(result[:, 0], result[:, 1])
    pair_tmp[...] = jnp.maximum(most[..., 0:128], most[..., 128:256]).reshape(256, 128)
    low = jnp.maximum(pair_tmp[pl.ds(0, 128, stride=2), :], pair_tmp[pl.ds(1, 128, stride=2), :])
    r_low[2:6, 1:3] = low.astype(BF).reshape(4, 2, ROWS, 128)

    going = start_xz(36, r_low, (2, 1))
    middle = start_xz(48, r_mid, 1)

    wait_rims(skipping, rim_enc, s_rim)
    ends += start_rows(34, s_rim, (8, 23), y_enc, yr_enc, 256)
    fine_own(r_enc, h_enc, w_skip, 5, 8)
    arrived(going)
    clear_rim(r_low, (2, 1))
    low = r_low[...].astype(F32).reshape(8, 4, 2, 8, 128).reshape(8, 8, 8, 128)
    s_low[:, :, 8:16] = low
    s_low[:, :, 0:8] = jnp.zeros_like(low)
    s_low[:, :, 16:24] = jnp.zeros_like(low)
    rows = s_low.reshape(2048, 128)
    for number, row in enumerate((8, 9, 14, 15)):
        y_low[number // 2, pl.ds((number % 2) * 64, 64), :] = rows[pl.ds(row, 64, stride=32), :].astype(BF)
    going = start([
        message(44, y_low.at[0], yr_low.at[1], 0, -1, 0),
        message(45, y_low.at[1], yr_low.at[0], 0, 1, 0),
    ])
    wait_xz(middle, r_mid, s_mid)
    middle = start_y(48, s_mid, y_mid, yr_mid)
    fine_rims(rim_enc, side_enc, w_skip)
    for q in range(3):
        loads[("wb", q)].wait()
    wait_rows(ends, s_rim, yr_enc, y_wide, y_grid, y_window, 2)
    fine_ends(w_skip)
    arrived(going)
    for number, row in enumerate((6, 7, 16, 17)):
        edge = at_low("gy") if number < 2 else at_high("gy")
        value = yr_low[number // 2, pl.ds((number % 2) * 64, 64), :].astype(F32)
        rows[pl.ds(row, 64, stride=32), :] = jnp.where(edge, 0.0, value)

    def low_plane(x, carry):
        for slot, first in enumerate((4, 5, 3)):
            low_lanes[x, :, :, slot * 128:(slot + 1) * 128] = s_low[x, :, first:first + 16].astype(BF)
        return carry

    lax.fori_loop(0, 8, low_plane, 0)
    parts = [cells(low_lanes, pl.ds(p, 6), pl.ds(r, 6)) for p in range(3) for r in range(3)]
    result = dot(jnp.concatenate(parts, axis=1), w_bottom.reshape(3456, 256)[...])
    result = jnp.maximum(result + bb_ref[...], 0.0).reshape(6, 6, ROWS, 256)
    index = lax.broadcasted_iota(jnp.int32, (6, 6, ROWS, 256), 0)
    zindex = lax.broadcasted_iota(jnp.int32, (6, 6, ROWS, 256), 1)
    yindex = lax.broadcasted_iota(jnp.int32, (6, 6, ROWS, 256), 2)
    outside = False
    for where, first, last, axis in ((index, 0, 5, "gx"), (zindex, 0, 5, "gz"), (yindex, 3, 12, "gy")):
        outside = outside | ((where == first) & at_low(axis)) | ((where == last) & at_high(axis))
    result = jnp.where(outside, 0.0, result).reshape(576, 256)
    for half in range(2):
        bottom_tmp[half] = result[:, half * 128:(half + 1) * 128]

    for half in range(2):
        doubled = s_up.at[half].reshape(36 * 32, 128)
        for step in range(10):
            value = bottom_tmp.at[half][pl.ds(3 + step, 36, stride=16), :]
            doubled[pl.ds(6 + 2 * step, 36, stride=32), :] = value
            doubled[pl.ds(7 + 2 * step, 36, stride=32), :] = value
    for slot, first in enumerate((8, 9, 7)):
        for half in range(2):
            lanes = slice(slot * 256 + half * 128, slot * 256 + half * 128 + 128)
            up_lanes[:, :, :, lanes] = s_up[half, :, first:first + 16].astype(BF).reshape(6, 6, ROWS, 128)

    wait_y(middle, s_mid, yr_mid)
    beside_both(s_mid, hu_mid, hd_mid, NXM + 2)
    for dz in range(2):
        for q in range(3):
            loads[("wrm", dz, q)].wait()

    for dx in range(2):
        parts = []
        for p in range(3):
            for zo in range(4):
                index = (pl.ds((dx + p) // 2, 4), (dx + p) % 2, pl.ds(zo // 2, 4), zo % 2)
                parts += [cells(ref, *index) for ref in (r_mid_pairs, hu_mid_pairs, hd_mid_pairs)]
        result = dot(jnp.concatenate(parts, axis=1), w_rm_skip.reshape(4608, 256)[...])
        parts = []
        for xt in range(2):
            for zt in range(3):
                parts.append(cells(up_lanes, pl.ds(xt + dx, 4), pl.ds(zt, 4)))
        weight = w_rm_up.reshape(2, 4608, 256)[dx]
        result = result + dot(jnp.concatenate(parts, axis=1), weight)
        result = jnp.maximum(result + bias_rise, 0.0).reshape(4, 4, ROWS, 256)
        for dz, index in enumerate(((pl.ds(0, 4), 1), (pl.ds(1, 4), 0))):
            place = (pl.ds(0, 4), 1) if dx == 0 else (pl.ds(1, 4), 0)
            value = result[..., dz * 128:(dz + 1) * 128]
            r_dec_pairs[place + index] = value.astype(BF)
            s_dec_pairs[:, dx, :, dz, 8:24] = value

    going = start_rims(60, r_dec, rim_dec)
    ends = start_rows(68, s_dec, (8, 23), y_dec, yr_dec, 0)

    def dec_sides(x, carry):
        hu_dec[x + 1, 1:NZM + 1] = s_dec[x, :, 9:25].astype(BF)
        hd_dec[x + 1, 1:NZM + 1] = s_dec[x, :, 7:23].astype(BF)
        return carry

    lax.fori_loop(0, NXM, dec_sides, 0)

    weight = w_rf_up.reshape(2, 2304, 256)

    def up_own(step, carry):
        x = 2 * step
        for dx in range(2):
            parts = []
            for xt in range(2):
                for zt in range(3):
                    parts += [cells(ref, pl.ds(x + xt + dx, 2), pl.ds(zt, 8)) for ref in (r_dec, hu_dec, hd_dec)]
            result = dot(jnp.concatenate(parts, axis=1), weight[dx])
            for i in range(2):
                for dz, lanes in halves:
                    acc[4 * step + 2 * i + dx, :, dz] += result[i * 128:(i + 1) * 128, lanes].reshape(8, ROWS, 128)
        return carry

    lax.fori_loop(0, 3, up_own, 0)
    wait_rims(going, rim_dec, s_dec_rim)
    ends += start_rows(70, s_dec_rim, (8, 23), y_dec, yr_dec, 64)
    lax.fori_loop(3, 4, up_own, 0)
    n = NXM
    for dst, first in ((up_dec, 9), (down_dec, 7)):
        rows = slice(first, first + ROWS)
        dst[0, 1:n + 1] = s_dec_rim[0:n, rows].astype(BF)
        dst[1, 1:n + 1] = s_dec_rim[n:2 * n, rows].astype(BF)
        dst[2] = s_dec_rim[2 * n:3 * n + 2, rows].astype(BF)
        dst[3] = s_dec_rim[4 * n:5 * n + 2, rows].astype(BF)
    sides = (rim_dec, up_dec, down_dec)
    for low_high, x, first in ((0, 0, 0), (1, NXF - 1, 3)):
        parts = [cells(ref, low_high, pl.ds(zt, 8)) for zt in range(3) for ref in sides]
        result = dot(jnp.concatenate(parts, axis=1), w_rf_up[first].reshape(1152, 256))
        for dz, lanes in halves:
            acc[x, :, dz] += result[:, lanes].reshape(8, ROWS, 128)
    acc_pairs = acc.reshape(8, 2, 8, 2, ROWS, 128)
    for low_high, z, zt in ((2, 0, 0), (3, 7, 2)):
        for dx in range(2):
            parts = [cells(ref, low_high, pl.ds(xt + dx, 8)) for xt in range(2) for ref in sides]
            result = dot(jnp.concatenate(parts, axis=1), w_rf_up[2 * dx:2 * dx + 2, zt].reshape(768, 256))
            for dz, lanes in halves:
                acc_pairs[:, dx, z, dz] += result[:, lanes].reshape(8, ROWS, 128)
    wait_rows(ends, s_dec_rim, yr_dec, y_dec_wide, y_dec_grid, y_dec_window, 1)
    for number, row, slot in ((0, 0, 2), (1, ROWS - 1, 1)):
        results = []
        for dx in range(2):
            parts = []
            for xt in range(2):
                for zt in range(3):
                    parts.append(y_dec_window[number, zt, xt + dx:xt + dx + 8].reshape(64, 128).astype(BF))
            part = dot(jnp.concatenate(parts, axis=1), w_rf_up[2 * dx:2 * dx + 2, :, slot].reshape(768, 256))
            results.append(part.reshape(8, 8, 256))
        result = jnp.stack(results, axis=1).reshape(128, 256)
        for dz, lanes in halves:
            acc_rows[pl.ds(dz * ROWS + row, 128, stride=32), :] += result[:, lanes]

    def turn_out(x, carry):
        for y in range(ROWS):
            value = acc_rows[pl.ds(x * NZF * ROWS + y, NZF, stride=ROWS), :]
            value = (value + bias_last).astype(BF)
            out_v[x, 2 * y] = value[:, 0:64]
            out_v[x, 2 * y + 1] = value[:, 64:128]
        return carry

    lax.fori_loop(0, NXF, turn_out, 0)
    for message_sent in sent:
        message_sent.wait_send()


def scratch():
    vmem = pltpu.VMEM
    fine = (NXF + 2, NZF + 2, ROWS, 128)
    mid = pool = (NXM + 2, NZM + 2, ROWS, 128)
    rim = (4, NXF + 2, ROWS, 128)
    rim_m = (4, NXM + 2, ROWS, 128)
    mid_s = (NXM + 4, NZM + 2, 32, 128)
    return [
        *[vmem(fine, BF), vmem(fine, BF), vmem(rim, BF), vmem(rim, BF), vmem((2, TF, 128), BF), vmem((2, TF, 128), BF)] * 2,
        vmem((NXF, NZF, 32, 128), F32), vmem((96, 32, 128), F32), vmem((2, TF, 128), F32), vmem((2, NXF + 2, 32, 128), F32),
        vmem((2, 4, NXF + 2, 8, 128), F32),
        vmem(pool, BF), vmem(pool, BF), vmem(mid_s, F32), vmem((2, TM, 128), BF), vmem((2, TM, 128), BF),
        vmem(mid, BF), vmem(mid, BF), vmem(mid, BF), vmem(mid_s, F32), vmem((2, TM, 128), BF), vmem((2, TM, 128), BF),
        vmem((8, 4, ROWS, 128), BF), vmem((8, 8, 32, 128), F32), vmem((2, 128, 128), BF), vmem((2, 128, 128), BF),
        vmem((256, 128), F32),
        vmem((8, 8, ROWS, 384), BF), vmem((2, 576, 128), F32), vmem((2, 36, 32, 128), F32), vmem((6, 6, ROWS, 768), BF),
        vmem(mid, BF), vmem(mid, BF), vmem(mid, BF), vmem(rim_m, BF), vmem(rim_m, BF), vmem(rim_m, BF),
        vmem((2, TM, 128), BF), vmem((2, TM, 128), BF), vmem((NXM, NZM, 32, 128), F32), vmem((48, 32, 128), F32),
        vmem((2, TM, 128), F32), vmem((2, NXM + 2, 32, 128), F32), vmem((2, 3, NXM + 2, 8, 128), F32),
        vmem((3, 3, 3, 64, 64), BF), vmem((3, 3, 3, 64, 192), BF), vmem((3, 3, 3, 192, 64), BF), vmem((3, 3, 3, 256, 128), BF),
        vmem((3, 4, 4, 64, 256), BF), vmem((3, 4, 4, 64, 256), BF), vmem((3, 4, 4, 64, 256), BF),
        vmem((3, 3, 3, 128, 256), BF), vmem((3, 4, 3, 128, 256), BF), vmem((4, 3, 3, 256, 256), BF),
        vmem((4, 3, 3, 128, 256), BF),
        vmem((NXF, 8, 2, ROWS, 128), F32), vmem((NXF, 32, NZF, 64), BF),
        pltpu.SemaphoreType.DMA((12 * LEVELS,)), pltpu.SemaphoreType.DMA((12 * LEVELS,)), pltpu.SemaphoreType.DMA((32,)),
    ]


def on_device(sizes, volume, wf, bf, wm, bm, wb, bb, wrm, brm, wrf, brf):
    hbm = pl.BlockSpec(memory_space=pl.ANY)
    return pl.pallas_call(
        functools.partial(kernel, sizes),
        out_shape=pltpu.VMEM((NXF, 32, NZF, 64), BF),
        in_specs=[hbm] * 6 + [pl.BlockSpec(memory_space=pltpu.VMEM)] * 5,
        out_specs=pl.BlockSpec(memory_space=pltpu.VMEM),
        scratch_shapes=scratch(),
        compiler_params=pltpu.CompilerParams(
            collective_id=0, has_side_effects=True, vmem_limit_bytes=56 * 2**20
        ),
    )(volume, wf, wm, wb, wrm, wrf.transpose(0, 1, 2, 4, 3), *(bias.reshape(1, -1) for bias in (bf, bm, bb, brm, brf)))


def solution(mesh):
    return jax.shard_map(
        functools.partial(on_device, dict(mesh.shape)),
        mesh=mesh,
        in_specs=(P("gx", "gy", "gz", None),) + (P(),) * 10,
        out_specs=P("gx", "gy", "gz", None),
        check_vma=False,
    )
```

```python
import functools

import jax
import jax.numpy as jnp
from jax import lax
from jax.experimental import pallas as pl
from jax.experimental.pallas import tpu as pltpu
from jax.sharding import PartitionSpec as P

BF = jnp.bfloat16
F32 = jnp.float32
MESH = pl.DeviceIdType.MESH

NXF, NZF, ROWS = 16, 16, 16
NXM, NZM = 8, 8
TF, TM = 352, 112
LEVELS = 6
PEERS = [(x, 0, z) for x in (-1, 0, 1) for z in (-1, 0, 1) if x or z] + [(0, -1, 0), (0, 1, 0)]


def dot(a, b):
    return jnp.dot(a, b, preferred_element_type=F32)


def cells(ref, *index):
    value = ref[index]
    return value.reshape(-1, value.shape[-1])


def kernel(
    sizes,
    vol, wf_hbm, wm_hbm, wb_hbm, wrm_hbm, wrf_hbm, bf_ref, bm_ref, bb_ref, brm_ref, brf_ref,
    out_v,
    r_in, h_in, rim_in, side_in, y_in, yr_in,
    r_enc, h_enc, rim_enc, side_enc, y_enc, yr_enc,
    s_fine, s_rim, y_wide, y_grid, y_window,
    r_pool, h_pool, s_pool, y_pool, yr_pool,
    r_mid, hu_mid, hd_mid, s_mid, y_mid, yr_mid,
    r_low, s_low, y_low, yr_low, pair_tmp,
    low_lanes, bottom_tmp, s_up, up_lanes,
    r_dec, hu_dec, hd_dec, rim_dec, up_dec, down_dec, y_dec, yr_dec, s_dec, s_dec_rim, y_dec_wide, y_dec_grid, y_dec_window,
    wf_raw, wrf_turned, wrf_raw, wrm_raw,
    w_fine, w_skip, w_mid, w_bottom, w_rm_skip, w_rm_up, w_rf_up,
    acc, vol_v,
    send_sem, recv_sem, local_sem,
):
    spots = {axis: lax.axis_index(axis) for axis in ("gx", "gy", "gz")}

    def near(steps):
        return {
            axis: lax.rem(spots[axis] + (step + sizes[axis]), sizes[axis]) for axis, step in zip(sizes, steps) if step
        }

    def at_low(axis):
        return spots[axis] == 0

    def at_high(axis):
        return spots[axis] == sizes[axis] - 1

    def message(number, src, dst, *steps):
        return pltpu.make_async_remote_copy(
            src_ref=src, dst_ref=dst, send_sem=send_sem.at[number], recv_sem=recv_sem.at[number],
            device_id=near(steps), device_id_type=MESH,
        )

    sent = []

    def start(copies):
        for copy in copies:
            copy.start()
        sent.extend(copies)
        return copies

    def arrived(copies):
        for copy in copies:
            copy.wait_recv()

    loads = {}

    def load(name, src, dst):
        copy = pltpu.make_async_copy(src, dst, local_sem.at[len(loads)])
        copy.start()
        loads[name] = copy

    for name, planes in (("vol_low", pl.ds(0, 1)), ("vol_high", pl.ds(NXF - 1, 1)), ("vol", pl.ds(1, NXF - 2))):
        load(name, vol.at[planes], vol_v.at[planes])

    barrier = pltpu.get_barrier_semaphore()
    for peer in PEERS:
        pl.semaphore_signal(barrier, inc=1, device_id=near(peer), device_id_type=MESH)

    load("wf", wf_hbm, wf_raw)
    load("wrf", wrf_hbm, wrf_turned)
    for dz in range(2):
        lanes = pl.ds(dz * 128, 128)
        for q, slot in ((1, 0), (2, 2), (0, 3)):
            load(("wm", dz, q), wm_hbm.at[:, q], w_mid.at[:, dz:dz + 3, slot, :, lanes])
    for q, slot in ((1, 0), (2, 1), (0, 2)):
        load(("wb", q), wb_hbm.at[:, q], w_bottom.at[:, :, slot])
    for dz in range(2):
        lanes = pl.ds(dz * 128, 128)
        for q, slot in ((1, 0), (2, 1), (0, 2)):
            load(("wrm", dz, q), wrm_hbm.at[:, q, :, 0:128, :], w_rm_skip.at[:, dz:dz + 3, slot, :, lanes])
    load("wrm_raw", wrm_hbm.at[:, :, :, 128:384, :], wrm_raw)

    for ref in (r_in, h_in, r_enc, h_enc, r_dec, hu_dec, hd_dec):
        nx, nz = ref.shape[0], ref.shape[1]
        for plane in (0, nx - 1):
            ref[plane] = jnp.zeros(ref.shape[1:], BF)
        for plane in (0, nz - 1):
            ref[:, plane] = jnp.zeros((nx, ROWS, 128), BF)
    for ref in (rim_in, rim_enc, rim_dec, side_in, side_enc, up_dec, down_dec):
        for end in (0, ref.shape[1] - 1):
            ref[0:2, end] = jnp.zeros((2, ROWS, 128), BF)
    for ref, count in ((s_fine, 256), (s_dec, 64), (s_rim, 96), (s_dec_rim, 48)):
        rows = ref.reshape(count * 32, 128)
        for row in (7, 24):
            rows[pl.ds(row, count, stride=32), :] = jnp.zeros((count, 128), F32)

    def start_xz(base, ref, depth, first=0, last=8):
        depths = depth if isinstance(depth, tuple) else (depth, depth)
        nx, nz = ref.shape[0] - 2 * depths[0], ref.shape[1] - 2 * depths[1]

        def part(n, side, depth):
            own, rim = pl.ds(depth, n), pl.ds(depth, depth)
            if side == 0:
                return own, own
            if side < 0:
                return rim, pl.ds(n + depth, depth)
            return pl.ds(n, depth), pl.ds(0, depth)

        copies = []
        for number, (dx, dz) in enumerate(((-1, -1), (-1, 1), (1, -1), (1, 1), (-1, 0), (1, 0), (0, -1), (0, 1))):
            (src_x, dst_x), (src_z, dst_z) = part(nx, dx, depths[0]), part(nz, dz, depths[1])
            if first <= number < last:
                copies.append(message(base + number, ref.at[src_x, src_z], ref.at[dst_x, dst_z], dx, 0, dz))
        return start(copies)

    def clear_rim(ref, depth):
        dx, dz = depth if isinstance(depth, tuple) else (depth, depth)
        nx, nz = ref.shape[0], ref.shape[1]
        for edge, index in (
            (at_low("gx"), (pl.ds(0, dx),)), (at_high("gx"), (pl.ds(nx - dx, dx),)),
            (at_low("gz"), (pl.ds(0, nx), pl.ds(0, dz))), (at_high("gz"), (pl.ds(0, nx), pl.ds(nz - dz, dz))),
        ):
            @pl.when(edge)
            def _():
                ref[index] = jnp.zeros(ref.at[index].shape, BF)

    def wait_xz(copies, ref, s):
        arrived(copies)
        clear_rim(ref, 1)
        nx, nz = ref.shape[0], ref.shape[1]
        for plane in (0, nx - 1):
            s[plane, :, 8:24] = ref[plane].astype(F32)
        for plane in (0, nz - 1):
            s[1:nx - 1, plane, 8:24] = ref[1:nx - 1, plane].astype(F32)

    def start_y(base, s, ys, yr):
        count = ys.shape[1]
        rows = s.reshape(s.shape[0] * s.shape[1] * 32, 128)
        ys[0] = rows[pl.ds(8, count, stride=32), :].astype(BF)
        ys[1] = rows[pl.ds(23, count, stride=32), :].astype(BF)
        return start([
            message(base + 8, ys.at[0], yr.at[1], 0, -1, 0),
            message(base + 9, ys.at[1], yr.at[0], 0, 1, 0),
        ])

    def wait_y(copies, s, yr):
        arrived(copies)
        count = yr.shape[1]
        rows = s.reshape(s.shape[0] * s.shape[1] * 32, 128)
        low = jnp.where(at_low("gy"), 0.0, yr[0].astype(F32))
        high = jnp.where(at_high("gy"), 0.0, yr[1].astype(F32))
        rows[pl.ds(7, count, stride=32), :] = low
        rows[pl.ds(24, count, stride=32), :] = high

    def start_rims(base, ref, rim, first=0, last=8):
        nx, nz = ref.shape[0] - 2, ref.shape[1] - 2
        own_x, own_z = pl.ds(1, nx), pl.ds(1, nz)
        paths = (
            (ref.at[1, 1], rim.at[3, nx + 1], -1, 0, -1),
            (ref.at[1, nz], rim.at[2, nx + 1], -1, 0, 1),
            (ref.at[nx, 1], rim.at[3, 0], 1, 0, -1),
            (ref.at[nx, nz], rim.at[2, 0], 1, 0, 1),
            (ref.at[1, own_z], rim.at[1, own_z], -1, 0, 0),
            (ref.at[nx, own_z], rim.at[0, own_z], 1, 0, 0),
            (ref.at[own_x, 1], rim.at[3, own_x], 0, 0, -1),
            (ref.at[own_x, nz], rim.at[2, own_x], 0, 0, 1),
        )
        return start([message(base + number, *paths[number]) for number in range(first, last)])

    def wait_rims(copies, rim, s):
        arrived(copies)
        n = rim.shape[1] - 2
        empty = jnp.zeros((n + 2, ROWS, 128), BF)
        for edge, side, end in (
            (at_low("gx"), 0, 0), (at_high("gx"), 1, n + 1), (at_low("gz"), 2, None), (at_high("gz"), 3, None),
        ):
            @pl.when(edge)
            def _():
                rim[side] = empty
                if end is not None:
                    rim[2:4, end] = empty[0:2]

        s[0:n, 8:24] = rim[0, 1:n + 1].astype(F32)
        s[n:2 * n, 8:24] = rim[1, 1:n + 1].astype(F32)
        s[2 * n:3 * n + 2, 8:24] = rim[2].astype(F32)
        s[4 * n:5 * n + 2, 8:24] = rim[3].astype(F32)

    def start_rows(base, s, rows, ys, yr, first):
        count = s.shape[0] if len(s.shape) == 3 else s.shape[0] * s.shape[1]
        flat = s.reshape(count * 32, 128)
        part = pl.ds(first, count)
        for number, row in enumerate(rows):
            ys[number, part] = flat[pl.ds(row, count, stride=32), :].astype(BF)
        return start([
            message(base, ys.at[0, part], yr.at[1, part], 0, -1, 0),
            message(base + 1, ys.at[1, part], yr.at[0, part], 0, 1, 0),
        ])

    def wait_rows(copies, s_side, yr, wide, grid, window, step):
        arrived(copies)
        more = s_side.shape[0]
        count = yr.shape[1] - more
        n = grid.shape[1] - 2
        for number, edge in enumerate((at_low("gy"), at_high("gy"))):
            value = jnp.where(edge, 0.0, yr[number].astype(F32))
            wide[number] = value
            grid[number, 1:n + 1, 8:8 + n] = value[0:count].reshape(n, n, 128)
            grid[number, 0, 8:8 + n] = value[count:count + n]
            grid[number, n + 1, 8:8 + n] = value[count + n:count + 2 * n]
            flat = grid.at[number].reshape((n + 2) * 32, 128)
            flat[pl.ds(7, n + 2, stride=32), :] = wide[number, count + 2 * n:count + 3 * n + 2]
            flat[pl.ds(8 + n, n + 2, stride=32), :] = wide[number, count + 4 * n:count + 5 * n + 2]

            def gather(x, carry):
                for tap in range(window.shape[1]):
                    window[number, tap, x] = flat[pl.ds(x * 32 + 7 + tap, 8, stride=step), :]
                return carry

            lax.fori_loop(0, n + 2, gather, 0)

    def select_rows(s, index):
        lane = lax.broadcasted_iota(jnp.int32, (ROWS, 128), 1)
        return jnp.where(lane < 64, s[index + (slice(9, 25),)], s[index + (slice(7, 23),)]).astype(BF)

    def beside(s, dst, planes):
        lane = lax.broadcasted_iota(jnp.int32, dst.shape[1:], 2)

        def plane(x, carry):
            dst[x] = jnp.where(lane < 64, s[x, :, 9:25], s[x, :, 7:23]).astype(BF)
            return carry

        lax.fori_loop(0, planes, plane, 0)

    def beside_both(s, up, down, planes):
        def plane(x, carry):
            up[x] = s[x, :, 9:25].astype(BF)
            down[x] = s[x, :, 7:23].astype(BF)
            return carry

        lax.fori_loop(0, planes, plane, 0)

    def spread(raw, first, dst):
        dst[...] = jnp.zeros(dst.shape, BF)

        def one(p, carry):
            for r in range(3):
                taps = [raw[p, q, r, first:first + 64, :] for q in range(3)]
                none = jnp.zeros_like(taps[0])
                pairs = ((taps[1], taps[0]), (taps[2], taps[1]), (none, taps[2]), (taps[0], none))
                for slot, pair in enumerate(pairs):
                    block = jnp.concatenate(pair, axis=1)
                    for dz in range(2):
                        dst[p, r + dz, slot, :, dz * 128:(dz + 1) * 128] = block
            return carry

        lax.fori_loop(0, 3, one, 0)

    def fine_window(ref, side, x, count):
        ref, side = (value.reshape(NXF + 2, 9, 2, ROWS, 128) for value in (ref, side))
        parts = []
        for p in range(3):
            for zo in range(4):
                index = (pl.ds(x + p, count), pl.ds(zo // 2, 8), zo % 2)
                parts += [cells(ref, *index), cells(side, *index)]
        return jnp.concatenate(parts, axis=1)

    acc_rows = acc.reshape(NXF * 8 * 2 * ROWS, 128)
    halves = ((0, slice(0, 128)), (1, slice(128, 256)))

    def fine_own(ref, side, weight, first, last):
        def step(pair, carry):
            x = 2 * pair
            result = dot(fine_window(ref, side, x, 2), weight.reshape(3072, 256)[...])
            for dz, lanes in halves:
                acc[pl.ds(x, 2), :, dz] = result[:, lanes].reshape(2, 8, ROWS, 128)
            return carry

        lax.fori_loop(first, last, step, 0)

    def fine_sides(ref, side):
        def plane(x, carry):
            side[x + 1, 1:NZF + 1] = select_rows(ref, (x, slice(None)))
            return carry

        lax.fori_loop(0, NXF, plane, 0)

    def fine_rims(rim, side, weight):
        n = NXF
        side[0, 1:n + 1] = select_rows(s_rim, (slice(0, n),))
        side[1, 1:n + 1] = select_rows(s_rim, (slice(n, 2 * n),))
        side[2] = select_rows(s_rim, (slice(2 * n, 3 * n + 2),))
        side[3] = select_rows(s_rim, (slice(4 * n, 5 * n + 2),))
        rim_pairs, side_pairs = (value.reshape(4, 9, 2, ROWS, 128) for value in (rim, side))
        for low_high, x, p in ((0, 0, 0), (1, NXF - 1, 2)):
            parts = []
            for zo in range(4):
                index = (low_high, pl.ds(zo // 2, 8), zo % 2)
                parts += [cells(rim_pairs, *index), cells(side_pairs, *index)]
            result = dot(jnp.concatenate(parts, axis=1), weight[p].reshape(1024, 256))
            for dz, lanes in halves:
                acc[x, :, dz] += result[:, lanes].reshape(8, ROWS, 128)
        for low_high, z, zo in ((2, 0, 0), (3, 7, 3)):
            parts = []
            for p in range(3):
                parts += [cells(rim, low_high, pl.ds(p, NXF)), cells(side, low_high, pl.ds(p, NXF))]
            result = dot(jnp.concatenate(parts, axis=1), weight[:, zo].reshape(768, 256))
            for dz, lanes in halves:
                acc[:, z, dz] += result[:, lanes].reshape(NXF, ROWS, 128)

    def fine_ends(weight):
        lane = lax.broadcasted_iota(jnp.int32, (128, 128), 1)
        for number, row in ((0, 0), (1, ROWS - 1)):
            used = (lane >= 64) if number == 0 else (lane < 64)
            parts = []
            for p in range(3):
                for zo in range(4):
                    value = y_window[number, zo, p:p + NXF].reshape(128, 128)
                    parts.append(jnp.where(used, value, 0.0).astype(BF))
            result = dot(jnp.concatenate(parts, axis=1), weight[:, :, 2:4].reshape(1536, 256))
            for dz, lanes in halves:
                acc_rows[pl.ds(dz * ROWS + row, 128, stride=32), :] += result[:, lanes]

    fine_rows = s_fine.reshape(NXF * NZF * 32, 128)

    def turn_in(x, carry):
        for y in range(ROWS):
            pair = jnp.concatenate([vol_v[x, 2 * y], vol_v[x, 2 * y + 1]], axis=1)
            fine_rows[pl.ds(x * NZF * 32 + 8 + y, NZF, stride=32), :] = pair.astype(F32)
        r_in[x + 1, 1:NZF + 1] = s_fine[x, :, 8:24].astype(BF)
        return carry

    loads["vol_low"].wait()
    loads["vol_high"].wait()
    lax.fori_loop(0, 2, lambda i, carry: turn_in(i * (NXF - 1), carry), 0)
    pl.semaphore_wait(barrier, len(PEERS))
    going = start_rims(0, r_in, rim_in, 0, 6)
    loads["vol"].wait()
    lax.fori_loop(1, NXF - 1, turn_in, 0)
    going += start_rims(0, r_in, rim_in, 6, 8)
    ends = start_rows(8, s_fine, (8, 23), y_in, yr_in, 0)
    fine_sides(s_fine, h_in)
    loads["wf"].wait()
    spread(wf_raw, 0, w_fine)
    fine_own(r_in, h_in, w_fine, 0, 6)
    wait_rims(going, rim_in, s_rim)
    ends += start_rows(10, s_rim, (8, 23), y_in, yr_in, 256)
    fine_own(r_in, h_in, w_fine, 6, 8)
    fine_rims(rim_in, side_in, w_fine)
    w_mid[:, :, 1] = jnp.zeros((3, 4, 64, 256), BF)
    w_mid[:, 3, :, :, 0:128] = jnp.zeros((3, 4, 64, 128), BF)
    w_mid[:, 0, :, :, 128:256] = jnp.zeros((3, 4, 64, 128), BF)
    w_rm_skip[:, 3, :, :, 0:128] = jnp.zeros((3, 3, 128, 128), BF)
    w_rm_skip[:, 0, :, :, 128:256] = jnp.zeros((3, 3, 128, 128), BF)
    wait_rows(ends, s_rim, yr_in, y_wide, y_grid, y_window, 2)
    fine_ends(w_fine)

    bias_fine = jnp.concatenate([bf_ref[...]] * 2, axis=1)
    bias_last = jnp.concatenate([brf_ref[...]] * 2, axis=1)
    r_enc_pairs = r_enc.reshape(NXF + 2, 9, 2, ROWS, 128)
    s_fine_pairs = s_fine.reshape(NXF, 8, 2, 32, 128)
    r_pool_pairs = r_pool.reshape(NXM + 2, 5, 2, ROWS, 128)
    s_pool_pairs = s_pool.reshape(NXM + 4, 5, 2, 32, 128)

    def fine(pair, carry):
        x = 2 * pair
        values = []
        for dz, index in enumerate(((pl.ds(0, 8), 1), (pl.ds(1, 8), 0))):
            value = jnp.maximum(acc[pl.ds(x, 2), :, dz] + bias_fine, 0.0)
            r_enc_pairs[(pl.ds(x + 1, 2),) + index] = value.astype(BF)
            s_fine_pairs[pl.ds(x, 2), :, dz, 8:24] = value
            values.append(value)
        most = jnp.maximum(jnp.max(values[0], axis=0), jnp.max(values[1], axis=0)).reshape(128, 128)
        most = jnp.maximum(most, pltpu.roll(most, 64, 1)).reshape(4, 2, ROWS, 128)
        for index, half in (((pl.ds(0, 4), 1), 0), ((pl.ds(1, 4), 0), 1)):
            r_pool_pairs[(pair + 1,) + index] = most[:, half].astype(BF)
            s_pool_pairs[(pair + 1,) + index + (pl.ds(8, 16),)] = most[:, half]
        return carry

    lax.fori_loop(0, 2, lambda i, carry: fine(i * 7, carry), 0)
    going = start_xz(12, r_pool, 1, 0, 6)
    lax.fori_loop(1, 7, fine, 0)

    going += start_xz(12, r_pool, 1, 6, 8)
    loads["wrf"].wait()
    same = lax.broadcasted_iota(jnp.int32, (192, 192), 0) == lax.broadcasted_iota(jnp.int32, (192, 192), 1)
    identity = jnp.where(same, 1.0, 0.0).astype(BF)

    def turn_weight(p, carry):
        turned = lax.dot_general(
            identity, wrf_turned[p].reshape(576, 192), (((1,), (1,)), ((), ())), preferred_element_type=F32
        ).astype(BF)
        for q in range(3):
            for r in range(3):
                first = (3 * q + r) * 64
                wrf_raw[p, q, r] = turned[:, first:first + 64]
        return carry

    lax.fori_loop(0, 3, turn_weight, 0)
    spread(wrf_raw, 0, w_skip)
    fine_sides(s_fine, h_enc)
    fine_own(r_enc, h_enc, w_skip, 0, 2)
    loads["wrm_raw"].wait()

    def sums(parts):
        return (parts[0], parts[1] + parts[2], parts[0] + parts[1], parts[2])

    def rise_mid(chunk, carry):
        rows = pl.ds(pl.multiple_of(chunk * 16, 16), 16)
        for q, slot in ((1, 0), (2, 1), (0, 2)):
            by_r = [sums([wrm_raw[p, q, r, rows, :].astype(F32) for p in range(3)]) for r in range(3)]
            for x_sum in range(4):
                z_sums = sums([by_r[r][x_sum] for r in range(3)])
                for z_sum, (zt, dz) in enumerate(((0, 0), (1, 0), (1, 1), (2, 1))):
                    w_rm_up[x_sum, zt, slot, rows, dz * 128:(dz + 1) * 128] = z_sums[z_sum].astype(BF)
        return carry

    w_rm_up[:, 0, :, :, 128:256] = jnp.zeros((4, 3, 256, 128), BF)
    w_rm_up[:, 2, :, :, 0:128] = jnp.zeros((4, 3, 256, 128), BF)
    lax.fori_loop(0, 16, rise_mid, 0)


    wait_xz(going, r_pool, s_pool)
    going = start_y(12, s_pool, y_pool, yr_pool)
    skipping = start_rims(24, r_enc, rim_enc)
    ends = start_rows(32, s_fine, (8, 23), y_enc, yr_enc, 0)
    def rise_fine(chunk, carry):
        src = pl.ds(pl.multiple_of(64 + chunk * 16, 16), 16)
        rows = pl.ds(pl.multiple_of(chunk * 16, 16), 16)
        by_q = []
        for q in range(3):
            by_r = [sums([wrf_raw[p, q, r, src, :].astype(F32) for p in range(3)]) for r in range(3)]
            by_q.append([sums([by_r[r][x_sum] for r in range(3)]) for x_sum in range(4)])
        none = jnp.zeros((16, 64), F32)
        for x_sum in range(4):
            for z_sum, (zt, dz) in enumerate(((0, 0), (1, 0), (1, 1), (2, 1))):
                taps = [by_q[q][x_sum][z_sum] for q in range(3)]
                pairs = ((taps[1] + taps[2], taps[0] + taps[1]), (none, taps[2]), (taps[0], none))
                for slot, pair in enumerate(pairs):
                    block = jnp.concatenate(pair, axis=1).astype(BF)
                    w_rf_up[x_sum, zt, slot, rows, dz * 128:(dz + 1) * 128] = block
        return carry

    w_rf_up[:, 0, :, :, 128:256] = jnp.zeros((4, 3, 128, 128), BF)
    w_rf_up[:, 2, :, :, 0:128] = jnp.zeros((4, 3, 128, 128), BF)
    lax.fori_loop(0, 8, rise_fine, 0)

    fine_own(r_enc, h_enc, w_skip, 2, 4)
    for dz in range(2):
        for q in range(3):
            loads[("wm", dz, q)].wait()
    wait_y(going, s_pool, yr_pool)
    beside(s_pool, h_pool, NXM + 2)

    parts = []
    for p in range(3):
        for zo in range(4):
            index = (pl.ds(p, 8), pl.ds(zo // 2, 4), zo % 2)
            parts += [cells(ref, *index) for ref in (r_pool_pairs, h_pool.reshape(NXM + 2, 5, 2, ROWS, 128))]
    result = dot(jnp.concatenate(parts, axis=1), w_mid.reshape(3072, 256)[...])
    r_mid_pairs, hu_mid_pairs, hd_mid_pairs, r_dec_pairs = (
        ref.reshape(5, 2, 5, 2, ROWS, 128) for ref in (r_mid, hu_mid, hd_mid, r_dec)
    )
    s_mid_pairs = s_mid.reshape(6, 2, 5, 2, 32, 128)
    s_dec_pairs = s_dec.reshape(4, 2, 4, 2, 32, 128)
    bias_mid = jnp.concatenate([bm_ref[...]] * 2, axis=1)
    bias_rise = jnp.concatenate([brm_ref[...]] * 2, axis=1)
    result = jnp.maximum(result + bias_mid, 0.0).reshape(4, 2, 4, ROWS, 256)
    for dz, index in enumerate(((pl.ds(0, 4), 1), (pl.ds(1, 4), 0))):
        value = result[..., dz * 128:(dz + 1) * 128]
        for dx in range(2):
            place = (pl.ds(0, 4), 1) if dx == 0 else (pl.ds(1, 4), 0)
            r_mid_pairs[place + index] = value[:, dx].astype(BF)
            s_mid_pairs[place + index + (pl.ds(8, 16),)] = value[:, dx]
    most = jnp.maximum(result[:, 0], result[:, 1])
    pair_tmp[...] = jnp.maximum(most[..., 0:128], most[..., 128:256]).reshape(256, 128)
    low = jnp.maximum(pair_tmp[pl.ds(0, 128, stride=2), :], pair_tmp[pl.ds(1, 128, stride=2), :])
    r_low[2:6, 1:3] = low.astype(BF).reshape(4, 2, ROWS, 128)

    going = start_xz(36, r_low, (2, 1))
    middle = start_xz(48, r_mid, 1)

    wait_rims(skipping, rim_enc, s_rim)
    ends += start_rows(34, s_rim, (8, 23), y_enc, yr_enc, 256)
    fine_own(r_enc, h_enc, w_skip, 4, 8)
    arrived(going)
    clear_rim(r_low, (2, 1))
    low = r_low[...].astype(F32).reshape(8, 4, 2, 8, 128).reshape(8, 8, 8, 128)
    s_low[:, :, 8:16] = low
    s_low[:, :, 0:8] = jnp.zeros_like(low)
    s_low[:, :, 16:24] = jnp.zeros_like(low)
    rows = s_low.reshape(2048, 128)
    for number, row in enumerate((8, 9, 14, 15)):
        y_low[number // 2, pl.ds((number % 2) * 64, 64), :] = rows[pl.ds(row, 64, stride=32), :].astype(BF)
    going = start([
        message(44, y_low.at[0], yr_low.at[1], 0, -1, 0),
        message(45, y_low.at[1], yr_low.at[0], 0, 1, 0),
    ])
    wait_xz(middle, r_mid, s_mid)
    middle = start_y(48, s_mid, y_mid, yr_mid)
    for q in range(3):
        loads[("wb", q)].wait()
    arrived(going)
    for number, row in enumerate((6, 7, 16, 17)):
        edge = at_low("gy") if number < 2 else at_high("gy")
        value = yr_low[number // 2, pl.ds((number % 2) * 64, 64), :].astype(F32)
        rows[pl.ds(row, 64, stride=32), :] = jnp.where(edge, 0.0, value)

    def low_plane(x, carry):
        for slot, first in enumerate((4, 5, 3)):
            low_lanes[x, :, :, slot * 128:(slot + 1) * 128] = s_low[x, :, first:first + 16].astype(BF)
        return carry

    lax.fori_loop(0, 8, low_plane, 0)
    parts = [cells(low_lanes, pl.ds(p, 6), pl.ds(r, 6)) for p in range(3) for r in range(3)]
    result = dot(jnp.concatenate(parts, axis=1), w_bottom.reshape(3456, 256)[...])
    result = jnp.maximum(result + bb_ref[...], 0.0).reshape(6, 6, ROWS, 256)
    index = lax.broadcasted_iota(jnp.int32, (6, 6, ROWS, 256), 0)
    zindex = lax.broadcasted_iota(jnp.int32, (6, 6, ROWS, 256), 1)
    yindex = lax.broadcasted_iota(jnp.int32, (6, 6, ROWS, 256), 2)
    outside = False
    for where, first, last, axis in ((index, 0, 5, "gx"), (zindex, 0, 5, "gz"), (yindex, 3, 12, "gy")):
        outside = outside | ((where == first) & at_low(axis)) | ((where == last) & at_high(axis))
    result = jnp.where(outside, 0.0, result).reshape(576, 256)
    for half in range(2):
        bottom_tmp[half] = result[:, half * 128:(half + 1) * 128]

    for half in range(2):
        doubled = s_up.at[half].reshape(36 * 32, 128)
        for step in range(10):
            value = bottom_tmp.at[half][pl.ds(3 + step, 36, stride=16), :]
            doubled[pl.ds(6 + 2 * step, 36, stride=32), :] = value
            doubled[pl.ds(7 + 2 * step, 36, stride=32), :] = value
    for slot, first in enumerate((8, 9, 7)):
        for half in range(2):
            lanes = slice(slot * 256 + half * 128, slot * 256 + half * 128 + 128)
            up_lanes[:, :, :, lanes] = s_up[half, :, first:first + 16].astype(BF).reshape(6, 6, ROWS, 128)

    wait_y(middle, s_mid, yr_mid)
    beside_both(s_mid, hu_mid, hd_mid, NXM + 2)
    for dz in range(2):
        for q in range(3):
            loads[("wrm", dz, q)].wait()

    for dx in range(2):
        parts = []
        for p in range(3):
            for zo in range(4):
                index = (pl.ds((dx + p) // 2, 4), (dx + p) % 2, pl.ds(zo // 2, 4), zo % 2)
                parts += [cells(ref, *index) for ref in (r_mid_pairs, hu_mid_pairs, hd_mid_pairs)]
        result = dot(jnp.concatenate(parts, axis=1), w_rm_skip.reshape(4608, 256)[...])
        parts = []
        for xt in range(2):
            for zt in range(3):
                parts.append(cells(up_lanes, pl.ds(xt + dx, 4), pl.ds(zt, 4)))
        weight = w_rm_up.reshape(2, 4608, 256)[dx]
        result = result + dot(jnp.concatenate(parts, axis=1), weight)
        result = jnp.maximum(result + bias_rise, 0.0).reshape(4, 4, ROWS, 256)
        for dz, index in enumerate(((pl.ds(0, 4), 1), (pl.ds(1, 4), 0))):
            place = (pl.ds(0, 4), 1) if dx == 0 else (pl.ds(1, 4), 0)
            value = result[..., dz * 128:(dz + 1) * 128]
            r_dec_pairs[place + index] = value.astype(BF)
            s_dec_pairs[:, dx, :, dz, 8:24] = value

    going = start_rims(60, r_dec, rim_dec)
    ends_enc = ends
    ends = start_rows(68, s_dec, (8, 23), y_dec, yr_dec, 0)

    def dec_sides(x, carry):
        hu_dec[x + 1, 1:NZM + 1] = s_dec[x, :, 9:25].astype(BF)
        hd_dec[x + 1, 1:NZM + 1] = s_dec[x, :, 7:23].astype(BF)
        return carry

    lax.fori_loop(0, NXM, dec_sides, 0)

    weight = w_rf_up.reshape(2, 2304, 256)

    def up_own(step, carry):
        x = 2 * step
        for dx in range(2):
            parts = []
            for xt in range(2):
                for zt in range(3):
                    parts += [cells(ref, pl.ds(x + xt + dx, 2), pl.ds(zt, 8)) for ref in (r_dec, hu_dec, hd_dec)]
            result = dot(jnp.concatenate(parts, axis=1), weight[dx])
            for i in range(2):
                for dz, lanes in halves:
                    acc[4 * step + 2 * i + dx, :, dz] += result[i * 128:(i + 1) * 128, lanes].reshape(8, ROWS, 128)
        return carry

    lax.fori_loop(0, 2, up_own, 0)
    fine_rims(rim_enc, side_enc, w_skip)
    wait_rows(ends_enc, s_rim, yr_enc, y_wide, y_grid, y_window, 2)
    fine_ends(w_skip)
    wait_rims(going, rim_dec, s_dec_rim)
    ends += start_rows(70, s_dec_rim, (8, 23), y_dec, yr_dec, 64)
    lax.fori_loop(2, 4, up_own, 0)
    n = NXM
    for dst, first in ((up_dec, 9), (down_dec, 7)):
        rows = slice(first, first + ROWS)
        dst[0, 1:n + 1] = s_dec_rim[0:n, rows].astype(BF)
        dst[1, 1:n + 1] = s_dec_rim[n:2 * n, rows].astype(BF)
        dst[2] = s_dec_rim[2 * n:3 * n + 2, rows].astype(BF)
        dst[3] = s_dec_rim[4 * n:5 * n + 2, rows].astype(BF)
    sides = (rim_dec, up_dec, down_dec)
    for low_high, x, first in ((0, 0, 0), (1, NXF - 1, 3)):
        parts = [cells(ref, low_high, pl.ds(zt, 8)) for zt in range(3) for ref in sides]
        result = dot(jnp.concatenate(parts, axis=1), w_rf_up[first].reshape(1152, 256))
        for dz, lanes in halves:
            acc[x, :, dz] += result[:, lanes].reshape(8, ROWS, 128)
    acc_pairs = acc.reshape(8, 2, 8, 2, ROWS, 128)
    for low_high, z, zt in ((2, 0, 0), (3, 7, 2)):
        for dx in range(2):
            parts = [cells(ref, low_high, pl.ds(xt + dx, 8)) for xt in range(2) for ref in sides]
            result = dot(jnp.concatenate(parts, axis=1), w_rf_up[2 * dx:2 * dx + 2, zt].reshape(768, 256))
            for dz, lanes in halves:
                acc_pairs[:, dx, z, dz] += result[:, lanes].reshape(8, ROWS, 128)
    wait_rows(ends, s_dec_rim, yr_dec, y_dec_wide, y_dec_grid, y_dec_window, 1)
    for number, row, slot in ((0, 0, 2), (1, ROWS - 1, 1)):
        results = []
        for dx in range(2):
            parts = []
            for xt in range(2):
                for zt in range(3):
                    parts.append(y_dec_window[number, zt, xt + dx:xt + dx + 8].reshape(64, 128).astype(BF))
            part = dot(jnp.concatenate(parts, axis=1), w_rf_up[2 * dx:2 * dx + 2, :, slot].reshape(768, 256))
            results.append(part.reshape(8, 8, 256))
        result = jnp.stack(results, axis=1).reshape(128, 256)
        for dz, lanes in halves:
            acc_rows[pl.ds(dz * ROWS + row, 128, stride=32), :] += result[:, lanes]

    def turn_out(x, carry):
        for y in range(ROWS):
            value = acc_rows[pl.ds(x * NZF * ROWS + y, NZF, stride=ROWS), :]
            value = (value + bias_last).astype(BF)
            out_v[x, 2 * y] = value[:, 0:64]
            out_v[x, 2 * y + 1] = value[:, 64:128]
        return carry

    lax.fori_loop(0, NXF, turn_out, 0)
    for message_sent in sent:
        message_sent.wait_send()


def scratch():
    vmem = pltpu.VMEM
    fine = (NXF + 2, NZF + 2, ROWS, 128)
    mid = pool = (NXM + 2, NZM + 2, ROWS, 128)
    rim = (4, NXF + 2, ROWS, 128)
    rim_m = (4, NXM + 2, ROWS, 128)
    mid_s = (NXM + 4, NZM + 2, 32, 128)
    return [
        *[vmem(fine, BF), vmem(fine, BF), vmem(rim, BF), vmem(rim, BF), vmem((2, TF, 128), BF), vmem((2, TF, 128), BF)] * 2,
        vmem((NXF, NZF, 32, 128), F32), vmem((96, 32, 128), F32), vmem((2, TF, 128), F32), vmem((2, NXF + 2, 32, 128), F32),
        vmem((2, 4, NXF + 2, 8, 128), F32),
        vmem(pool, BF), vmem(pool, BF), vmem(mid_s, F32), vmem((2, TM, 128), BF), vmem((2, TM, 128), BF),
        vmem(mid, BF), vmem(mid, BF), vmem(mid, BF), vmem(mid_s, F32), vmem((2, TM, 128), BF), vmem((2, TM, 128), BF),
        vmem((8, 4, ROWS, 128), BF), vmem((8, 8, 32, 128), F32), vmem((2, 128, 128), BF), vmem((2, 128, 128), BF),
        vmem((256, 128), F32),
        vmem((8, 8, ROWS, 384), BF), vmem((2, 576, 128), F32), vmem((2, 36, 32, 128), F32), vmem((6, 6, ROWS, 768), BF),
        vmem(mid, BF), vmem(mid, BF), vmem(mid, BF), vmem(rim_m, BF), vmem(rim_m, BF), vmem(rim_m, BF),
        vmem((2, TM, 128), BF), vmem((2, TM, 128), BF), vmem((NXM, NZM, 32, 128), F32), vmem((48, 32, 128), F32),
        vmem((2, TM, 128), F32), vmem((2, NXM + 2, 32, 128), F32), vmem((2, 3, NXM + 2, 8, 128), F32),
        vmem((3, 3, 3, 64, 64), BF), vmem((3, 3, 3, 64, 192), BF), vmem((3, 3, 3, 192, 64), BF), vmem((3, 3, 3, 256, 128), BF),
        vmem((3, 4, 4, 64, 256), BF), vmem((3, 4, 4, 64, 256), BF), vmem((3, 4, 4, 64, 256), BF),
        vmem((3, 3, 3, 128, 256), BF), vmem((3, 4, 3, 128, 256), BF), vmem((4, 3, 3, 256, 256), BF),
        vmem((4, 3, 3, 128, 256), BF),
        vmem((NXF, 8, 2, ROWS, 128), F32), vmem((NXF, 32, NZF, 64), BF),
        pltpu.SemaphoreType.DMA((12 * LEVELS,)), pltpu.SemaphoreType.DMA((12 * LEVELS,)), pltpu.SemaphoreType.DMA((32,)),
    ]


def on_device(sizes, volume, wf, bf, wm, bm, wb, bb, wrm, brm, wrf, brf):
    hbm = pl.BlockSpec(memory_space=pl.ANY)
    return pl.pallas_call(
        functools.partial(kernel, sizes),
        out_shape=pltpu.VMEM((NXF, 32, NZF, 64), BF),
        in_specs=[hbm] * 6 + [pl.BlockSpec(memory_space=pltpu.VMEM)] * 5,
        out_specs=pl.BlockSpec(memory_space=pltpu.VMEM),
        scratch_shapes=scratch(),
        compiler_params=pltpu.CompilerParams(
            collective_id=0, has_side_effects=True, vmem_limit_bytes=56 * 2**20
        ),
    )(volume, wf, wm, wb, wrm, wrf.transpose(0, 1, 2, 4, 3), *(bias.reshape(1, -1) for bias in (bf, bm, bb, brm, brf)))


def solution(mesh):
    return jax.shard_map(
        functools.partial(on_device, dict(mesh.shape)),
        mesh=mesh,
        in_specs=(P("gx", "gy", "gz", None),) + (P(),) * 10,
        out_specs=P("gx", "gy", "gz", None),
        check_vma=False,
    )
```

```python
import functools

import jax
import jax.numpy as jnp
from jax import lax
from jax.experimental import pallas as pl
from jax.experimental.pallas import tpu as pltpu
from jax.sharding import PartitionSpec as P

BF = jnp.bfloat16
F32 = jnp.float32
MESH = pl.DeviceIdType.MESH

NXF, NZF, ROWS = 16, 16, 16
NXM, NZM = 8, 8
TF, TM = 352, 112
LEVELS = 6
PEERS = [(x, 0, z) for x in (-1, 0, 1) for z in (-1, 0, 1) if x or z] + [(0, -1, 0), (0, 1, 0)]


def dot(a, b):
    return jnp.dot(a, b, preferred_element_type=F32)


def cells(ref, *index):
    value = ref[index]
    return value.reshape(-1, value.shape[-1])


def kernel(
    sizes,
    vol, wf_hbm, wm_hbm, wb_hbm, wrm_hbm, wrf_hbm, bf_ref, bm_ref, bb_ref, brm_ref, brf_ref,
    out_v,
    r_in, h_in, rim_in, side_in, y_in, yr_in,
    r_enc, h_enc, rim_enc, side_enc, y_enc, yr_enc,
    s_fine, s_rim, y_wide, y_grid, y_window,
    r_pool, h_pool, s_pool, y_pool, yr_pool,
    r_mid, hu_mid, hd_mid, s_mid, y_mid, yr_mid,
    r_low, s_low, y_low, yr_low, pair_tmp,
    low_lanes, bottom_tmp, s_up, up_lanes,
    r_dec, hu_dec, hd_dec, rim_dec, up_dec, down_dec, y_dec, yr_dec, s_dec, s_dec_rim, y_dec_wide, y_dec_grid, y_dec_window,
    wf_raw, wrf_turned, wrf_raw, wrm_raw,
    w_fine, w_skip, w_mid, w_bottom, w_rm_skip, w_rm_up, w_rf_up,
    acc, vol_v,
    send_sem, recv_sem, local_sem,
):
    spots = {axis: lax.axis_index(axis) for axis in ("gx", "gy", "gz")}

    def near(steps):
        return {
            axis: lax.rem(spots[axis] + (step + sizes[axis]), sizes[axis]) for axis, step in zip(sizes, steps) if step
        }

    def at_low(axis):
        return spots[axis] == 0

    def at_high(axis):
        return spots[axis] == sizes[axis] - 1

    def message(number, src, dst, *steps):
        return pltpu.make_async_remote_copy(
            src_ref=src, dst_ref=dst, send_sem=send_sem.at[number], recv_sem=recv_sem.at[number],
            device_id=near(steps), device_id_type=MESH,
        )

    sent = []

    def start(copies):
        for copy in copies:
            copy.start()
        sent.extend(copies)
        return copies

    def arrived(copies):
        for copy in copies:
            copy.wait_recv()

    loads = {}

    def load(name, src, dst):
        copy = pltpu.make_async_copy(src, dst, local_sem.at[len(loads)])
        copy.start()
        loads[name] = copy

    for name, planes in (("vol_low", pl.ds(0, 1)), ("vol_high", pl.ds(NXF - 1, 1)), ("vol", pl.ds(1, NXF - 2))):
        load(name, vol.at[planes], vol_v.at[planes])

    barrier = pltpu.get_barrier_semaphore()
    for peer in PEERS:
        pl.semaphore_signal(barrier, inc=1, device_id=near(peer), device_id_type=MESH)

    load("wf", wf_hbm, wf_raw)
    load("wrf", wrf_hbm, wrf_turned)
    for dz in range(2):
        lanes = pl.ds(dz * 128, 128)
        for q, slot in ((1, 0), (2, 2), (0, 3)):
            load(("wm", dz, q), wm_hbm.at[:, q], w_mid.at[:, dz:dz + 3, slot, :, lanes])
    for q, slot in ((1, 0), (2, 1), (0, 2)):
        load(("wb", q), wb_hbm.at[:, q], w_bottom.at[:, :, slot])
    for dz in range(2):
        lanes = pl.ds(dz * 128, 128)
        for q, slot in ((1, 0), (2, 1), (0, 2)):
            load(("wrm", dz, q), wrm_hbm.at[:, q, :, 0:128, :], w_rm_skip.at[:, dz:dz + 3, slot, :, lanes])
    load("wrm_raw", wrm_hbm.at[:, :, :, 128:384, :], wrm_raw)

    for ref in (r_in, h_in, r_enc, h_enc, r_dec, hu_dec, hd_dec):
        nx, nz = ref.shape[0], ref.shape[1]
        for plane in (0, nx - 1):
            ref[plane] = jnp.zeros(ref.shape[1:], BF)
        for plane in (0, nz - 1):
            ref[:, plane] = jnp.zeros((nx, ROWS, 128), BF)
    for ref in (rim_in, rim_enc, rim_dec, side_in, side_enc, up_dec, down_dec):
        for end in (0, ref.shape[1] - 1):
            ref[0:2, end] = jnp.zeros((2, ROWS, 128), BF)
    for ref, count in ((s_fine, 256), (s_dec, 64), (s_rim, 96), (s_dec_rim, 48)):
        rows = ref.reshape(count * 32, 128)
        for row in (7, 24):
            rows[pl.ds(row, count, stride=32), :] = jnp.zeros((count, 128), F32)

    def start_xz(base, ref, depth, first=0, last=8):
        depths = depth if isinstance(depth, tuple) else (depth, depth)
        nx, nz = ref.shape[0] - 2 * depths[0], ref.shape[1] - 2 * depths[1]

        def part(n, side, depth):
            own, rim = pl.ds(depth, n), pl.ds(depth, depth)
            if side == 0:
                return own, own
            if side < 0:
                return rim, pl.ds(n + depth, depth)
            return pl.ds(n, depth), pl.ds(0, depth)

        copies = []
        for number, (dx, dz) in enumerate(((-1, -1), (-1, 1), (1, -1), (1, 1), (-1, 0), (1, 0), (0, -1), (0, 1))):
            (src_x, dst_x), (src_z, dst_z) = part(nx, dx, depths[0]), part(nz, dz, depths[1])
            if first <= number < last:
                copies.append(message(base + number, ref.at[src_x, src_z], ref.at[dst_x, dst_z], dx, 0, dz))
        return start(copies)

    def clear_rim(ref, depth):
        dx, dz = depth if isinstance(depth, tuple) else (depth, depth)
        nx, nz = ref.shape[0], ref.shape[1]
        for edge, index in (
            (at_low("gx"), (pl.ds(0, dx),)), (at_high("gx"), (pl.ds(nx - dx, dx),)),
            (at_low("gz"), (pl.ds(0, nx), pl.ds(0, dz))), (at_high("gz"), (pl.ds(0, nx), pl.ds(nz - dz, dz))),
        ):
            @pl.when(edge)
            def _():
                ref[index] = jnp.zeros(ref.at[index].shape, BF)

    def wait_xz(copies, ref, s):
        arrived(copies)
        clear_rim(ref, 1)
        nx, nz = ref.shape[0], ref.shape[1]
        for plane in (0, nx - 1):
            s[plane, :, 8:24] = ref[plane].astype(F32)
        for plane in (0, nz - 1):
            s[1:nx - 1, plane, 8:24] = ref[1:nx - 1, plane].astype(F32)

    def start_y(base, s, ys, yr):
        count = ys.shape[1]
        rows = s.reshape(s.shape[0] * s.shape[1] * 32, 128)
        ys[0] = rows[pl.ds(8, count, stride=32), :].astype(BF)
        ys[1] = rows[pl.ds(23, count, stride=32), :].astype(BF)
        return start([
            message(base + 8, ys.at[0], yr.at[1], 0, -1, 0),
            message(base + 9, ys.at[1], yr.at[0], 0, 1, 0),
        ])

    def wait_y(copies, s, yr):
        arrived(copies)
        count = yr.shape[1]
        rows = s.reshape(s.shape[0] * s.shape[1] * 32, 128)
        low = jnp.where(at_low("gy"), 0.0, yr[0].astype(F32))
        high = jnp.where(at_high("gy"), 0.0, yr[1].astype(F32))
        rows[pl.ds(7, count, stride=32), :] = low
        rows[pl.ds(24, count, stride=32), :] = high

    def start_rims(base, ref, rim, first=0, last=8):
        nx, nz = ref.shape[0] - 2, ref.shape[1] - 2
        own_x, own_z = pl.ds(1, nx), pl.ds(1, nz)
        paths = (
            (ref.at[1, 1], rim.at[3, nx + 1], -1, 0, -1),
            (ref.at[1, nz], rim.at[2, nx + 1], -1, 0, 1),
            (ref.at[nx, 1], rim.at[3, 0], 1, 0, -1),
            (ref.at[nx, nz], rim.at[2, 0], 1, 0, 1),
            (ref.at[1, own_z], rim.at[1, own_z], -1, 0, 0),
            (ref.at[nx, own_z], rim.at[0, own_z], 1, 0, 0),
            (ref.at[own_x, 1], rim.at[3, own_x], 0, 0, -1),
            (ref.at[own_x, nz], rim.at[2, own_x], 0, 0, 1),
        )
        return start([message(base + number, *paths[number]) for number in range(first, last)])

    def wait_rims(copies, rim, s):
        arrived(copies)
        n = rim.shape[1] - 2
        empty = jnp.zeros((n + 2, ROWS, 128), BF)
        for edge, side, end in (
            (at_low("gx"), 0, 0), (at_high("gx"), 1, n + 1), (at_low("gz"), 2, None), (at_high("gz"), 3, None),
        ):
            @pl.when(edge)
            def _():
                rim[side] = empty
                if end is not None:
                    rim[2:4, end] = empty[0:2]

        s[0:n, 8:24] = rim[0, 1:n + 1].astype(F32)
        s[n:2 * n, 8:24] = rim[1, 1:n + 1].astype(F32)
        s[2 * n:3 * n + 2, 8:24] = rim[2].astype(F32)
        s[4 * n:5 * n + 2, 8:24] = rim[3].astype(F32)

    def start_rows(base, s, rows, ys, yr, first):
        count = s.shape[0] if len(s.shape) == 3 else s.shape[0] * s.shape[1]
        flat = s.reshape(count * 32, 128)
        part = pl.ds(first, count)
        for number, row in enumerate(rows):
            ys[number, part] = flat[pl.ds(row, count, stride=32), :].astype(BF)
        return start([
            message(base, ys.at[0, part], yr.at[1, part], 0, -1, 0),
            message(base + 1, ys.at[1, part], yr.at[0, part], 0, 1, 0),
        ])

    def wait_rows(copies, s_side, yr, wide, grid, window, step):
        arrived(copies)
        more = s_side.shape[0]
        count = yr.shape[1] - more
        n = grid.shape[1] - 2
        for number, edge in enumerate((at_low("gy"), at_high("gy"))):
            value = jnp.where(edge, 0.0, yr[number].astype(F32))
            wide[number] = value
            grid[number, 1:n + 1, 8:8 + n] = value[0:count].reshape(n, n, 128)
            grid[number, 0, 8:8 + n] = value[count:count + n]
            grid[number, n + 1, 8:8 + n] = value[count + n:count + 2 * n]
            flat = grid.at[number].reshape((n + 2) * 32, 128)
            flat[pl.ds(7, n + 2, stride=32), :] = wide[number, count + 2 * n:count + 3 * n + 2]
            flat[pl.ds(8 + n, n + 2, stride=32), :] = wide[number, count + 4 * n:count + 5 * n + 2]

            def gather(x, carry):
                for tap in range(window.shape[1]):
                    window[number, tap, x] = flat[pl.ds(x * 32 + 7 + tap, 8, stride=step), :]
                return carry

            lax.fori_loop(0, n + 2, gather, 0)

    def select_rows(s, index):
        lane = lax.broadcasted_iota(jnp.int32, (ROWS, 128), 1)
        return jnp.where(lane < 64, s[index + (slice(9, 25),)], s[index + (slice(7, 23),)]).astype(BF)

    def beside(s, dst, planes):
        lane = lax.broadcasted_iota(jnp.int32, dst.shape[1:], 2)

        def plane(x, carry):
            dst[x] = jnp.where(lane < 64, s[x, :, 9:25], s[x, :, 7:23]).astype(BF)
            return carry

        lax.fori_loop(0, planes, plane, 0)

    def beside_both(s, up, down, planes):
        def plane(x, carry):
            up[x] = s[x, :, 9:25].astype(BF)
            down[x] = s[x, :, 7:23].astype(BF)
            return carry

        lax.fori_loop(0, planes, plane, 0)

    def spread(raw, first, dst):
        dst[...] = jnp.zeros(dst.shape, BF)

        def one(p, carry):
            for r in range(3):
                taps = [raw[p, q, r, first:first + 64, :] for q in range(3)]
                none = jnp.zeros_like(taps[0])
                pairs = ((taps[1], taps[0]), (taps[2], taps[1]), (none, taps[2]), (taps[0], none))
                for slot, pair in enumerate(pairs):
                    block = jnp.concatenate(pair, axis=1)
                    for dz in range(2):
                        dst[p, r + dz, slot, :, dz * 128:(dz + 1) * 128] = block
            return carry

        lax.fori_loop(0, 3, one, 0)

    def fine_window(ref, side, x, count):
        ref, side = (value.reshape(NXF + 2, 9, 2, ROWS, 128) for value in (ref, side))
        parts = []
        for p in range(3):
            for zo in range(4):
                index = (pl.ds(x + p, count), pl.ds(zo // 2, 8), zo % 2)
                parts += [cells(ref, *index), cells(side, *index)]
        return jnp.concatenate(parts, axis=1)

    acc_rows = acc.reshape(NXF * 8 * 2 * ROWS, 128)
    halves = ((0, slice(0, 128)), (1, slice(128, 256)))

    def fine_own(ref, side, weight, first, last):
        def step(pair, carry):
            x = 2 * pair
            result = dot(fine_window(ref, side, x, 2), weight.reshape(3072, 256)[...])
            for dz, lanes in halves:
                acc[pl.ds(x, 2), :, dz] = result[:, lanes].reshape(2, 8, ROWS, 128)
            return carry

        lax.fori_loop(first, last, step, 0)

    def fine_sides(ref, side):
        def plane(x, carry):
            side[x + 1, 1:NZF + 1] = select_rows(ref, (x, slice(None)))
            return carry

        lax.fori_loop(0, NXF, plane, 0)

    def fine_rims(rim, side, weight):
        n = NXF
        side[0, 1:n + 1] = select_rows(s_rim, (slice(0, n),))
        side[1, 1:n + 1] = select_rows(s_rim, (slice(n, 2 * n),))
        side[2] = select_rows(s_rim, (slice(2 * n, 3 * n + 2),))
        side[3] = select_rows(s_rim, (slice(4 * n, 5 * n + 2),))
        rim_pairs, side_pairs = (value.reshape(4, 9, 2, ROWS, 128) for value in (rim, side))
        for low_high, x, p in ((0, 0, 0), (1, NXF - 1, 2)):
            parts = []
            for zo in range(4):
                index = (low_high, pl.ds(zo // 2, 8), zo % 2)
                parts += [cells(rim_pairs, *index), cells(side_pairs, *index)]
            result = dot(jnp.concatenate(parts, axis=1), weight[p].reshape(1024, 256))
            for dz, lanes in halves:
                acc[x, :, dz] += result[:, lanes].reshape(8, ROWS, 128)
        for low_high, z, zo in ((2, 0, 0), (3, 7, 3)):
            parts = []
            for p in range(3):
                parts += [cells(rim, low_high, pl.ds(p, NXF)), cells(side, low_high, pl.ds(p, NXF))]
            result = dot(jnp.concatenate(parts, axis=1), weight[:, zo].reshape(768, 256))
            for dz, lanes in halves:
                acc[:, z, dz] += result[:, lanes].reshape(NXF, ROWS, 128)

    def fine_ends(weight):
        lane = lax.broadcasted_iota(jnp.int32, (128, 128), 1)
        for number, row in ((0, 0), (1, ROWS - 1)):
            used = (lane >= 64) if number == 0 else (lane < 64)
            parts = []
            for p in range(3):
                for zo in range(4):
                    value = y_window[number, zo, p:p + NXF].reshape(128, 128)
                    parts.append(jnp.where(used, value, 0.0).astype(BF))
            result = dot(jnp.concatenate(parts, axis=1), weight[:, :, 2:4].reshape(1536, 256))
            for dz, lanes in halves:
                acc_rows[pl.ds(dz * ROWS + row, 128, stride=32), :] += result[:, lanes]

    fine_rows = s_fine.reshape(NXF * NZF * 32, 128)

    def turn_in(x, carry):
        for y in range(ROWS):
            pair = jnp.concatenate([vol_v[x, 2 * y], vol_v[x, 2 * y + 1]], axis=1)
            fine_rows[pl.ds(x * NZF * 32 + 8 + y, NZF, stride=32), :] = pair.astype(F32)
        r_in[x + 1, 1:NZF + 1] = s_fine[x, :, 8:24].astype(BF)
        return carry

    loads["vol_low"].wait()
    loads["vol_high"].wait()
    lax.fori_loop(0, 2, lambda i, carry: turn_in(i * (NXF - 1), carry), 0)
    pl.semaphore_wait(barrier, len(PEERS))
    going = start_rims(0, r_in, rim_in, 0, 6)
    loads["vol"].wait()
    lax.fori_loop(1, NXF - 1, turn_in, 0)
    going += start_rims(0, r_in, rim_in, 6, 8)
    ends = start_rows(8, s_fine, (8, 23), y_in, yr_in, 0)
    fine_sides(s_fine, h_in)
    loads["wf"].wait()
    spread(wf_raw, 0, w_fine)
    fine_own(r_in, h_in, w_fine, 0, 6)
    wait_rims(going, rim_in, s_rim)
    ends += start_rows(10, s_rim, (8, 23), y_in, yr_in, 256)
    fine_own(r_in, h_in, w_fine, 6, 8)
    fine_rims(rim_in, side_in, w_fine)
    w_mid[:, :, 1] = jnp.zeros((3, 4, 64, 256), BF)
    w_mid[:, 3, :, :, 0:128] = jnp.zeros((3, 4, 64, 128), BF)
    w_mid[:, 0, :, :, 128:256] = jnp.zeros((3, 4, 64, 128), BF)
    w_rm_skip[:, 3, :, :, 0:128] = jnp.zeros((3, 3, 128, 128), BF)
    w_rm_skip[:, 0, :, :, 128:256] = jnp.zeros((3, 3, 128, 128), BF)
    wait_rows(ends, s_rim, yr_in, y_wide, y_grid, y_window, 2)
    fine_ends(w_fine)

    bias_fine = jnp.concatenate([bf_ref[...]] * 2, axis=1)
    bias_last = jnp.concatenate([brf_ref[...]] * 2, axis=1)
    r_enc_pairs = r_enc.reshape(NXF + 2, 9, 2, ROWS, 128)
    s_fine_pairs = s_fine.reshape(NXF, 8, 2, 32, 128)
    r_pool_pairs = r_pool.reshape(NXM + 2, 5, 2, ROWS, 128)
    s_pool_pairs = s_pool.reshape(NXM + 4, 5, 2, 32, 128)

    def fine(pair, carry):
        x = 2 * pair
        values = []
        for dz, index in enumerate(((pl.ds(0, 8), 1), (pl.ds(1, 8), 0))):
            value = jnp.maximum(acc[pl.ds(x, 2), :, dz] + bias_fine, 0.0)
            r_enc_pairs[(pl.ds(x + 1, 2),) + index] = value.astype(BF)
            s_fine_pairs[pl.ds(x, 2), :, dz, 8:24] = value
            values.append(value)
        most = jnp.maximum(jnp.max(values[0], axis=0), jnp.max(values[1], axis=0)).reshape(128, 128)
        most = jnp.maximum(most, pltpu.roll(most, 64, 1)).reshape(4, 2, ROWS, 128)
        for index, half in (((pl.ds(0, 4), 1), 0), ((pl.ds(1, 4), 0), 1)):
            r_pool_pairs[(pair + 1,) + index] = most[:, half].astype(BF)
            s_pool_pairs[(pair + 1,) + index + (pl.ds(8, 16),)] = most[:, half]
        return carry

    lax.fori_loop(0, 2, lambda i, carry: fine(i * 7, carry), 0)
    going = start_xz(12, r_pool, 1, 0, 6)
    lax.fori_loop(1, 7, fine, 0)

    going += start_xz(12, r_pool, 1, 6, 8)
    loads["wrf"].wait()
    same = lax.broadcasted_iota(jnp.int32, (192, 192), 0) == lax.broadcasted_iota(jnp.int32, (192, 192), 1)
    identity = jnp.where(same, 1.0, 0.0).astype(BF)

    def turn_weight(p, carry):
        turned = lax.dot_general(
            identity, wrf_turned[p].reshape(576, 192), (((1,), (1,)), ((), ())), preferred_element_type=F32
        ).astype(BF)
        for q in range(3):
            for r in range(3):
                first = (3 * q + r) * 64
                wrf_raw[p, q, r] = turned[:, first:first + 64]
        return carry

    lax.fori_loop(0, 3, turn_weight, 0)
    spread(wrf_raw, 0, w_skip)
    fine_sides(s_fine, h_enc)
    fine_own(r_enc, h_enc, w_skip, 0, 2)
    loads["wrm_raw"].wait()

    def sums(parts):
        return (parts[0], parts[1] + parts[2], parts[0] + parts[1], parts[2])

    def rise_mid(chunk, carry):
        rows = pl.ds(pl.multiple_of(chunk * 16, 16), 16)
        for q, slot in ((1, 0), (2, 1), (0, 2)):
            by_r = [sums([wrm_raw[p, q, r, rows, :].astype(F32) for p in range(3)]) for r in range(3)]
            for x_sum in range(4):
                z_sums = sums([by_r[r][x_sum] for r in range(3)])
                for z_sum, (zt, dz) in enumerate(((0, 0), (1, 0), (1, 1), (2, 1))):
                    w_rm_up[x_sum, zt, slot, rows, dz * 128:(dz + 1) * 128] = z_sums[z_sum].astype(BF)
        return carry

    w_rm_up[:, 0, :, :, 128:256] = jnp.zeros((4, 3, 256, 128), BF)
    w_rm_up[:, 2, :, :, 0:128] = jnp.zeros((4, 3, 256, 128), BF)
    lax.fori_loop(0, 16, rise_mid, 0)


    wait_xz(going, r_pool, s_pool)
    going = start_y(12, s_pool, y_pool, yr_pool)
    skipping = start_rims(24, r_enc, rim_enc)
    ends = start_rows(32, s_fine, (8, 23), y_enc, yr_enc, 0)
    def rise_fine(chunk, carry):
        src = pl.ds(pl.multiple_of(64 + chunk * 16, 16), 16)
        rows = pl.ds(pl.multiple_of(chunk * 16, 16), 16)
        by_q = []
        for q in range(3):
            by_r = [sums([wrf_raw[p, q, r, src, :].astype(F32) for p in range(3)]) for r in range(3)]
            by_q.append([sums([by_r[r][x_sum] for r in range(3)]) for x_sum in range(4)])
        none = jnp.zeros((16, 64), F32)
        for x_sum in range(4):
            for z_sum, (zt, dz) in enumerate(((0, 0), (1, 0), (1, 1), (2, 1))):
                taps = [by_q[q][x_sum][z_sum] for q in range(3)]
                pairs = ((taps[1] + taps[2], taps[0] + taps[1]), (none, taps[2]), (taps[0], none))
                for slot, pair in enumerate(pairs):
                    block = jnp.concatenate(pair, axis=1).astype(BF)
                    w_rf_up[x_sum, zt, slot, rows, dz * 128:(dz + 1) * 128] = block
        return carry

    w_rf_up[:, 0, :, :, 128:256] = jnp.zeros((4, 3, 128, 128), BF)
    w_rf_up[:, 2, :, :, 0:128] = jnp.zeros((4, 3, 128, 128), BF)
    lax.fori_loop(0, 8, rise_fine, 0)

    fine_own(r_enc, h_enc, w_skip, 2, 3)
    for dz in range(2):
        for q in range(3):
            loads[("wm", dz, q)].wait()
    wait_y(going, s_pool, yr_pool)
    beside(s_pool, h_pool, NXM + 2)

    parts = []
    for p in range(3):
        for zo in range(4):
            index = (pl.ds(p, 8), pl.ds(zo // 2, 4), zo % 2)
            parts += [cells(ref, *index) for ref in (r_pool_pairs, h_pool.reshape(NXM + 2, 5, 2, ROWS, 128))]
    result = dot(jnp.concatenate(parts, axis=1), w_mid.reshape(3072, 256)[...])
    r_mid_pairs, hu_mid_pairs, hd_mid_pairs, r_dec_pairs = (
        ref.reshape(5, 2, 5, 2, ROWS, 128) for ref in (r_mid, hu_mid, hd_mid, r_dec)
    )
    s_mid_pairs = s_mid.reshape(6, 2, 5, 2, 32, 128)
    s_dec_pairs = s_dec.reshape(4, 2, 4, 2, 32, 128)
    bias_mid = jnp.concatenate([bm_ref[...]] * 2, axis=1)
    bias_rise = jnp.concatenate([brm_ref[...]] * 2, axis=1)
    result = jnp.maximum(result + bias_mid, 0.0).reshape(4, 2, 4, ROWS, 256)
    for dz, index in enumerate(((pl.ds(0, 4), 1), (pl.ds(1, 4), 0))):
        value = result[..., dz * 128:(dz + 1) * 128]
        for dx in range(2):
            place = (pl.ds(0, 4), 1) if dx == 0 else (pl.ds(1, 4), 0)
            r_mid_pairs[place + index] = value[:, dx].astype(BF)
            s_mid_pairs[place + index + (pl.ds(8, 16),)] = value[:, dx]
    most = jnp.maximum(result[:, 0], result[:, 1])
    pair_tmp[...] = jnp.maximum(most[..., 0:128], most[..., 128:256]).reshape(256, 128)
    low = jnp.maximum(pair_tmp[pl.ds(0, 128, stride=2), :], pair_tmp[pl.ds(1, 128, stride=2), :])
    r_low[2:6, 1:3] = low.astype(BF).reshape(4, 2, ROWS, 128)

    going = start_xz(36, r_low, (2, 1))
    middle = start_xz(48, r_mid, 1)

    wait_rims(skipping, rim_enc, s_rim)
    ends += start_rows(34, s_rim, (8, 23), y_enc, yr_enc, 256)
    fine_own(r_enc, h_enc, w_skip, 3, 8)
    arrived(going)
    clear_rim(r_low, (2, 1))
    low = r_low[...].astype(F32).reshape(8, 4, 2, 8, 128).reshape(8, 8, 8, 128)
    s_low[:, :, 8:16] = low
    s_low[:, :, 0:8] = jnp.zeros_like(low)
    s_low[:, :, 16:24] = jnp.zeros_like(low)
    rows = s_low.reshape(2048, 128)
    for number, row in enumerate((8, 9, 14, 15)):
        y_low[number // 2, pl.ds((number % 2) * 64, 64), :] = rows[pl.ds(row, 64, stride=32), :].astype(BF)
    going = start([
        message(44, y_low.at[0], yr_low.at[1], 0, -1, 0),
        message(45, y_low.at[1], yr_low.at[0], 0, 1, 0),
    ])
    wait_xz(middle, r_mid, s_mid)
    middle = start_y(48, s_mid, y_mid, yr_mid)
    for q in range(3):
        loads[("wb", q)].wait()
    arrived(going)
    for number, row in enumerate((6, 7, 16, 17)):
        edge = at_low("gy") if number < 2 else at_high("gy")
        value = yr_low[number // 2, pl.ds((number % 2) * 64, 64), :].astype(F32)
        rows[pl.ds(row, 64, stride=32), :] = jnp.where(edge, 0.0, value)

    def low_plane(x, carry):
        for slot, first in enumerate((4, 5, 3)):
            low_lanes[x, :, :, slot * 128:(slot + 1) * 128] = s_low[x, :, first:first + 16].astype(BF)
        return carry

    lax.fori_loop(0, 8, low_plane, 0)
    parts = [cells(low_lanes, pl.ds(p, 6), pl.ds(r, 6)) for p in range(3) for r in range(3)]
    result = dot(jnp.concatenate(parts, axis=1), w_bottom.reshape(3456, 256)[...])
    result = jnp.maximum(result + bb_ref[...], 0.0).reshape(6, 6, ROWS, 256)
    index = lax.broadcasted_iota(jnp.int32, (6, 6, ROWS, 256), 0)
    zindex = lax.broadcasted_iota(jnp.int32, (6, 6, ROWS, 256), 1)
    yindex = lax.broadcasted_iota(jnp.int32, (6, 6, ROWS, 256), 2)
    outside = False
    for where, first, last, axis in ((index, 0, 5, "gx"), (zindex, 0, 5, "gz"), (yindex, 3, 12, "gy")):
        outside = outside | ((where == first) & at_low(axis)) | ((where == last) & at_high(axis))
    result = jnp.where(outside, 0.0, result).reshape(576, 256)
    for half in range(2):
        bottom_tmp[half] = result[:, half * 128:(half + 1) * 128]

    for half in range(2):
        doubled = s_up.at[half].reshape(36 * 32, 128)
        for step in range(10):
            value = bottom_tmp.at[half][pl.ds(3 + step, 36, stride=16), :]
            doubled[pl.ds(6 + 2 * step, 36, stride=32), :] = value
            doubled[pl.ds(7 + 2 * step, 36, stride=32), :] = value
    for slot, first in enumerate((8, 9, 7)):
        for half in range(2):
            lanes = slice(slot * 256 + half * 128, slot * 256 + half * 128 + 128)
            up_lanes[:, :, :, lanes] = s_up[half, :, first:first + 16].astype(BF).reshape(6, 6, ROWS, 128)

    wait_y(middle, s_mid, yr_mid)
    beside_both(s_mid, hu_mid, hd_mid, NXM + 2)
    for dz in range(2):
        for q in range(3):
            loads[("wrm", dz, q)].wait()

    for dx in range(2):
        parts = []
        for p in range(3):
            for zo in range(4):
                index = (pl.ds((dx + p) // 2, 4), (dx + p) % 2, pl.ds(zo // 2, 4), zo % 2)
                parts += [cells(ref, *index) for ref in (r_mid_pairs, hu_mid_pairs, hd_mid_pairs)]
        result = dot(jnp.concatenate(parts, axis=1), w_rm_skip.reshape(4608, 256)[...])
        parts = []
        for xt in range(2):
            for zt in range(3):
                parts.append(cells(up_lanes, pl.ds(xt + dx, 4), pl.ds(zt, 4)))
        weight = w_rm_up.reshape(2, 4608, 256)[dx]
        result = result + dot(jnp.concatenate(parts, axis=1), weight)
        result = jnp.maximum(result + bias_rise, 0.0).reshape(4, 4, ROWS, 256)
        for dz, index in enumerate(((pl.ds(0, 4), 1), (pl.ds(1, 4), 0))):
            place = (pl.ds(0, 4), 1) if dx == 0 else (pl.ds(1, 4), 0)
            value = result[..., dz * 128:(dz + 1) * 128]
            r_dec_pairs[place + index] = value.astype(BF)
            s_dec_pairs[:, dx, :, dz, 8:24] = value

    going = start_rims(60, r_dec, rim_dec)
    ends_enc = ends
    ends = start_rows(68, s_dec, (8, 23), y_dec, yr_dec, 0)

    def dec_sides(x, carry):
        hu_dec[x + 1, 1:NZM + 1] = s_dec[x, :, 9:25].astype(BF)
        hd_dec[x + 1, 1:NZM + 1] = s_dec[x, :, 7:23].astype(BF)
        return carry

    lax.fori_loop(0, NXM, dec_sides, 0)

    weight = w_rf_up.reshape(2, 2304, 256)

    def up_own(step, carry):
        x = 2 * step
        for dx in range(2):
            parts = []
            for xt in range(2):
                for zt in range(3):
                    parts += [cells(ref, pl.ds(x + xt + dx, 2), pl.ds(zt, 8)) for ref in (r_dec, hu_dec, hd_dec)]
            result = dot(jnp.concatenate(parts, axis=1), weight[dx])
            for i in range(2):
                for dz, lanes in halves:
                    acc[4 * step + 2 * i + dx, :, dz] += result[i * 128:(i + 1) * 128, lanes].reshape(8, ROWS, 128)
        return carry

    lax.fori_loop(0, 2, up_own, 0)
    fine_rims(rim_enc, side_enc, w_skip)
    wait_rows(ends_enc, s_rim, yr_enc, y_wide, y_grid, y_window, 2)
    fine_ends(w_skip)
    wait_rims(going, rim_dec, s_dec_rim)
    ends += start_rows(70, s_dec_rim, (8, 23), y_dec, yr_dec, 64)
    lax.fori_loop(2, 4, up_own, 0)
    n = NXM
    for dst, first in ((up_dec, 9), (down_dec, 7)):
        rows = slice(first, first + ROWS)
        dst[0, 1:n + 1] = s_dec_rim[0:n, rows].astype(BF)
        dst[1, 1:n + 1] = s_dec_rim[n:2 * n, rows].astype(BF)
        dst[2] = s_dec_rim[2 * n:3 * n + 2, rows].astype(BF)
        dst[3] = s_dec_rim[4 * n:5 * n + 2, rows].astype(BF)
    sides = (rim_dec, up_dec, down_dec)
    for low_high, x, first in ((0, 0, 0), (1, NXF - 1, 3)):
        parts = [cells(ref, low_high, pl.ds(zt, 8)) for zt in range(3) for ref in sides]
        result = dot(jnp.concatenate(parts, axis=1), w_rf_up[first].reshape(1152, 256))
        for dz, lanes in halves:
            acc[x, :, dz] += result[:, lanes].reshape(8, ROWS, 128)
    acc_pairs = acc.reshape(8, 2, 8, 2, ROWS, 128)
    for low_high, z, zt in ((2, 0, 0), (3, 7, 2)):
        for dx in range(2):
            parts = [cells(ref, low_high, pl.ds(xt + dx, 8)) for xt in range(2) for ref in sides]
            result = dot(jnp.concatenate(parts, axis=1), w_rf_up[2 * dx:2 * dx + 2, zt].reshape(768, 256))
            for dz, lanes in halves:
                acc_pairs[:, dx, z, dz] += result[:, lanes].reshape(8, ROWS, 128)
    wait_rows(ends, s_dec_rim, yr_dec, y_dec_wide, y_dec_grid, y_dec_window, 1)
    for number, row, slot in ((0, 0, 2), (1, ROWS - 1, 1)):
        results = []
        for dx in range(2):
            parts = []
            for xt in range(2):
                for zt in range(3):
                    parts.append(y_dec_window[number, zt, xt + dx:xt + dx + 8].reshape(64, 128).astype(BF))
            part = dot(jnp.concatenate(parts, axis=1), w_rf_up[2 * dx:2 * dx + 2, :, slot].reshape(768, 256))
            results.append(part.reshape(8, 8, 256))
        result = jnp.stack(results, axis=1).reshape(128, 256)
        for dz, lanes in halves:
            acc_rows[pl.ds(dz * ROWS + row, 128, stride=32), :] += result[:, lanes]

    def turn_out(x, carry):
        for y in range(ROWS):
            value = acc_rows[pl.ds(x * NZF * ROWS + y, NZF, stride=ROWS), :]
            value = (value + bias_last).astype(BF)
            out_v[x, 2 * y] = value[:, 0:64]
            out_v[x, 2 * y + 1] = value[:, 64:128]
        return carry

    lax.fori_loop(0, NXF, turn_out, 0)
    for message_sent in sent:
        message_sent.wait_send()


def scratch():
    vmem = pltpu.VMEM
    fine = (NXF + 2, NZF + 2, ROWS, 128)
    mid = pool = (NXM + 2, NZM + 2, ROWS, 128)
    rim = (4, NXF + 2, ROWS, 128)
    rim_m = (4, NXM + 2, ROWS, 128)
    mid_s = (NXM + 4, NZM + 2, 32, 128)
    return [
        *[vmem(fine, BF), vmem(fine, BF), vmem(rim, BF), vmem(rim, BF), vmem((2, TF, 128), BF), vmem((2, TF, 128), BF)] * 2,
        vmem((NXF, NZF, 32, 128), F32), vmem((96, 32, 128), F32), vmem((2, TF, 128), F32), vmem((2, NXF + 2, 32, 128), F32),
        vmem((2, 4, NXF + 2, 8, 128), F32),
        vmem(pool, BF), vmem(pool, BF), vmem(mid_s, F32), vmem((2, TM, 128), BF), vmem((2, TM, 128), BF),
        vmem(mid, BF), vmem(mid, BF), vmem(mid, BF), vmem(mid_s, F32), vmem((2, TM, 128), BF), vmem((2, TM, 128), BF),
        vmem((8, 4, ROWS, 128), BF), vmem((8, 8, 32, 128), F32), vmem((2, 128, 128), BF), vmem((2, 128, 128), BF),
        vmem((256, 128), F32),
        vmem((8, 8, ROWS, 384), BF), vmem((2, 576, 128), F32), vmem((2, 36, 32, 128), F32), vmem((6, 6, ROWS, 768), BF),
        vmem(mid, BF), vmem(mid, BF), vmem(mid, BF), vmem(rim_m, BF), vmem(rim_m, BF), vmem(rim_m, BF),
        vmem((2, TM, 128), BF), vmem((2, TM, 128), BF), vmem((NXM, NZM, 32, 128), F32), vmem((48, 32, 128), F32),
        vmem((2, TM, 128), F32), vmem((2, NXM + 2, 32, 128), F32), vmem((2, 3, NXM + 2, 8, 128), F32),
        vmem((3, 3, 3, 64, 64), BF), vmem((3, 3, 3, 64, 192), BF), vmem((3, 3, 3, 192, 64), BF), vmem((3, 3, 3, 256, 128), BF),
        vmem((3, 4, 4, 64, 256), BF), vmem((3, 4, 4, 64, 256), BF), vmem((3, 4, 4, 64, 256), BF),
        vmem((3, 3, 3, 128, 256), BF), vmem((3, 4, 3, 128, 256), BF), vmem((4, 3, 3, 256, 256), BF),
        vmem((4, 3, 3, 128, 256), BF),
        vmem((NXF, 8, 2, ROWS, 128), F32), vmem((NXF, 32, NZF, 64), BF),
        pltpu.SemaphoreType.DMA((12 * LEVELS,)), pltpu.SemaphoreType.DMA((12 * LEVELS,)), pltpu.SemaphoreType.DMA((32,)),
    ]


def on_device(sizes, volume, wf, bf, wm, bm, wb, bb, wrm, brm, wrf, brf):
    hbm = pl.BlockSpec(memory_space=pl.ANY)
    return pl.pallas_call(
        functools.partial(kernel, sizes),
        out_shape=pltpu.VMEM((NXF, 32, NZF, 64), BF),
        in_specs=[hbm] * 6 + [pl.BlockSpec(memory_space=pltpu.VMEM)] * 5,
        out_specs=pl.BlockSpec(memory_space=pltpu.VMEM),
        scratch_shapes=scratch(),
        compiler_params=pltpu.CompilerParams(
            collective_id=0, has_side_effects=True, vmem_limit_bytes=56 * 2**20
        ),
    )(volume, wf, wm, wb, wrm, wrf.transpose(0, 1, 2, 4, 3), *(bias.reshape(1, -1) for bias in (bf, bm, bb, brm, brf)))


def solution(mesh):
    return jax.shard_map(
        functools.partial(on_device, dict(mesh.shape)),
        mesh=mesh,
        in_specs=(P("gx", "gy", "gz", None),) + (P(),) * 10,
        out_specs=P("gx", "gy", "gz", None),
        check_vma=False,
    )
```
